128 devices in a mesh: pipe: 8 (over y, core), cross: 16 (over x, z).
Axes of the slice: x: 4, y: 4, z: 4, core: 2. Of those that a mesh axis runs over, the one named last changes fastest.
Arguments:
- pops_first: float32 [19, 128, 128, 128], P(None, 'pipe', 'cross'), may hold values from 0.02 to 0.1
- pops_second: float32 [19, 128, 128, 128], P(None, 'pipe', 'cross'), may hold values from 0.02 to 0.1
- phase_first: float32 [128, 128, 128], P('pipe', 'cross'), may hold values from -1 to 1
- phase_second: float32 [128, 128, 128], P('pipe', 'cross'), may hold values from -1 to 1
- adjoint_last: float32 [19, 128, 128, 128], P(None, 'pipe', 'cross'), may hold values from -6 to 6
- wettability: float32 [4096], replicated, may hold values from -0.8 to 0.8
- fluid: int32 [128, 128, 128], P('pipe', 'cross'), may hold values from 0 to 1, as said below
- wall: int32 [128, 128, 128], P('pipe', 'cross'), may hold values from 0 to 1, as said below
- patch: int32 [128, 128, 128], P('pipe', 'cross'), may hold values from 0 to 4095, as said below
Outputs:
- adjoint_first: float32 [19, 128, 128, 128], P(None, 'pipe', 'cross')
- wettability_gradient: float32 [4096], replicated
The draws below stay inside these ranges and needn't reach their ends.
Inputs may be any that keep to these rules, and one draw needn't show every extreme that they name: 1 marks fluid nodes; every node with the first or last index along the second or the third dimension is solid. `wall`: 1 exactly on solid nodes that have a fluid node at one of the 18 lattice offsets, indices modulo the grid. `patch`: read only where wall is 1.
All inputs are finite; a program needn't handle non-finite values.
Results may differ from the reference program's by a relative error of at most 0.0001.
Values sent between devices are 32-bit elements; how exact they have to be, the bound alone decides.
No kernel may reach another device: no remote copies, remote signals or barrier semaphores. Data moves between devices by JAX's collectives and lax.ppermute only.
A program may use at most 64 MiB of HBM per device.

```python
import jax
import jax.numpy as jnp
from jax import lax

CX = 16
NZ = 128
PATCHES = 4096
NX = 128
NY = 128


lattice_vel = ((0, 0, 0), (1, 0, 0), (-1, 0, 0), (0, 1, 0), (0, -1, 0), (0, 0, 1), (0, 0, -1), (1, 1, 0), (-1, -1, 0), (1, -1, 0), (-1, 1, 0), (1, 0, 1), (-1, 0, -1), (1, 0, -1), (-1, 0, 1), (0, 1, 1), (0, -1, -1), (0, 1, -1), (0, -1, 1))


def geometry(key):
    rough = jax.random.randint(key, (NX, NY, NZ), -3, 4)
    xs = jnp.arange(NX, dtype=jnp.int32)[:, None, None]
    ys = jnp.arange(NY, dtype=jnp.int32)[None, :, None]
    zs = jnp.arange(NZ, dtype=jnp.int32)[None, None, :]
    drift = xs * (NY // 8) // NX - NY // 16
    across = 2 * ys - NY + 1 - drift
    depth = 2 * zs - NZ + 1
    level = across * across * 64 // (NY * NY) + depth * depth * 64 // (NZ * NZ) + rough
    return (level < 44).astype(jnp.int32)


def surface(fluid):
    near = jnp.zeros_like(fluid)
    for move in lattice_vel[1:]:
        near = jnp.maximum(near, jnp.roll(fluid, (-move[0], -move[1], -move[2]), axis=(0, 1, 2)))
    return (1 - fluid) * near


def draw_fluid(key, part):
    return geometry(key)


def draw_wall(key, part):
    return surface(geometry(key))


def draw_patch(key, part):
    key = jax.random.fold_in(key, 7)
    return jax.random.randint(key, (NX, NY, NZ), 0, PATCHES).astype(jnp.int32)


def steps_of(key, extent, shards, low, largest):
    level, own = 1.0, jax.random.fold_in(key, 6)
    for dim, blocks in shards:
        steps = jnp.exp(jax.random.uniform(jax.random.fold_in(own, dim), (blocks,), jnp.float32, low / len(shards), largest / len(shards)))
        level = level * jnp.repeat(steps, extent[dim] // blocks).reshape([-1 if axis == dim else 1 for axis in range(len(extent))])
    return level


def centred(stream_key, dims, width, bound, cuts=(), kind=jnp.bfloat16):
    array = jax.random.normal(stream_key, dims, jnp.float32) * width
    if len(cuts) > 0:
        array = steps_of(stream_key, dims, cuts, -0.22, 0.18) * array
    return jnp.clip(array, min=-bound, max=bound).astype(kind)


def setup_inputs(seed: int = 0) -> dict:
    key_of = jax.random.split(jax.random.key(seed), 10)
    return {
        "pops_first": jnp.clip(0.02 + 0.08 * jax.random.uniform(key_of[0], (19, NX, NY, NZ), jnp.float32) ** steps_of(key_of[0], (19, NX, NY, NZ), ((1, 8), (2, 16)), -0.2, 0.2), 0.02, 0.1),
        "pops_second": jnp.clip(0.02 + 0.08 * jax.random.uniform(key_of[1], (19, NX, NY, NZ), jnp.float32) ** steps_of(key_of[1], (19, NX, NY, NZ), ((1, 8), (2, 16)), -0.2, 0.2), 0.02, 0.1),
        "phase_first": jnp.clip(jax.random.uniform(key_of[2], (NX, NY, NZ), jnp.float32, -1.0, 1.0) * steps_of(key_of[2], (NX, NY, NZ), ((0, 8), (1, 16)), -0.4, 0.0), -1.0, 1.0),
        "phase_second": jnp.clip(jax.random.uniform(key_of[3], (NX, NY, NZ), jnp.float32, -1.0, 1.0) * steps_of(key_of[3], (NX, NY, NZ), ((0, 8), (1, 16)), -0.4, 0.0), -1.0, 1.0),
        "adjoint_last": centred(key_of[4], (19, NX, NY, NZ), 1.0, 6.0, ((1, 8), (2, 16)), jnp.float32),
        "wettability": jnp.clip(jax.random.uniform(key_of[5], (PATCHES,), jnp.float32, -0.8, 0.8), -0.8, 0.8),
        "fluid": draw_fluid(jax.random.fold_in(key_of[9], 71), 0),
        "wall": draw_wall(jax.random.fold_in(key_of[9], 71), 0),
        "patch": draw_patch(jax.random.fold_in(key_of[9], 71), 0),
    }


lattice_vel = ((0, 0, 0), (1, 0, 0), (-1, 0, 0), (0, 1, 0), (0, -1, 0), (0, 0, 1), (0, 0, -1), (1, 1, 0), (-1, -1, 0), (1, -1, 0), (-1, 1, 0), (1, 0, 1), (-1, 0, -1), (1, 0, -1), (-1, 0, 1), (0, 1, 1), (0, -1, -1), (0, 1, -1), (0, -1, 1))
lattice_wts = (1.0 / 3.0,) + (1.0 / 18.0,) * 6 + (1.0 / 36.0,) * 12
opposite = (0, 2, 1, 4, 3, 6, 5, 8, 7, 10, 9, 12, 11, 14, 13, 16, 15, 18, 17)
strength = 2.0
relax_heavy = 1.0
relax_light = 0.7

def collide(pops, grad, omega):
    vel = jnp.asarray(lattice_vel, dtype=jnp.float32)
    wts = jnp.asarray(lattice_wts, dtype=jnp.float32).reshape(19, 1, 1, 1)
    density = lax.optimization_barrier(jnp.sum(pops, axis=0))
    momentum = jnp.einsum('id,ixyz->dxyz', vel, pops, precision=lax.Precision.HIGHEST)
    speed = momentum / density
    along = jnp.einsum('id,dxyz->ixyz', vel, speed, precision=lax.Precision.HIGHEST)
    usq = lax.optimization_barrier(jnp.sum(speed * speed, axis=0))
    equil = wts * density * (1.0 + 3.0 * along + 4.5 * along * along - 1.5 * usq)
    normal = jnp.einsum('id,dxyz->ixyz', vel, grad, precision=lax.Precision.HIGHEST)
    nsq = lax.optimization_barrier(jnp.sum(grad * grad, axis=0))
    extra = strength * wts * (normal * normal - nsq / 3.0) / jnp.sqrt(1.0 + nsq)
    return pops - omega * (pops - equil) + extra

def shift_field(field, move):
    return jnp.roll(field, (-move[0], -move[1], -move[2]), axis=(-3, -2, -1))

def color_gradient(phi):
    total = [jnp.zeros_like(phi), jnp.zeros_like(phi), jnp.zeros_like(phi)]
    for i in range(1, 19):
        moved = shift_field(phi, lattice_vel[i])
        for d in range(3):
            if lattice_vel[i][d] != 0:
                total[d] = total[d] + 3.0 * lattice_wts[i] * lattice_vel[i][d] * moved
    return jnp.stack(total)

def gradient_back(dgrad):
    result = jnp.zeros_like(dgrad[0])
    for i in range(1, 19):
        move = lattice_vel[i]
        proj = move[0] * dgrad[0] + move[1] * dgrad[1] + move[2] * dgrad[2]
        result = result + 3.0 * lattice_wts[i] * shift_field(proj, (-move[0], -move[1], -move[2]))
    return result

def propagate_back(adjoint, fluid_w):
    rows = []
    for i in range(19):
        move = lattice_vel[i]
        ahead = shift_field(fluid_w, move)
        rows.append(fluid_w * (ahead * shift_field(adjoint[i], move) + (1.0 - ahead) * adjoint[opposite[i]]))
    return jnp.stack(rows)

def collide_back(pops, grad, omega, post):
    blocks = NX // CX

    def split(field):
        return jnp.moveaxis(field.reshape((field.shape[0], blocks, CX) + field.shape[2:]), 1, 0)

    def join(field):
        moved = jnp.moveaxis(field, 0, 1)
        return moved.reshape((moved.shape[0], NX) + moved.shape[3:])

    def single(items):
        block_pops, block_grad, block_omega, block_post = items
        _, pull = jax.vjp(lambda a, b: collide(a, b, block_omega), block_pops, block_grad)
        return pull(block_post)
    adjoint, dgrad = lax.map(single, (split(pops), split(grad), omega.reshape(blocks, CX, NY, NZ), split(post)))
    return (join(adjoint), join(dgrad))

def reference(pops_first, pops_second, phase_first, phase_second, adjoint_last, wettability, fluid, wall, patch):
    fluid_w = fluid.astype(jnp.float32)
    wall_w = wall.astype(jnp.float32)
    contact = wall_w * wettability[patch]
    adjoint = adjoint_last
    total = jnp.zeros((PATCHES,), jnp.float32)
    for pops, phase in ((pops_second, phase_second), (pops_first, phase_first)):
        phi = fluid_w * phase + contact
        grad = color_gradient(phi)
        omega = 1.0 / (relax_heavy * (1.0 + phase) * 0.5 + relax_light * (1.0 - phase) * 0.5)
        post = propagate_back(adjoint, fluid_w)
        adjoint, dgrad = collide_back(pops, grad, omega, post)
        dphi = gradient_back(dgrad)
        total = total + jax.ops.segment_sum((dphi * wall_w).reshape(-1), patch.reshape(-1), num_segments=PATCHES)
    return (adjoint, total)
```

```python
import functools

import jax
import jax.numpy as jnp
from jax import lax
from jax.experimental import pallas as pl
from jax.experimental.pallas import tpu as pltpu
from jax.sharding import PartitionSpec as P

lattice_vel = (
    (0, 0, 0),
    (1, 0, 0),
    (-1, 0, 0),
    (0, 1, 0),
    (0, -1, 0),
    (0, 0, 1),
    (0, 0, -1),
    (1, 1, 0),
    (-1, -1, 0),
    (1, -1, 0),
    (-1, 1, 0),
    (1, 0, 1),
    (-1, 0, -1),
    (1, 0, -1),
    (-1, 0, 1),
    (0, 1, 1),
    (0, -1, -1),
    (0, 1, -1),
    (0, -1, 1),
)
opposite = (0, 2, 1, 4, 3, 6, 5, 8, 7, 10, 9, 12, 11, 14, 13, 16, 15, 18, 17)
relax_heavy = 1.0
relax_light = 0.7

x_plus = (1, 7, 9, 11, 13)
x_minus = (2, 8, 10, 12, 14)
y_plus = (3, 7, 10, 15, 17)
y_minus = (4, 8, 9, 16, 18)

NX = 16
NY = 8
NZ = 128
WX = NX + 2
LOW = 8
ROWS = 24
FIELDS = 5
f32 = jnp.float32


def tile(ref, lead, x, move):
    index = lead + (x + 1 + move[0], pl.ds(LOW + move[1], NY), slice(None))
    value = ref[index]
    if move[2]:
        value = pltpu.roll(value, (-move[2]) % NZ, 1)
    return value


def pack_x_kernel(adj_a, adj_b, *refs):
    firsts, lasts, up, down = refs[:FIELDS], refs[FIELDS : 2 * FIELDS], refs[-2], refs[-1]
    for k in range(5):
        up[k] = adj_a[x_plus[k], 0]
        down[k] = adj_b[x_minus[k], 0]
    for k in range(FIELDS):
        up[5 + k] = firsts[k][0].astype(f32)
        down[5 + k] = lasts[k][0].astype(f32)


def pack_x(adjoint, fields):
    first4 = pl.BlockSpec((19, 1, NY, NZ), lambda i: (0, 0, 0, 0))
    last4 = pl.BlockSpec((19, 1, NY, NZ), lambda i: (0, NX - 1, 0, 0))
    first3 = pl.BlockSpec((1, NY, NZ), lambda i: (0, 0, 0))
    last3 = pl.BlockSpec((1, NY, NZ), lambda i: (NX - 1, 0, 0))
    face = jax.ShapeDtypeStruct((5 + FIELDS, NY, NZ), f32)
    whole = pl.BlockSpec((5 + FIELDS, NY, NZ), lambda i: (0, 0, 0))
    return pl.pallas_call(
        pack_x_kernel,
        grid=(1,),
        in_specs=[first4, last4] + [first3] * FIELDS + [last3] * FIELDS,
        out_specs=[whole, whole],
        out_shape=[face, face],
        name="pack_x",
    )(adjoint, adjoint, *fields, *fields)


def pack_rows(out, slot, own, index, row, low, high):
    flat = own.reshape(own.shape[0] * NX * NY, NZ) if len(own.shape) == 4 else own.reshape(NX * NY, NZ)
    start = (index or 0) * NX * NY + row
    value = flat[pl.ds(start, NX, stride=NY), :]
    out[pl.ds(slot * WX + 1, NX), :] = value.astype(f32)
    if low is not None:
        out[pl.ds(slot * WX, 1), :] = low[0][low[1], pl.ds(row, 1), :]
    if high is not None:
        out[pl.ds(slot * WX + WX - 1, 1), :] = high[0][high[1], pl.ds(row, 1), :]


def pack_pops_y(adj, low, high, up, down):
    for out, pops, row in ((up, y_plus, 0), (down, y_minus, NY - 1)):
        for k, p in enumerate(pops):
            move = lattice_vel[p][0]
            pack_rows(
                out,
                k,
                adj,
                p,
                row,
                (low, x_minus.index(p)) if move < 0 else None,
                (high, x_plus.index(p)) if move > 0 else None,
            )


def pack_y_kernel(adj, *refs):
    fields, low, high, up, down = refs[:FIELDS], refs[-4], refs[-3], refs[-2], refs[-1]
    pack_pops_y(adj, low, high, up, down)
    for out, row in ((up, 0), (down, NY - 1)):
        for k in range(FIELDS):
            pack_rows(out, 5 + k, fields[k], None, row, (low, 5 + k), (high, 5 + k))


def pack_y(adjoint, fields, low, high):
    rows = (5 + FIELDS) * WX
    out = jax.ShapeDtypeStruct((rows, NZ), f32)
    return pl.pallas_call(pack_y_kernel, out_shape=[out, out], name="pack_y")(
        adjoint, *fields, low, high
    )


def pack_y_second_kernel(adj, low, high, up, down):
    pack_pops_y(adj, low, high, up, down)


def pack_y_second(adjoint, low, high):
    out = jax.ShapeDtypeStruct((5 * WX, NZ), f32)
    return pl.pallas_call(pack_y_second_kernel, out_shape=[out, out], name="pack_y_second")(
        adjoint, low, high
    )


def fill_rows(pad, lead, row, buf, slot):
    for x in range(WX):
        pad[lead + (x, pl.ds(row, 1), slice(None))] = buf[pl.ds(slot * WX + x, 1), :]


def fill_pops(pad, adj, x_low, x_high, y_low, y_high):
    def copy(x, carry):
        for p in range(19):
            pad[p, x + 1, pl.ds(LOW, NY), :] = adj[p, x]
        return carry

    lax.fori_loop(0, NX, copy, 0)
    for k in range(5):
        pad[x_minus[k], 0, pl.ds(LOW, NY), :] = x_low[k]
        pad[x_plus[k], WX - 1, pl.ds(LOW, NY), :] = x_high[k]
        fill_rows(pad, (y_minus[k],), LOW - 1, y_low, k)
        fill_rows(pad, (y_plus[k],), LOW + NY, y_high, k)


def fill_field(pad, lead, own, slot, x_low, x_high, y_low, y_high):
    for x in range(NX):
        pad[lead + (x + 1, pl.ds(LOW, NY), slice(None))] = own[x].astype(f32)
    pad[lead + (0, pl.ds(LOW, NY), slice(None))] = x_low[5 + slot]
    pad[lead + (WX - 1, pl.ds(LOW, NY), slice(None))] = x_high[5 + slot]
    fill_rows(pad, lead, LOW - 1, y_low, 5 + slot)
    fill_rows(pad, lead, LOW + NY, y_high, 5 + slot)


def look_up(table, index):
    high = lax.shift_right_logical(index, 7)
    low = index & 127
    result = jnp.zeros(index.shape, f32)
    for r in range(32):
        row = jnp.broadcast_to(table[pl.ds(r, 1), :], index.shape)
        picked = jnp.take_along_axis(row, low, axis=1, mode="promise_in_bounds")
        result = jnp.where(high == r, picked, result)
    return result


def gradient(view):
    sixth, twelfth = 1.0 / 6.0, 1.0 / 12.0

    def diff(a, b):
        return view(a) - view(b)

    xy = diff((1, 1, 0), (-1, -1, 0))
    xmy = diff((1, -1, 0), (-1, 1, 0))
    xz = diff((1, 0, 1), (-1, 0, -1))
    xmz = diff((1, 0, -1), (-1, 0, 1))
    yz = diff((0, 1, 1), (0, -1, -1))
    ymz = diff((0, 1, -1), (0, -1, 1))
    gx = sixth * diff((1, 0, 0), (-1, 0, 0)) + twelfth * (xy + xmy + xz + xmz)
    gy = sixth * diff((0, 1, 0), (0, -1, 0)) + twelfth * (xy - xmy + yz + ymz)
    gz = sixth * diff((0, 0, 1), (0, 0, -1)) + twelfth * (xz - xmz + yz - ymz)
    return gx, gy, gz


def moments(q):
    a, b = 1.0 / 18.0, 1.0 / 36.0

    def pair(i):
        return q[i] + q[i + 1], q[i] - q[i + 1]

    (sx, dx), (sy, dy), (sz, dz) = pair(1), pair(3), pair(5)
    (s7, d7), (s9, d9), (s11, d11) = pair(7), pair(9), pair(11)
    (s13, d13), (s15, d15), (s17, d17) = pair(13), pair(15), pair(17)
    xy, xz, yz = s7 + s9, s11 + s13, s15 + s17
    m0 = (1.0 / 3.0) * q[0] + a * (sx + sy + sz) + b * (xy + xz + yz)
    mx = a * dx + b * (d7 + d9 + d11 + d13)
    my = a * dy + b * (d7 - d9 + d15 + d17)
    mz = a * dz + b * (d11 - d13 + d15 - d17)
    mxx = a * sx + b * (xy + xz)
    myy = a * sy + b * (xy + yz)
    mzz = a * sz + b * (xz + yz)
    return m0, (mx, my, mz), (mxx, myy, mzz, b * (s7 - s9), b * (s11 - s13), b * (s15 - s17))


def velocity(f):
    density = f[0]
    for i in range(1, 19):
        density = density + f[i]
    d = {i: f[i] - f[i + 1] for i in range(1, 19, 2)}
    inv = 1.0 / density
    ux = (d[1] + d[7] + d[9] + d[11] + d[13]) * inv
    uy = (d[3] + d[7] - d[9] + d[15] + d[17]) * inv
    uz = (d[5] + d[11] - d[13] + d[15] - d[17]) * inv
    return ux, uy, uz


def apply_second(second, v):
    mxx, myy, mzz, mxy, mxz, myz = second
    x, y, z = v
    return (
        mxx * x + mxy * y + mxz * z,
        mxy * x + myy * y + myz * z,
        mxz * x + myz * y + mzz * z,
    )


def dot3(a, b):
    return a[0] * b[0] + a[1] * b[1] + a[2] * b[2]


def collide_back(post, f, phase, n, store):
    q0, q1, q2 = moments(post)
    u = velocity(f)
    omega = 1.0 / (relax_heavy * (1.0 + phase) * 0.5 + relax_light * (1.0 - phase) * 0.5)
    q2u = apply_second(q2, u)
    along = q0 - 4.5 * dot3(u, q2u) + 1.5 * dot3(u, u) * q0
    base = omega * along
    bx, by, bz = [omega * (3.0 * q1[d] + 9.0 * q2u[d] - 3.0 * u[d] * q0) for d in range(3)]
    keep = 1.0 - omega
    store(0, keep * post[0] + base)
    slopes = (bx, by, bz, bx + by, bx - by, bx + bz, bx - bz, by + bz, by - bz)
    for k, slope in enumerate(slopes):
        i = 1 + 2 * k
        store(i, keep * post[i] + (base + slope))
        store(i + 1, keep * post[i + 1] + (base - slope))
    nsq = dot3(n, n)
    root = 1.0 / jnp.sqrt(1.0 + nsq)
    q2n = apply_second(q2, n)
    energy = dot3(n, q2n) - (1.0 / 3.0) * nsq * q0
    third = (4.0 / 3.0) * q0
    tail = 2.0 * energy * root * root * root
    return [root * (4.0 * q2n[d] - third * n[d]) - tail * n[d] for d in range(3)]


def propagate_back(adj_pad, fluid_pad, x):
    here = tile(fluid_pad, (), x, (0, 0, 0))
    post = [here * adj_pad[0, x + 1, pl.ds(LOW, NY), :]]
    for i in range(1, 19):
        ahead = tile(fluid_pad, (), x, lattice_vel[i])
        moved = tile(adj_pad, (i,), x, lattice_vel[i])
        back = adj_pad[opposite[i], x + 1, pl.ds(LOW, NY), :]
        post.append(here * jnp.where(ahead != 0.0, moved, back))
    return post


def second_kernel(
    pops, phase_a, phase_b, adj, table, fluid, wall, patch,
    x_low, x_high, y_low, y_high,
    adj_out, dgrad_out, grad_out, up, down,
    adj_pad, field_pad, phi_pad,
):
    own = (phase_a, phase_b, fluid, wall, patch)
    for k in range(FIELDS):
        fill_field(field_pad, (k,), own[k], k, x_low, x_high, y_low, y_high)
    fill_pops(adj_pad, adj, x_low, x_high, y_low, y_high)

    def imposed(x, carry):
        for rows in (pl.ds(LOW - 1, NY), pl.ds(LOW + NY - 1, NY)):
            index = field_pad[4, x, rows, :].astype(jnp.int32) & 4095
            contact = field_pad[3, x, rows, :] * look_up(table, index)
            wet = field_pad[2, x, rows, :]
            phi_pad[0, x, rows, :] = wet * field_pad[0, x, rows, :] + contact
            phi_pad[1, x, rows, :] = wet * field_pad[1, x, rows, :] + contact
        return carry

    lax.fori_loop(0, WX, imposed, 0)

    def plane(x, carry):
        first = gradient(lambda move: tile(phi_pad, (0,), x, move))
        for d in range(3):
            grad_out[d, x] = first[d]
        n = gradient(lambda move: tile(phi_pad, (1,), x, move))
        post = propagate_back(adj_pad, field_pad.at[2], x)

        def store(i, value):
            adj_out[i, x] = value

        dgrad = collide_back(post, [pops[i, x] for i in range(19)], phase_b[x], n, store)
        for d in range(3):
            dgrad_out[d, x] = dgrad[d]
        return carry

    lax.fori_loop(0, NX, plane, 0)
    for k in range(5):
        up[k] = adj_out[x_plus[k], 0]
        down[k] = adj_out[x_minus[k], NX - 1]


def second_step(pops, phase_a, phase_b, adj, table, fluid, wall, patch, *halo):
    block = jax.ShapeDtypeStruct((19, NX, NY, NZ), f32)
    vector = jax.ShapeDtypeStruct((3, NX, NY, NZ), f32)
    face = jax.ShapeDtypeStruct((5, NY, NZ), f32)
    return pl.pallas_call(
        second_kernel,
        out_shape=[block, vector, vector, face, face],
        scratch_shapes=[
            pltpu.VMEM((19, WX, ROWS, NZ), f32),
            pltpu.VMEM((FIELDS, WX, ROWS, NZ), f32),
            pltpu.VMEM((2, WX, ROWS, NZ), f32),
        ],
        compiler_params=pltpu.CompilerParams(vmem_limit_bytes=48 * 1024 * 1024),
        name="second_step",
    )(pops, phase_a, phase_b, adj, table, fluid, wall, patch, *halo)


def first_kernel(
    pops, phase, adj, dgrad_in, grad, fluid, wall, patch,
    x_low, x_high, y_low, y_high, x_low2, x_high2, y_low2, y_high2,
    adj_out, total_out,
    adj_pad, field_pad, dgrad_pad, acc,
):
    for k, own in ((2, fluid), (3, wall), (4, patch)):
        slot = k - 2
        field_pad[slot, :, pl.ds(0, LOW), :] = jnp.zeros((WX, LOW, NZ), f32)
        field_pad[slot, :, pl.ds(LOW + NY, LOW), :] = jnp.zeros((WX, LOW, NZ), f32)
        fill_field(field_pad, (slot,), own, k, x_low, x_high, y_low, y_high)
    fill_pops(adj_pad, adj, x_low2, x_high2, y_low2, y_high2)
    dgrad_pad[...] = jnp.zeros_like(dgrad_pad)
    acc[...] = jnp.zeros_like(acc)

    def plane(x, carry):
        post = propagate_back(adj_pad, field_pad.at[0], x)

        def store(i, value):
            adj_out[i, x] = value

        n = [grad[d, x] for d in range(3)]
        dgrad = collide_back(post, [pops[i, x] for i in range(19)], phase[x], n, store)
        for d in range(3):
            dgrad_pad[d, x + 2, pl.ds(LOW, NY), :] = dgrad[d] + dgrad_in[d, x]
        return carry

    lax.fori_loop(0, NX, plane, 0)

    row_iota = lax.broadcasted_iota(jnp.int32, (64, NZ), 0)

    def scatter(x, carry):
        lefts, rights = [], []
        for start, count in ((LOW - 1, NY), (LOW + NY - 1, 2)):

            def view(d, move):
                value = dgrad_pad[d, x + 1 + move[0], pl.ds(start + move[1], NY), :]
                if move[2]:
                    value = pltpu.roll(value, (-move[2]) % NZ, 1)
                return value

            gx = gradient_part(lambda m: view(0, m), 0)
            gy = gradient_part(lambda m: view(1, m), 1)
            gz = gradient_part(lambda m: view(2, m), 2)
            on_wall = field_pad[1, x, pl.ds(start, NY), :]
            value = -(gx + gy + gz) * on_wall
            index = field_pad[2, x, pl.ds(start, NY), :].astype(jnp.int32)
            key = (lax.shift_right_logical(index, 6) & 1) * 32 + lax.shift_right_logical(index, 7)
            low = index & 63
            big = value.astype(jnp.bfloat16).astype(f32)
            small = value - big
            for r in range(count):
                hit = row_iota == key[r : r + 1, :]
                left = jnp.concatenate(
                    [jnp.where(hit, big[r : r + 1, :], 0.0), jnp.where(hit, small[r : r + 1, :], 0.0)], axis=0
                )
                lefts.append(left.astype(jnp.bfloat16))
                rights.append((row_iota == low[r : r + 1, :]).astype(f32).astype(jnp.bfloat16))
        left = jnp.concatenate(lefts, axis=1)
        right = jnp.concatenate(rights, axis=1)
        acc[...] += lax.dot_general(
            left, right, (((1,), (1,)), ((), ())), preferred_element_type=f32
        )
        return carry

    lax.fori_loop(0, WX, scatter, 0)
    both = acc[pl.ds(0, 64), :] + acc[pl.ds(64, 64), :]
    total_out[...] = jnp.concatenate([both[:32], both[32:]], axis=1)


def gradient_part(view, d):
    result = None
    for i in range(1, 19, 2):
        move = lattice_vel[i]
        if move[d] == 0:
            continue
        term = view(move) - view(lattice_vel[i + 1])
        weight = 1.0 / 6.0 if i < 7 else 1.0 / 12.0
        if move[d] < 0:
            weight = -weight
        result = weight * term if result is None else result + weight * term
    return result


def first_step(*args):
    block = jax.ShapeDtypeStruct((19, NX, NY, NZ), f32)
    total = jax.ShapeDtypeStruct((32, NZ), f32)
    return pl.pallas_call(
        first_kernel,
        out_shape=[block, total],
        scratch_shapes=[
            pltpu.VMEM((19, WX, ROWS, NZ), f32),
            pltpu.VMEM((3, WX, ROWS, NZ), f32),
            pltpu.VMEM((3, WX + 2, ROWS, NZ), f32),
            pltpu.VMEM((128, 64), f32),
        ],
        compiler_params=pltpu.CompilerParams(vmem_limit_bytes=48 * 1024 * 1024),
        name="first_step",
    )(*args)


def ring(axis, value, step):
    count = lax.axis_size(axis)
    return lax.ppermute(value, axis, [(i, (i + step) % count) for i in range(count)])


def group_sum(value, axis, stride, size):
    count = lax.axis_size(axis)
    got = []
    for s in range(1, size):
        pairs = []
        for i in range(count):
            digit = (i // stride) % size
            pairs.append((i, i + ((digit + s) % size - digit) * stride))
        got.append(lax.ppermute(value, axis, pairs))
    for part in got:
        value = value + part
    return value


def shards(
    pops_first,
    pops_second,
    phase_first,
    phase_second,
    adjoint_last,
    wettability,
    fluid,
    wall,
    patch,
):
    table = wettability.reshape(32, NZ)
    fields = (phase_first, phase_second, fluid, wall, patch)
    up, down = pack_x(adjoint_last, fields)
    x_high, x_low = ring("pipe", up, -1), ring("pipe", down, 1)
    up, down = pack_y(adjoint_last, fields, x_low, x_high)
    y_high, y_low = ring("cross", up, -1), ring("cross", down, 1)
    halo = (x_low, x_high, y_low, y_high)
    adjoint, dgrad, grad, up, down = second_step(
        pops_second, phase_first, phase_second, adjoint_last, table, fluid, wall, patch, *halo
    )
    x_high2, x_low2 = ring("pipe", up, -1), ring("pipe", down, 1)
    up, down = pack_y_second(adjoint, x_low2, x_high2)
    y_high2, y_low2 = ring("cross", up, -1), ring("cross", down, 1)
    adjoint, total = first_step(
        pops_first, phase_first, adjoint, dgrad, grad, fluid, wall, patch,
        *halo, x_low2, x_high2, y_low2, y_high2,
    )
    total = group_sum(total, "pipe", 1, 2)
    total = group_sum(total, "pipe", 2, 4)
    total = group_sum(total, "cross", 1, 4)
    total = group_sum(total, "cross", 4, 4)
    return adjoint, total.reshape(wettability.shape)


def solution(mesh):
    return jax.shard_map(
        shards,
        mesh=mesh,
        in_specs=(
            P(None, "pipe", "cross", None),
            P(None, "pipe", "cross", None),
            P("pipe", "cross", None),
            P("pipe", "cross", None),
            P(None, "pipe", "cross", None),
            P(),
            P("pipe", "cross", None),
            P("pipe", "cross", None),
            P("pipe", "cross", None),
        ),
        out_specs=(P(None, "pipe", "cross", None), P()),
        check_vma=False,
    )
```

```python
import functools

import jax
import jax.numpy as jnp
from jax import lax
from jax.experimental import pallas as pl
from jax.experimental.pallas import tpu as pltpu
from jax.sharding import PartitionSpec as P

lattice_vel = (
    (0, 0, 0),
    (1, 0, 0),
    (-1, 0, 0),
    (0, 1, 0),
    (0, -1, 0),
    (0, 0, 1),
    (0, 0, -1),
    (1, 1, 0),
    (-1, -1, 0),
    (1, -1, 0),
    (-1, 1, 0),
    (1, 0, 1),
    (-1, 0, -1),
    (1, 0, -1),
    (-1, 0, 1),
    (0, 1, 1),
    (0, -1, -1),
    (0, 1, -1),
    (0, -1, 1),
)
opposite = (0, 2, 1, 4, 3, 6, 5, 8, 7, 10, 9, 12, 11, 14, 13, 16, 15, 18, 17)
relax_heavy = 1.0
relax_light = 0.7

x_plus = (1, 7, 9, 11, 13)
x_minus = (2, 8, 10, 12, 14)
y_plus = (3, 7, 10, 15, 17)
y_minus = (4, 8, 9, 16, 18)

NX = 16
NY = 8
NZ = 128
WX = NX + 2
LOW = 8
ROWS = 24
FIELDS = 5
f32 = jnp.float32


def tile(ref, lead, x, move):
    index = lead + (x + 1 + move[0], pl.ds(LOW + move[1], NY), slice(None))
    value = ref[index]
    if move[2]:
        value = pltpu.roll(value, (-move[2]) % NZ, 1)
    return value


def look_up(table, index):
    high = lax.shift_right_logical(index, 7)
    low = index & 127
    result = jnp.zeros(index.shape, f32)
    for r in range(32):
        row = jnp.broadcast_to(table[pl.ds(r, 1), :], index.shape)
        picked = jnp.take_along_axis(row, low, axis=1, mode="promise_in_bounds")
        result = jnp.where(high == r, picked, result)
    return result


def roll_z(value, step):
    return pltpu.roll(value, (-step) % NZ, 1)


def gradient(view):
    sixth, twelfth = 1.0 / 6.0, 1.0 / 12.0
    east, west, north, south = view(1, 0), view(-1, 0), view(0, 1), view(0, -1)
    dx, dy = east - west, north - south
    xy = view(1, 1) - view(-1, -1)
    xmy = view(1, -1) - view(-1, 1)
    along = sixth * view(0, 0) + twelfth * (east + west + north + south)
    gx = sixth * dx + twelfth * (xy + xmy + roll_z(dx, 1) + roll_z(dx, -1))
    gy = sixth * dy + twelfth * (xy - xmy + roll_z(dy, 1) + roll_z(dy, -1))
    return gx, gy, roll_z(along, 1) - roll_z(along, -1)


def moments(q):
    a, b = 1.0 / 18.0, 1.0 / 36.0

    def pair(i):
        return q[i] + q[i + 1], q[i] - q[i + 1]

    (sx, dx), (sy, dy), (sz, dz) = pair(1), pair(3), pair(5)
    (s7, d7), (s9, d9), (s11, d11) = pair(7), pair(9), pair(11)
    (s13, d13), (s15, d15), (s17, d17) = pair(13), pair(15), pair(17)
    xy, xz, yz = s7 + s9, s11 + s13, s15 + s17
    m0 = (1.0 / 3.0) * q[0] + a * (sx + sy + sz) + b * (xy + xz + yz)
    mx = a * dx + b * (d7 + d9 + d11 + d13)
    my = a * dy + b * (d7 - d9 + d15 + d17)
    mz = a * dz + b * (d11 - d13 + d15 - d17)
    mxx = a * sx + b * (xy + xz)
    myy = a * sy + b * (xy + yz)
    mzz = a * sz + b * (xz + yz)
    return m0, (mx, my, mz), (mxx, myy, mzz, b * (s7 - s9), b * (s11 - s13), b * (s15 - s17))


def velocity(f):
    density = f[0]
    for i in range(1, 19):
        density = density + f[i]
    d = {i: f[i] - f[i + 1] for i in range(1, 19, 2)}
    inv = 1.0 / density
    ux = (d[1] + d[7] + d[9] + d[11] + d[13]) * inv
    uy = (d[3] + d[7] - d[9] + d[15] + d[17]) * inv
    uz = (d[5] + d[11] - d[13] + d[15] - d[17]) * inv
    return ux, uy, uz


def apply_second(second, v):
    mxx, myy, mzz, mxy, mxz, myz = second
    x, y, z = v
    return (
        mxx * x + mxy * y + mxz * z,
        mxy * x + myy * y + myz * z,
        mxz * x + myz * y + mzz * z,
    )


def dot3(a, b):
    return a[0] * b[0] + a[1] * b[1] + a[2] * b[2]


def collide_back(post, q, f, phase, store):
    q0, q1, q2 = q
    u = velocity(f)
    omega = 1.0 / (relax_heavy * (1.0 + phase) * 0.5 + relax_light * (1.0 - phase) * 0.5)
    q2u = apply_second(q2, u)
    along = q0 - 4.5 * dot3(u, q2u) + 1.5 * dot3(u, u) * q0
    base = omega * along
    bx, by, bz = [omega * (3.0 * q1[d] + 9.0 * q2u[d] - 3.0 * u[d] * q0) for d in range(3)]
    keep = 1.0 - omega
    store(0, keep * post[0] + base)
    slopes = (bx, by, bz, bx + by, bx - by, bx + bz, bx - bz, by + bz, by - bz)
    for k, slope in enumerate(slopes):
        i = 1 + 2 * k
        store(i, keep * post[i] + (base + slope))
        store(i + 1, keep * post[i + 1] + (base - slope))


def gradient_back(q0, q2, n):
    nsq = dot3(n, n)
    root = 1.0 / jnp.sqrt(1.0 + nsq)
    q2n = apply_second(q2, n)
    energy = dot3(n, q2n) - (1.0 / 3.0) * nsq * q0
    third = (4.0 / 3.0) * q0
    tail = 2.0 * energy * root * root * root
    return [root * (4.0 * q2n[d] - third * n[d]) - tail * n[d] for d in range(3)]


def gradient_adjoint(view):
    sixth, twelfth = 1.0 / 6.0, 1.0 / 12.0
    xe, xw, yn, ys = view(0, 1, 0), view(0, -1, 0), view(1, 0, 1), view(1, 0, -1)
    zc = sixth * view(2, 0, 0)
    around = view(2, 1, 0) + view(2, -1, 0) + view(2, 0, 1) + view(2, 0, -1)
    across = xe - xw + yn - ys
    flat = sixth * across + twelfth * (
        view(0, 1, 1) + view(1, 1, 1) - view(0, -1, -1) - view(1, -1, -1)
        + view(0, 1, -1) - view(1, 1, -1) - view(0, -1, 1) + view(1, -1, 1)
    )
    ahead = zc + twelfth * (across + around)
    behind = twelfth * (across - around) - zc
    return -(flat + roll_z(ahead, 1) + roll_z(behind, -1))


def side_adjoint(rows, sign):
    sixth, twelfth = 1.0 / 6.0, 1.0 / 12.0
    gx, gy, gz = [lambda move, d=d: rows[d, pl.ds(1 + move, WX), :] for d in range(3)]
    flat = sixth * sign * gy(0) + twelfth * (sign * (gy(1) + gy(-1)) + gx(1) - gx(-1))
    return -(flat + twelfth * (roll_z(sign * gy(0) + gz(0), 1) + roll_z(sign * gy(0) - gz(0), -1)))


def whole_call(kernel, name, out_shape, args, scratch=(), aliases=None, in_hbm=False):
    options = {}
    if in_hbm:
        options["in_specs"] = [pl.BlockSpec(memory_space=pl.ANY)] * len(args)
    else:
        options["compiler_params"] = pltpu.CompilerParams(vmem_limit_bytes=24 * 1024 * 1024)
    return pl.pallas_call(
        kernel,
        out_shape=[jax.ShapeDtypeStruct(shape, kind) for shape, kind in out_shape],
        scratch_shapes=scratch,
        input_output_aliases=aliases or {},
        name=name,
        **options,
    )(*args)


def take_rows(out, slot, flat, start):
    out[pl.ds(slot * NX, NX), :] = flat[pl.ds(start, NX, stride=NY), :].astype(f32)


def pack_kernel(adj_hbm, *refs):
    hbm, (x_up, x_down, y_up, y_down), (adj, *fields) = refs[:FIELDS], refs[FIELDS : FIELDS + 4], refs[FIELDS + 4 : -1]
    sem = refs[-1]
    copies = [pltpu.make_async_copy(adj_hbm, adj, sem.at[0])]
    for k in range(FIELDS):
        copies.append(pltpu.make_async_copy(hbm[k], fields[k], sem.at[k + 1]))
    for copy in copies:
        copy.start()
    for copy in copies:
        copy.wait()
    flat = adj.reshape(19 * NX * NY, NZ)
    for k in range(5):
        x_up[k] = adj[x_plus[k], 0]
        x_down[k] = adj[x_minus[k], NX - 1]
        take_rows(y_up, k, flat, y_plus[k] * NX * NY)
        take_rows(y_down, k, flat, y_minus[k] * NX * NY + NY - 1)
    for k in range(FIELDS):
        x_up[5 + k] = fields[k][0].astype(f32)
        x_down[5 + k] = fields[k][NX - 1].astype(f32)
        rows = fields[k].reshape(NX * NY, NZ)
        take_rows(y_up, 5 + k, rows, 0)
        take_rows(y_down, 5 + k, rows, NY - 1)


def pack(adjoint, fields):
    face, side = ((5 + FIELDS, NY, NZ), f32), (((5 + FIELDS) * NX, NZ), f32)
    scratch = [pltpu.VMEM((19, NX, NY, NZ), f32)]
    scratch += [pltpu.VMEM((NX, NY, NZ), field.dtype) for field in fields]
    scratch.append(pltpu.SemaphoreType.DMA((1 + FIELDS,)))
    return whole_call(pack_kernel, "pack", [face, face, side, side], (adjoint, *fields), scratch, in_hbm=True)


edge_up = (10, 7)
edge_down = (8, 9)


def pack_edges_kernel(count, low, high, _, up, down):
    for out, pops, row in ((up, edge_up, 0), (down, edge_down, NY - 1)):
        out[pl.ds(0, 1), :] = low[x_minus.index(pops[0]), pl.ds(row, 1), :]
        out[pl.ds(1, 1), :] = high[x_plus.index(pops[1]), pl.ds(row, 1), :]
        for k in range(count):
            out[pl.ds(2 + k, 1), :] = low[5 + k, pl.ds(row, 1), :]
            out[pl.ds(2 + count + k, 1), :] = high[5 + k, pl.ds(row, 1), :]
        used = 2 + 2 * count
        size = out.shape[0]
        out[pl.ds(used, size - used), :] = jnp.zeros((size - used, NZ), f32)


def pack_edges(low, high, count, after):
    out = ((16 if count else 8, NZ), f32)
    kernel = functools.partial(pack_edges_kernel, count)
    return whole_call(kernel, "pack_edges", [out, out], (low, high, after))


def fill_sides(pad, lead, y_low, low_slot, y_high, high_slot):
    for x in range(NX):
        pad[lead + (x + 1, pl.ds(LOW - 1, 1), slice(None))] = y_low[pl.ds(low_slot * NX + x, 1), :]
        pad[lead + (x + 1, pl.ds(LOW + NY, 1), slice(None))] = y_high[pl.ds(high_slot * NX + x, 1), :]


def fill_pops(pad, adj, planes, y_low, y_high):
    for p in range(19):
        for x in planes:
            pad[p, x + 1, pl.ds(LOW, NY), :] = adj[p, x]
    for k in range(5):
        for x in planes:
            pad[y_minus[k], x + 1, pl.ds(LOW - 1, 1), :] = y_low[pl.ds(k * NX + x, 1), :]
            pad[y_plus[k], x + 1, pl.ds(LOW + NY, 1), :] = y_high[pl.ds(k * NX + x, 1), :]


def fill_pops_outer(pad, x_low, x_high, e_low, e_high):
    for k in range(5):
        pad[x_minus[k], 0, pl.ds(LOW, NY), :] = x_low[k]
        pad[x_plus[k], WX - 1, pl.ds(LOW, NY), :] = x_high[k]
    for row, pops, edge in ((LOW + NY, edge_up, e_high), (LOW - 1, edge_down, e_low)):
        pad[pops[0], 0, pl.ds(row, 1), :] = edge[pl.ds(0, 1), :]
        pad[pops[1], WX - 1, pl.ds(row, 1), :] = edge[pl.ds(1, 1), :]


def fill_field(pad, lead, own, slot, y_low, y_high):
    for x in range(NX):
        pad[lead + (x + 1, pl.ds(LOW, NY), slice(None))] = own[x].astype(f32)
    fill_sides(pad, lead, y_low, 5 + slot, y_high, 5 + slot)


def fill_field_outer(pad, lead, slot, x_low, x_high, e_low, e_high):
    pad[lead + (0, pl.ds(LOW, NY), slice(None))] = x_low[5 + slot]
    pad[lead + (WX - 1, pl.ds(LOW, NY), slice(None))] = x_high[5 + slot]
    for row, edge in ((LOW + NY, e_high), (LOW - 1, e_low)):
        pad[lead + (0, pl.ds(row, 1), slice(None))] = edge[pl.ds(2 + slot, 1), :]
        pad[lead + (WX - 1, pl.ds(row, 1), slice(None))] = edge[pl.ds(2 + FIELDS + slot, 1), :]


def propagate_back(adj_pad, fluid_pad, x):
    here = tile(fluid_pad, (), x, (0, 0, 0))
    post = [here * adj_pad[0, x + 1, pl.ds(LOW, NY), :]]
    for i in range(1, 19):
        ahead = tile(fluid_pad, (), x, lattice_vel[i])
        moved = tile(adj_pad, (i,), x, lattice_vel[i])
        back = adj_pad[opposite[i], x + 1, pl.ds(LOW, NY), :]
        post.append(here * jnp.where(ahead != 0.0, moved, back))
    return post


def step_plane(x, adj_pad, fluid_pad, pops, phase, adj_out, mom_out):
    post = propagate_back(adj_pad, fluid_pad, x)
    q = moments(post)

    def store(i, value):
        adj_out[i, x] = value

    collide_back(post, q, [pops[i, x] for i in range(19)], phase[x], store)
    if mom_out is not None:
        mom_out[0, x] = q[0]
        for k in range(6):
            mom_out[1 + k, x] = q[2][k]


inner = range(1, NX - 1)


def second_inner_kernel(pops, phase, adj, fluid, y_low, y_high, adj_out, mom_out, adj_pad, fluid_pad):
    fill_field(fluid_pad, (), fluid, 2, y_low, y_high)
    fill_pops(adj_pad, adj, range(NX), y_low, y_high)

    def plane(x, carry):
        step_plane(x, adj_pad, fluid_pad, pops, phase, adj_out, mom_out)
        return carry

    lax.fori_loop(1, NX - 1, plane, 0)


block = ((19, NX, NY, NZ), f32)
seven = ((7, NX, NY, NZ), f32)
vector = ((3, NX, NY, NZ), f32)


def pad_scratch():
    return [pltpu.VMEM((19, WX, ROWS, NZ), f32), pltpu.VMEM((WX, ROWS, NZ), f32)]


def second_outer_kernel(
    pops, phase, adj, fluid, y_low, y_high, x_low, x_high, e_low, e_high, adj_in, mom_in,
    adj_out, mom_out, x_up, x_down, y_up, y_down, adj_pad, fluid_pad,
):
    fill_field(fluid_pad, (), fluid, 2, y_low, y_high)
    fill_field_outer(fluid_pad, (), 2, x_low, x_high, e_low, e_high)
    fill_pops(adj_pad, adj, (0, 1, NX - 2, NX - 1), y_low, y_high)
    fill_pops_outer(adj_pad, x_low, x_high, e_low, e_high)
    for x in (0, NX - 1):
        step_plane(x, adj_pad, fluid_pad, pops, phase, adj_out, mom_out)
    flat = adj_out.reshape(19 * NX * NY, NZ)
    for k in range(5):
        x_up[k] = adj_out[x_plus[k], 0]
        x_down[k] = adj_out[x_minus[k], NX - 1]
        take_rows(y_up, k, flat, y_plus[k] * NX * NY)
        take_rows(y_down, k, flat, y_minus[k] * NX * NY + NY - 1)


def one_hots(index, row, hit_out, right_out, at):
    row_iota = lax.broadcasted_iota(jnp.int32, (64, NZ), 0)
    key = (lax.shift_right_logical(index, 6) & 1) * 32 + lax.shift_right_logical(index, 7)
    low = index & 63
    hit = jnp.where(row_iota == key[row : row + 1, :], 1.0, 0.0)
    hit_out[:, pl.ds(at, NZ)] = hit.astype(jnp.bfloat16)
    right = jnp.where(row_iota == low[row : row + 1, :], 1.0, 0.0)
    right_out[:, pl.ds(at, NZ)] = right.astype(jnp.bfloat16)


OWN = NX * NY * NZ
SIDE = WX * NZ
HALO = 2 * NY * NZ + 2 * SIDE


def own_kernel(table, phase_a, phase_b, fluid, wall, patch, phi_out, hit_out, right_out):
    def plane(x, carry):
        index = patch[x] & 4095
        contact = wall[x].astype(f32) * look_up(table, index)
        wet = fluid[x].astype(f32)
        phi_out[0, x] = wet * phase_a[x] + contact
        phi_out[1, x] = wet * phase_b[x] + contact
        for r in range(NY):
            one_hots(index, r, hit_out, right_out, pl.multiple_of((x * NY + r) * NZ, NZ))
        return carry

    lax.fori_loop(0, NX, plane, 0)


def middle_kernel(
    phi, table, fluid, wall, mom, y_low, y_high, x_low, x_high, e_low, e_high,
    dgrad_out, grad_out, fluid_out, wall_own, wall_face, wall_side, hit_out, right_out,
    phi_pad,
):
    fill_field(fluid_out, (), fluid, 2, y_low, y_high)
    fill_field_outer(fluid_out, (), 2, x_low, x_high, e_low, e_high)

    def copy(x, carry):
        for t in range(2):
            phi_pad[t, x + 1, pl.ds(LOW, NY), :] = phi[t, x]
        wall_own[x] = wall[x].astype(f32)
        return carry

    lax.fori_loop(0, NX, copy, 0)

    def imposed(slot):
        index = slot(4).astype(jnp.int32) & 4095
        contact = slot(3) * look_up(table, index)
        return index, [slot(2) * slot(t) + contact for t in range(2)]

    for side, (face, x) in enumerate(((x_low, 0), (x_high, WX - 1))):
        index, values = imposed(lambda k: face[5 + k])
        wall_face[side] = face[8]
        for t in range(2):
            phi_pad[t, x, pl.ds(LOW, NY), :] = values[t]
        for r in range(NY):
            one_hots(index, r, hit_out, right_out, (side * NY + r) * NZ)
    base = 2 * NY * NZ
    for side, (rows, edge, y) in enumerate(((y_low, e_low, LOW - 1), (y_high, e_high, LOW + NY))):
        index, values = imposed(lambda k: rows[pl.ds((5 + k) * NX, NX), :])
        wall_side[side, pl.ds(1, NX), :] = rows[pl.ds(8 * NX, NX), :]
        for x in range(NX):
            for t in range(2):
                phi_pad[t, x + 1, pl.ds(y, 1), :] = values[t][x : x + 1, :]
            one_hots(index, x, hit_out, right_out, base + side * SIDE + (x + 1) * NZ)
    corners = [(edge, first) for edge in (e_low, e_high) for first in (2, 2 + FIELDS)]

    def corner_rows(k):
        rows = [edge[pl.ds(first + k, 1), :] for edge, first in corners]
        return jnp.concatenate(rows + rows, axis=0)

    index, values = imposed(corner_rows)
    on_wall = corner_rows(3)
    for r in range(4):
        side, x, y = r // 2, (WX - 1) * (r % 2), (LOW - 1, LOW + NY)[r // 2]
        wall_side[side, pl.ds(x, 1), :] = on_wall[r : r + 1, :]
        for t in range(2):
            phi_pad[t, x, pl.ds(y, 1), :] = values[t][r : r + 1, :]
        one_hots(index, r, hit_out, right_out, base + side * SIDE + x * NZ)

    def plane(x, carry):
        def view(t):
            return lambda a, b: tile(phi_pad, (t,), x, (a, b, 0))

        first, n = gradient(view(0)), gradient(view(1))
        for d in range(3):
            grad_out[d, x] = first[d]
        dgrad = gradient_back(mom[0, x], [mom[1 + k, x] for k in range(6)], n)
        for d in range(3):
            dgrad_out[d, x] = dgrad[d]
        return carry

    lax.fori_loop(0, NX, plane, 0)


def own_terms(*args):
    hots = ((64, OWN), jnp.bfloat16)
    return whole_call(own_kernel, "own_terms", [((2, NX, NY, NZ), f32), hots, hots], args)


def middle(*args):
    shapes = [vector, vector, ((WX, ROWS, NZ), f32), ((NX, NY, NZ), f32), ((2, NY, NZ), f32), ((2, WX, NZ), f32)]
    shapes += [((64, HALO), jnp.bfloat16)] * 2
    return whole_call(middle_kernel, "middle", shapes, args, [pltpu.VMEM((2, WX, ROWS, NZ), f32)])


def weighted(hit, values):
    bigs, smalls = [], []
    for value in values:
        big = value.astype(jnp.bfloat16).astype(f32)
        for r in range(value.shape[0]):
            for rows, source in ((bigs, big), (smalls, value - big)):
                row = jnp.broadcast_to(source[r : r + 1, :], (16, NZ)).astype(jnp.bfloat16)
                rows.append(jnp.concatenate([row] * 4, axis=0))
    return jnp.concatenate(
        [hit * jnp.concatenate(bigs, axis=1), hit * jnp.concatenate(smalls, axis=1)], axis=0
    )


def table_sum(left, right):
    return lax.dot_general(left, right, (((1,), (1,)), ((), ())), preferred_element_type=f32)


def gradient_plane(x, adj_pad, fluid_pad, grad, dgrad_in, out):
    q0, _, q2 = moments(propagate_back(adj_pad, fluid_pad, x))
    dgrad = gradient_back(q0, q2, [grad[d, x] for d in range(3)])
    for d in range(3):
        out(d, x, dgrad[d] + dgrad_in[d, x])


def plane_adjoint(pad, x):
    return gradient_adjoint(lambda d, a, b: pad[d, x + 1 + a, pl.ds(LOW + b, NY), :])


GROUP = 4


def own_group(start, dgrad_pad, wall, hits, rights):
    values = [plane_adjoint(dgrad_pad, start + k + 1) * wall[start + k] for k in range(GROUP)]
    nodes = pl.ds(pl.multiple_of(start * NY * NZ, NY * NZ), GROUP * NY * NZ)
    return table_sum(weighted(hits[:, nodes], values), rights[:, nodes])


def first_inner_kernel(
    adj, fluid_pad, grad, dgrad_in, y_low, y_high, wall, hits, rights,
    dgrad_out, acc_out,
    adj_pad, dgrad_pad,
):
    fill_pops(adj_pad, adj, range(NX), y_low, y_high)
    dgrad_pad[...] = jnp.zeros_like(dgrad_pad)

    def out(d, x, value):
        dgrad_out[d, x] = value
        dgrad_pad[d, x + 2, pl.ds(LOW, NY), :] = value

    def plane(x, carry):
        gradient_plane(x, adj_pad, fluid_pad, grad, dgrad_in, out)
        return carry

    lax.fori_loop(1, NX - 1, plane, 0)
    acc_out[...] = jnp.zeros_like(acc_out)

    def group(g, carry):
        acc_out[...] += own_group(2 + g * GROUP, dgrad_pad, wall, hits, rights)
        return carry

    lax.fori_loop(0, (NX - 4) // GROUP, group, 0)


def first_outer_kernel(
    adj, fluid_pad, grad, dgrad_in, y_low, y_high, x_low, x_high, e_low, e_high, dgrad_inner, acc_in,
    wall, hits, rights, wall_face, wall_side, halo_hits, halo_rights,
    total_out,
    adj_pad, dgrad_pad, rows,
):
    fill_pops(adj_pad, adj, (0, 1, NX - 2, NX - 1), y_low, y_high)
    fill_pops_outer(adj_pad, x_low, x_high, e_low, e_high)
    for d in range(3):
        for x in (0, 1, 2, 3, NX, NX + 1, NX + 2, NX + 3):
            dgrad_pad[d, x] = jnp.zeros((ROWS, NZ), f32)

    def out(d, x, value):
        dgrad_pad[d, x + 2, pl.ds(LOW, NY), :] = value

    for x in (0, NX - 1):
        gradient_plane(x, adj_pad, fluid_pad, grad, dgrad_in, out)
    for x in inner:
        for d in range(3):
            out(d, x, dgrad_inner[d, x])
    values = [plane_adjoint(dgrad_pad, x + 1) * wall[x] for x in (0, 1, NX - 2, NX - 1)]
    total = acc_in[...]
    for k, start in enumerate((0, NX - 2)):
        nodes = pl.ds(start * NY * NZ, 2 * NY * NZ)
        total = total + table_sum(weighted(hits[:, nodes], values[2 * k : 2 * k + 2]), rights[:, nodes])
    values = [plane_adjoint(dgrad_pad, x) * wall_face[k] for k, x in enumerate((0, WX - 1))]
    flat = dgrad_pad.reshape(3 * (WX + 2) * ROWS, NZ)
    for side, (row, sign) in enumerate(((LOW, 1.0), (LOW + NY - 1, -1.0))):
        for d in range(3):
            rows[d] = flat[pl.ds(d * (WX + 2) * ROWS + row, WX + 2, stride=ROWS), :]
        values.append(side_adjoint(rows, sign) * wall_side[side])
    total = total + table_sum(weighted(halo_hits[...], values), halo_rights[...])
    both = total[:64] + total[64:]
    total_out[...] = jnp.concatenate([both[:32], both[32:]], axis=1)


def first_adjoint_kernel(
    pops, phase, adj, fluid_pad, y_low, y_high, x_low, x_high, e_low, e_high, adj_out, adj_pad
):
    fill_pops(adj_pad, adj, range(NX), y_low, y_high)
    fill_pops_outer(adj_pad, x_low, x_high, e_low, e_high)

    def plane(x, carry):
        step_plane(x, adj_pad, fluid_pad, pops, phase, adj_out, None)
        return carry

    lax.fori_loop(0, NX, plane, 0)


def ring(axis, value, step):
    count = lax.axis_size(axis)
    return lax.ppermute(value, axis, [(i, (i + step) % count) for i in range(count)])


def group_sum(value, axis, stride, size):
    count = lax.axis_size(axis)
    got = []
    for s in range(1, size):
        pairs = []
        for i in range(count):
            digit = (i // stride) % size
            pairs.append((i, i + ((digit + s) % size - digit) * stride))
        got.append(lax.ppermute(value, axis, pairs))
    for part in got:
        value = value + part
    return value


def shards(
    pops_first,
    pops_second,
    phase_first,
    phase_second,
    adjoint_last,
    wettability,
    fluid,
    wall,
    patch,
):
    table = wettability.reshape(32, NZ)
    fields = (phase_first, phase_second, fluid, wall, patch)
    x_up, x_down, y_up, y_down = pack(adjoint_last, fields)
    x_high, x_low = ring("pipe", x_up, -1), ring("pipe", x_down, 1)
    y_high, y_low = ring("cross", y_up, -1), ring("cross", y_down, 1)
    phi, hits, rights = own_terms(table, *fields)
    e_up, e_down = pack_edges(x_low, x_high, FIELDS, phi)
    e_high, e_low = ring("cross", e_up, -1), ring("cross", e_down, 1)
    given = (pops_second, phase_second, adjoint_last, fluid, y_low, y_high)
    adjoint, mom = whole_call(
        second_inner_kernel, "second_inner", [block, seven], given, pad_scratch()
    )
    outer = (x_low, x_high, e_low, e_high)
    face, side = ((5, NY, NZ), f32), ((5 * NX, NZ), f32)
    adjoint, mom, x_up, x_down, y_up, y_down = whole_call(
        second_outer_kernel,
        "second_outer",
        [block, seven, face, face, side, side],
        given + outer + (adjoint, mom),
        pad_scratch(),
        {10: 0, 11: 1},
    )
    x_high2, x_low2 = ring("pipe", x_up, -1), ring("pipe", x_down, 1)
    y_high2, y_low2 = ring("cross", y_up, -1), ring("cross", y_down, 1)
    dgrad, grad, fluid_pad, wall_own, wall_face, wall_side, halo_hits, halo_rights = middle(
        phi, table, fluid, wall, mom, y_low, y_high, *outer
    )
    e_up, e_down = pack_edges(x_low2, x_high2, 0, wall_side)
    e_high2, e_low2 = ring("cross", e_up, -1), ring("cross", e_down, 1)
    given = (adjoint, fluid_pad, grad, dgrad, y_low2, y_high2)
    nodes = (wall_own, hits, rights)
    adj_scratch = pad_scratch()[:1]
    dgrad_scratch = adj_scratch + [pltpu.VMEM((3, WX + 2, ROWS, NZ), f32)]
    dgrad_inner, acc = whole_call(
        first_inner_kernel, "first_inner", [vector, ((128, 64), f32)], given + nodes, dgrad_scratch
    )
    outer = (x_low2, x_high2, e_low2, e_high2)
    (total,) = whole_call(
        first_outer_kernel,
        "first_outer",
        [((32, NZ), f32)],
        given + outer + (dgrad_inner, acc) + nodes + (wall_face, wall_side, halo_hits, halo_rights),
        dgrad_scratch + [pltpu.VMEM((3, WX + 2, NZ), f32)],
    )
    (adjoint,) = whole_call(
        first_adjoint_kernel,
        "first_adjoint",
        [block],
        (pops_first, phase_first, adjoint, fluid_pad, y_low2, y_high2, *outer),
        adj_scratch,
    )
    total = group_sum(total, "pipe", 1, 2)
    total = group_sum(total, "pipe", 2, 4)
    total = group_sum(total, "cross", 1, 4)
    total = group_sum(total, "cross", 4, 4)
    return adjoint, total.reshape(wettability.shape)


def solution(mesh):
    return jax.shard_map(
        shards,
        mesh=mesh,
        in_specs=(
            P(None, "pipe", "cross", None),
            P(None, "pipe", "cross", None),
            P("pipe", "cross", None),
            P("pipe", "cross", None),
            P(None, "pipe", "cross", None),
            P(),
            P("pipe", "cross", None),
            P("pipe", "cross", None),
            P("pipe", "cross", None),
        ),
        out_specs=(P(None, "pipe", "cross", None), P()),
        check_vma=False,
    )
```

```python
import functools

import jax
import jax.numpy as jnp
from jax import lax
from jax.experimental import pallas as pl
from jax.experimental.pallas import tpu as pltpu
from jax.sharding import PartitionSpec as P

lattice_vel = (
    (0, 0, 0),
    (1, 0, 0),
    (-1, 0, 0),
    (0, 1, 0),
    (0, -1, 0),
    (0, 0, 1),
    (0, 0, -1),
    (1, 1, 0),
    (-1, -1, 0),
    (1, -1, 0),
    (-1, 1, 0),
    (1, 0, 1),
    (-1, 0, -1),
    (1, 0, -1),
    (-1, 0, 1),
    (0, 1, 1),
    (0, -1, -1),
    (0, 1, -1),
    (0, -1, 1),
)
opposite = (0, 2, 1, 4, 3, 6, 5, 8, 7, 10, 9, 12, 11, 14, 13, 16, 15, 18, 17)
relax_heavy = 1.0
relax_light = 0.7

x_plus = (1, 7, 9, 11, 13)
x_minus = (2, 8, 10, 12, 14)
y_plus = (3, 7, 10, 15, 17)
y_minus = (4, 8, 9, 16, 18)

NX = 16
NY = 8
NZ = 128
WX = NX + 2
LOW = 8
ROWS = 24
FIELDS = 5
f32 = jnp.float32


def tile(ref, lead, x, move):
    index = lead + (x + 1 + move[0], pl.ds(LOW + move[1], NY), slice(None))
    value = ref[index]
    if move[2]:
        value = pltpu.roll(value, (-move[2]) % NZ, 1)
    return value


def look_up(table, index):
    high = lax.shift_right_logical(index, 7)
    low = index & 127
    result = jnp.zeros(index.shape, f32)
    for r in range(32):
        row = jnp.broadcast_to(table[pl.ds(r, 1), :], index.shape)
        picked = jnp.take_along_axis(row, low, axis=1, mode="promise_in_bounds")
        result = jnp.where(high == r, picked, result)
    return result


def roll_z(value, step):
    return pltpu.roll(value, (-step) % NZ, 1)


def gradient(view):
    sixth, twelfth = 1.0 / 6.0, 1.0 / 12.0
    east, west, north, south = view(1, 0), view(-1, 0), view(0, 1), view(0, -1)
    dx, dy = east - west, north - south
    xy = view(1, 1) - view(-1, -1)
    xmy = view(1, -1) - view(-1, 1)
    along = sixth * view(0, 0) + twelfth * (east + west + north + south)
    gx = sixth * dx + twelfth * (xy + xmy + roll_z(dx, 1) + roll_z(dx, -1))
    gy = sixth * dy + twelfth * (xy - xmy + roll_z(dy, 1) + roll_z(dy, -1))
    return gx, gy, roll_z(along, 1) - roll_z(along, -1)


def moments(q):
    a, b = 1.0 / 18.0, 1.0 / 36.0

    def pair(i):
        return q[i] + q[i + 1], q[i] - q[i + 1]

    (sx, dx), (sy, dy), (sz, dz) = pair(1), pair(3), pair(5)
    (s7, d7), (s9, d9), (s11, d11) = pair(7), pair(9), pair(11)
    (s13, d13), (s15, d15), (s17, d17) = pair(13), pair(15), pair(17)
    xy, xz, yz = s7 + s9, s11 + s13, s15 + s17
    m0 = (1.0 / 3.0) * q[0] + a * (sx + sy + sz) + b * (xy + xz + yz)
    mx = a * dx + b * (d7 + d9 + d11 + d13)
    my = a * dy + b * (d7 - d9 + d15 + d17)
    mz = a * dz + b * (d11 - d13 + d15 - d17)
    mxx = a * sx + b * (xy + xz)
    myy = a * sy + b * (xy + yz)
    mzz = a * sz + b * (xz + yz)
    return m0, (mx, my, mz), (mxx, myy, mzz, b * (s7 - s9), b * (s11 - s13), b * (s15 - s17))


def velocity(f):
    density = f[0]
    for i in range(1, 19):
        density = density + f[i]
    d = {i: f[i] - f[i + 1] for i in range(1, 19, 2)}
    inv = 1.0 / density
    ux = (d[1] + d[7] + d[9] + d[11] + d[13]) * inv
    uy = (d[3] + d[7] - d[9] + d[15] + d[17]) * inv
    uz = (d[5] + d[11] - d[13] + d[15] - d[17]) * inv
    return ux, uy, uz


def apply_second(second, v):
    mxx, myy, mzz, mxy, mxz, myz = second
    x, y, z = v
    return (
        mxx * x + mxy * y + mxz * z,
        mxy * x + myy * y + myz * z,
        mxz * x + myz * y + mzz * z,
    )


def dot3(a, b):
    return a[0] * b[0] + a[1] * b[1] + a[2] * b[2]


def collide_back(post, q, u, phase, store):
    q0, q1, q2 = q
    omega = 1.0 / (relax_heavy * (1.0 + phase) * 0.5 + relax_light * (1.0 - phase) * 0.5)
    q2u = apply_second(q2, u)
    along = q0 - 4.5 * dot3(u, q2u) + 1.5 * dot3(u, u) * q0
    base = omega * along
    bx, by, bz = [omega * (3.0 * q1[d] + 9.0 * q2u[d] - 3.0 * u[d] * q0) for d in range(3)]
    keep = 1.0 - omega
    store(0, keep * post[0] + base)
    slopes = (bx, by, bz, bx + by, bx - by, bx + bz, bx - bz, by + bz, by - bz)
    for k, slope in enumerate(slopes):
        i = 1 + 2 * k
        store(i, keep * post[i] + (base + slope))
        store(i + 1, keep * post[i + 1] + (base - slope))


def gradient_back(q0, q2, n):
    nsq = dot3(n, n)
    root = 1.0 / jnp.sqrt(1.0 + nsq)
    q2n = apply_second(q2, n)
    energy = dot3(n, q2n) - (1.0 / 3.0) * nsq * q0
    third = (4.0 / 3.0) * q0
    tail = 2.0 * energy * root * root * root
    return [root * (4.0 * q2n[d] - third * n[d]) - tail * n[d] for d in range(3)]


def gradient_adjoint(view):
    sixth, twelfth = 1.0 / 6.0, 1.0 / 12.0
    xe, xw, yn, ys = view(0, 1, 0), view(0, -1, 0), view(1, 0, 1), view(1, 0, -1)
    zc = sixth * view(2, 0, 0)
    around = view(2, 1, 0) + view(2, -1, 0) + view(2, 0, 1) + view(2, 0, -1)
    across = xe - xw + yn - ys
    flat = sixth * across + twelfth * (
        view(0, 1, 1) + view(1, 1, 1) - view(0, -1, -1) - view(1, -1, -1)
        + view(0, 1, -1) - view(1, 1, -1) - view(0, -1, 1) + view(1, -1, 1)
    )
    ahead = zc + twelfth * (across + around)
    behind = twelfth * (across - around) - zc
    return -(flat + roll_z(ahead, 1) + roll_z(behind, -1))


def side_adjoint(rows, sign):
    sixth, twelfth = 1.0 / 6.0, 1.0 / 12.0
    gx, gy, gz = [lambda move, d=d: rows[d, pl.ds(1 + move, WX), :] for d in range(3)]
    flat = sixth * sign * gy(0) + twelfth * (sign * (gy(1) + gy(-1)) + gx(1) - gx(-1))
    return -(flat + twelfth * (roll_z(sign * gy(0) + gz(0), 1) + roll_z(sign * gy(0) - gz(0), -1)))


def whole_call(kernel, name, out_shape, args, scratch=(), aliases=None, in_hbm=False, specs=None):
    options = {}
    if in_hbm:
        options["in_specs"] = [pl.BlockSpec(memory_space=pl.ANY)] * len(args)
    else:
        if specs:
            options["in_specs"] = specs
        options["compiler_params"] = pltpu.CompilerParams(vmem_limit_bytes=24 * 1024 * 1024)
    return pl.pallas_call(
        kernel,
        out_shape=[
            pltpu.VMEM(shape, kind) if in_hbm else jax.ShapeDtypeStruct(shape, kind) for shape, kind in out_shape
        ],
        scratch_shapes=scratch,
        input_output_aliases=aliases or {},
        name=name,
        **options,
    )(*args)


class Pick:
    def __init__(self, first, a, b):
        self.first, self.a, self.b = first, a, b

    def __getitem__(self, index):
        return jnp.where(self.first, self.a[index], self.b[index])


def is_odd(axis):
    return lax.axis_index(axis) % 2 == 1


def sides(axis, a, b):
    odd = is_odd(axis)
    return Pick(odd, a, b), Pick(odd, b, a)


def put(odd, outs, index, up, down):
    outs[0][index] = jnp.where(odd, up, down)
    outs[1][index] = jnp.where(odd, down, up)


def put_rows(odd, outs, slot, flat, up, down):
    rows = [flat[pl.ds(start, NX, stride=NY), :].astype(f32) for start in (up, down)]
    put(odd, outs, (pl.ds(slot * NX, NX), slice(None)), *rows)


def put_pops(adj, x_outs, y_outs):
    odd_x, odd_y = is_odd("pipe"), is_odd("cross")
    flat = adj.reshape(19 * NX * NY, NZ)
    for k in range(5):
        put(odd_x, x_outs, k, adj[x_plus[k], 0], adj[x_minus[k], NX - 1])
        put_rows(odd_y, y_outs, k, flat, y_plus[k] * NX * NY, y_minus[k] * NX * NY + NY - 1)


def fetch(pairs, sem):
    copies = [pltpu.make_async_copy(a, b, sem.at[k]) for k, (a, b) in enumerate(pairs)]
    for copy in copies:
        copy.start()
    return copies


def pack_kernel(adj_hbm, *refs):
    hbm, (xa, xb, ya, yb), (adj, *fields) = refs[:FIELDS], refs[FIELDS : FIELDS + 4], refs[FIELDS + 4 : -1]
    for copy in fetch([(adj_hbm, adj), *zip(hbm, fields)], refs[-1]):
        copy.wait()
    put_pops(adj, (xa, xb), (ya, yb))
    odd_x, odd_y = is_odd("pipe"), is_odd("cross")
    for k in range(FIELDS):
        put(odd_x, (xa, xb), 5 + k, fields[k][0].astype(f32), fields[k][NX - 1].astype(f32))
        put_rows(odd_y, (ya, yb), 5 + k, fields[k].reshape(NX * NY, NZ), 0, NY - 1)


def pack(adjoint, fields):
    face, side = ((5 + FIELDS + 2, NY, NZ), f32), (((5 + FIELDS) * NX, NZ), f32)
    scratch = [pltpu.VMEM((19, NX, NY, NZ), f32)]
    scratch += [pltpu.VMEM((NX, NY, NZ), field.dtype) for field in fields]
    scratch.append(pltpu.SemaphoreType.DMA((1 + FIELDS,)))
    return whole_call(pack_kernel, "pack", [face, face, side, side], (adjoint, *fields), scratch, in_hbm=True)


edge_plus = (7, 9)
edge_minus = (10, 8)


def pack_edges_kernel(count, xa, xb, ya, yb, _, xa_out, xb_out):
    planes = 5 + count
    for k in range(planes):
        xa_out[k] = xa[k]
        xb_out[k] = xb[k]
    low, high = sides("cross", ya, yb)
    odd = is_odd("pipe")
    for e, (rows, pops) in enumerate(((high, y_plus), (low, y_minus))):
        xa_out[planes + e] = jnp.zeros((NY, NZ), f32)
        xb_out[planes + e] = jnp.zeros((NY, NZ), f32)
        starts = [(pops.index(edge_plus[e]), pops.index(edge_minus[e]))] + [(5 + k, 5 + k) for k in range(count)]
        for r, (up, down) in enumerate(starts):
            up_row = rows[pl.ds(up * NX, 1), :]
            down_row = rows[pl.ds(down * NX + NX - 1, 1), :]
            put(odd, (xa_out, xb_out), (planes + e, pl.ds(r, 1), slice(None)), up_row, down_row)


def pack_edges(x_pair, y_halo, count, after):
    out = ((5 + count + 2, NY, NZ), f32)
    kernel = functools.partial(pack_edges_kernel, count)
    return whole_call(kernel, "pack_edges", [out, out], (*x_pair, *y_halo, after))


def fill_sides(pad, lead, y_low, low_slot, y_high, high_slot):
    for x in range(NX):
        pad[lead + (x + 1, pl.ds(LOW - 1, 1), slice(None))] = y_low[pl.ds(low_slot * NX + x, 1), :]
        pad[lead + (x + 1, pl.ds(LOW + NY, 1), slice(None))] = y_high[pl.ds(high_slot * NX + x, 1), :]


def fill_pops(pad, adj, planes, y_low, y_high):
    for p in range(19):
        for x in planes:
            pad[p, x + 1, pl.ds(LOW, NY), :] = adj[p, x]
    for k in range(5):
        for x in planes:
            pad[y_minus[k], x + 1, pl.ds(LOW - 1, 1), :] = y_low[pl.ds(k * NX + x, 1), :]
            pad[y_plus[k], x + 1, pl.ds(LOW + NY, 1), :] = y_high[pl.ds(k * NX + x, 1), :]


def fill_pops_outer(pad, x_low, x_high, planes):
    for k in range(5):
        pad[x_minus[k], 0, pl.ds(LOW, NY), :] = x_low[k]
        pad[x_plus[k], WX - 1, pl.ds(LOW, NY), :] = x_high[k]
    for e, row in enumerate((LOW + NY, LOW - 1)):
        pad[edge_minus[e], 0, pl.ds(row, 1), :] = x_low[planes + e, pl.ds(0, 1), :]
        pad[edge_plus[e], WX - 1, pl.ds(row, 1), :] = x_high[planes + e, pl.ds(0, 1), :]


def fill_field(pad, lead, own, slot, y_low, y_high):
    for x in range(NX):
        pad[lead + (x + 1, pl.ds(LOW, NY), slice(None))] = own[x].astype(f32)
    fill_sides(pad, lead, y_low, 5 + slot, y_high, 5 + slot)


def fill_field_outer(pad, lead, slot, x_low, x_high):
    for x, face in ((0, x_low), (WX - 1, x_high)):
        pad[lead + (x, pl.ds(LOW, NY), slice(None))] = face[5 + slot]
        for e, row in enumerate((LOW + NY, LOW - 1)):
            pad[lead + (x, pl.ds(row, 1), slice(None))] = face[5 + FIELDS + e, pl.ds(1 + slot, 1), :]


def propagate_back(adj_pad, fluid_pad, x):
    here = tile(fluid_pad, (), x, (0, 0, 0))
    post = [here * adj_pad[0, x + 1, pl.ds(LOW, NY), :]]
    for i in range(1, 19):
        ahead = tile(fluid_pad, (), x, lattice_vel[i])
        moved = tile(adj_pad, (i,), x, lattice_vel[i])
        back = adj_pad[opposite[i], x + 1, pl.ds(LOW, NY), :]
        post.append(here * jnp.where(ahead != 0.0, moved, back))
    return post


def step_plane(x, adj_pad, fluid_pad, speed, phase, adj_out, mom_out, at=0):
    post = propagate_back(adj_pad, fluid_pad, x)
    q = moments(post)

    def store(i, value):
        adj_out[i, x - at] = value

    collide_back(post, q, [speed[d, x] for d in range(3)], phase[x], store)
    if mom_out is not None:
        mom_out[0, x] = q[0]
        for k in range(6):
            mom_out[1 + k, x] = q[2][k]


inner = range(1, NX - 1)


def second_inner_kernel(speed, phase, adj, fluid, ya, yb, adj_out, mom_out, adj_pad, fluid_pad):
    y_low, y_high = sides("cross", ya, yb)
    fill_field(fluid_pad, (), fluid, 2, y_low, y_high)
    fill_pops(adj_pad, adj, range(NX), y_low, y_high)

    def plane(x, carry):
        step_plane(x, adj_pad, fluid_pad, speed, phase, adj_out, mom_out)
        return carry

    lax.fori_loop(1, NX - 1, plane, 0)


block = ((19, NX, NY, NZ), f32)
seven = ((7, NX, NY, NZ), f32)
vector = ((3, NX, NY, NZ), f32)


def pad_scratch():
    return [pltpu.VMEM((19, WX, ROWS, NZ), f32), pltpu.VMEM((WX, ROWS, NZ), f32)]


def second_outer_kernel(
    speed, phase, adj, fluid, ya, yb, xa, xb, adj_in, mom_in,
    adj_out, mom_out, xa_out, xb_out, ya_out, yb_out, adj_pad, fluid_pad,
):
    (x_low, x_high), (y_low, y_high) = sides("pipe", xa, xb), sides("cross", ya, yb)
    fill_field(fluid_pad, (), fluid, 2, y_low, y_high)
    fill_field_outer(fluid_pad, (), 2, x_low, x_high)
    fill_pops(adj_pad, adj, (0, 1, NX - 2, NX - 1), y_low, y_high)
    fill_pops_outer(adj_pad, x_low, x_high, 5 + FIELDS)
    for x in (0, NX - 1):
        step_plane(x, adj_pad, fluid_pad, speed, phase, adj_out, mom_out)
    put_pops(adj_out, (xa_out, xb_out), (ya_out, yb_out))


def one_hots(index, row, hit_out, right_out, at):
    row_iota = lax.broadcasted_iota(jnp.int32, (64, NZ), 0)
    key = (lax.shift_right_logical(index, 6) & 1) * 32 + lax.shift_right_logical(index, 7)
    low = index & 63
    hit = jnp.where(row_iota == key[row : row + 1, :], 1.0, 0.0)
    hit_out[:, pl.ds(at, NZ)] = hit.astype(jnp.bfloat16)
    right = jnp.where(row_iota == low[row : row + 1, :], 1.0, 0.0)
    right_out[:, pl.ds(at, NZ)] = right.astype(jnp.bfloat16)


OWN = NX * NY * NZ
SIDE = WX * NZ
HALO = 2 * NY * NZ + 2 * SIDE


def store_velocity(pops, out):
    def plane(x, carry):
        u = velocity([pops[i, x] for i in range(19)])
        for d in range(3):
            out[d, x] = u[d]
        return carry

    lax.fori_loop(0, NX, plane, 0)


def own_kernel(
    table_hbm, phase_a_hbm, phase_b_hbm, fluid_hbm, wall_hbm, patch_hbm, pops_hbm,
    phi_out, hit_out, right_out, wall_out, speed_out,
    table, phase_a, phase_b, fluid, wall, patch, pops, sem,
):
    hbm = (table_hbm, phase_a_hbm, phase_b_hbm, fluid_hbm, wall_hbm, patch_hbm, pops_hbm)
    copies = fetch(zip(hbm, (table, phase_a, phase_b, fluid, wall, patch, pops)), sem)
    for copy in copies[:-1]:
        copy.wait()

    def plane(x, carry):
        index = patch[x] & 4095
        wall_out[x] = wall[x].astype(f32)
        contact = wall[x].astype(f32) * look_up(table, index)
        wet = fluid[x].astype(f32)
        phi_out[0, x] = wet * phase_a[x] + contact
        phi_out[1, x] = wet * phase_b[x] + contact
        for r in range(NY):
            one_hots(index, r, hit_out, right_out, pl.multiple_of((x * NY + r) * NZ, NZ))
        return carry

    lax.fori_loop(0, NX, plane, 0)
    copies[-1].wait()
    store_velocity(pops, speed_out)


def middle_kernel(
    phi, table, fluid, mom, ya, yb, xa, xb, pops_hbm,
    dgrad_out, grad_out, fluid_out, wall_face, wall_side, hit_out, right_out, speed_out,
    phi_pad, pops, sem,
):
    (copy_pops,) = fetch([(pops_hbm, pops)], sem)
    (x_low, x_high), (y_low, y_high) = sides("pipe", xa, xb), sides("cross", ya, yb)
    fill_field(fluid_out, (), fluid, 2, y_low, y_high)
    fill_field_outer(fluid_out, (), 2, x_low, x_high)

    def copy(x, carry):
        for t in range(2):
            phi_pad[t, x + 1, pl.ds(LOW, NY), :] = phi[t, x]
        return carry

    lax.fori_loop(0, NX, copy, 0)

    def imposed(slot):
        index = slot(4).astype(jnp.int32) & 4095
        contact = slot(3) * look_up(table, index)
        return index, [slot(2) * slot(t) + contact for t in range(2)]

    for side, (face, x) in enumerate(((x_low, 0), (x_high, WX - 1))):
        index, values = imposed(lambda k: face[5 + k])
        wall_face[side] = face[8]
        for t in range(2):
            phi_pad[t, x, pl.ds(LOW, NY), :] = values[t]
        for r in range(NY):
            one_hots(index, r, hit_out, right_out, (side * NY + r) * NZ)
    base = 2 * NY * NZ
    for side, (rows, y) in enumerate(((y_low, LOW - 1), (y_high, LOW + NY))):
        index, values = imposed(lambda k: rows[pl.ds((5 + k) * NX, NX), :])
        wall_side[side, pl.ds(1, NX), :] = rows[pl.ds(8 * NX, NX), :]
        for x in range(NX):
            for t in range(2):
                phi_pad[t, x + 1, pl.ds(y, 1), :] = values[t][x : x + 1, :]
            one_hots(index, x, hit_out, right_out, base + side * SIDE + (x + 1) * NZ)
    def corner_rows(k):
        rows = [face[5 + FIELDS + 1 - e, pl.ds(1 + k, 1), :] for e in range(2) for face in (x_low, x_high)]
        return jnp.concatenate(rows + rows, axis=0)

    index, values = imposed(corner_rows)
    on_wall = corner_rows(3)
    for r in range(4):
        side, x, y = r // 2, (WX - 1) * (r % 2), (LOW - 1, LOW + NY)[r // 2]
        wall_side[side, pl.ds(x, 1), :] = on_wall[r : r + 1, :]
        for t in range(2):
            phi_pad[t, x, pl.ds(y, 1), :] = values[t][r : r + 1, :]
        one_hots(index, r, hit_out, right_out, base + side * SIDE + x * NZ)

    def plane(x, carry):
        def view(t):
            return lambda a, b: tile(phi_pad, (t,), x, (a, b, 0))

        first, n = gradient(view(0)), gradient(view(1))
        for d in range(3):
            grad_out[d, x] = first[d]
        dgrad = gradient_back(mom[0, x], [mom[1 + k, x] for k in range(6)], n)
        for d in range(3):
            dgrad_out[d, x] = dgrad[d]
        return carry

    lax.fori_loop(0, NX, plane, 0)
    copy_pops.wait()
    store_velocity(pops, speed_out)


def own_terms(*args):
    hots = ((64, OWN), jnp.bfloat16)
    scratch = [pltpu.VMEM(arg.shape, arg.dtype) for arg in args] + [pltpu.SemaphoreType.DMA((len(args),))]
    shapes = [((2, NX, NY, NZ), f32), hots, hots, ((NX, NY, NZ), f32), vector]
    return whole_call(own_kernel, "own_terms", shapes, args, scratch, specs=[pl.BlockSpec(memory_space=pl.ANY)] * len(args))


def middle(*args):
    shapes = [vector, vector, ((WX, ROWS, NZ), f32), ((2, NY, NZ), f32), ((2, WX, NZ), f32)]
    shapes += [((64, HALO), jnp.bfloat16)] * 2 + [vector]
    scratch = [pltpu.VMEM((2, WX, ROWS, NZ), f32), pltpu.VMEM((19, NX, NY, NZ), f32), pltpu.SemaphoreType.DMA((1,))]
    specs = [pl.BlockSpec(memory_space=pltpu.VMEM)] * (len(args) - 1) + [pl.BlockSpec(memory_space=pl.ANY)]
    return whole_call(middle_kernel, "middle", shapes, args, scratch, specs=specs)


def weighted(hit, values):
    bigs, smalls = [], []
    for value in values:
        big = value.astype(jnp.bfloat16).astype(f32)
        for r in range(value.shape[0]):
            for rows, source in ((bigs, big), (smalls, value - big)):
                row = jnp.broadcast_to(source[r : r + 1, :], (16, NZ)).astype(jnp.bfloat16)
                rows.append(jnp.concatenate([row] * 4, axis=0))
    return jnp.concatenate(
        [hit * jnp.concatenate(bigs, axis=1), hit * jnp.concatenate(smalls, axis=1)], axis=0
    )


def table_sum(left, right):
    return lax.dot_general(left, right, (((1,), (1,)), ((), ())), preferred_element_type=f32)


def gradient_plane(x, adj_pad, fluid_pad, grad, dgrad_in, out):
    q0, _, q2 = moments(propagate_back(adj_pad, fluid_pad, x))
    dgrad = gradient_back(q0, q2, [grad[d, x] for d in range(3)])
    for d in range(3):
        out(d, x, dgrad[d] + dgrad_in[d, x])


def plane_adjoint(pad, x):
    return gradient_adjoint(lambda d, a, b: pad[d, x + 1 + a, pl.ds(LOW + b, NY), :])


GROUP = 4


def own_group(start, dgrad_pad, wall, hits, rights):
    values = [plane_adjoint(dgrad_pad, start + k + 1) * wall[start + k] for k in range(GROUP)]
    nodes = pl.ds(pl.multiple_of(start * NY * NZ, NY * NZ), GROUP * NY * NZ)
    return table_sum(weighted(hits[:, nodes], values), rights[:, nodes])


def first_inner_kernel(
    adj, fluid_pad, grad, dgrad_in, ya, yb, wall, hits, rights,
    dgrad_out, acc_out,
    adj_pad, dgrad_pad,
):
    y_low, y_high = sides("cross", ya, yb)
    fill_pops(adj_pad, adj, range(NX), y_low, y_high)
    dgrad_pad[...] = jnp.zeros_like(dgrad_pad)

    def out(d, x, value):
        dgrad_out[d, x] = value
        dgrad_pad[d, x + 2, pl.ds(LOW, NY), :] = value

    def plane(x, carry):
        gradient_plane(x, adj_pad, fluid_pad, grad, dgrad_in, out)
        return carry

    lax.fori_loop(1, NX - 1, plane, 0)
    acc_out[...] = jnp.zeros_like(acc_out)

    def group(g, carry):
        acc_out[...] += own_group(2 + g * GROUP, dgrad_pad, wall, hits, rights)
        return carry

    lax.fori_loop(0, (NX - 4) // GROUP, group, 0)


def first_outer_kernel(
    adj, fluid_pad, grad, dgrad_in, ya, yb, xa, xb, dgrad_inner, acc_in,
    wall, hits, rights, wall_face, wall_side, halo_hits, halo_rights,
    total_out,
    adj_pad, dgrad_pad, rows,
):
    (x_low, x_high), (y_low, y_high) = sides("pipe", xa, xb), sides("cross", ya, yb)
    fill_pops(adj_pad, adj, (0, 1, NX - 2, NX - 1), y_low, y_high)
    fill_pops_outer(adj_pad, x_low, x_high, 5)
    for d in range(3):
        for x in (0, 1, 2, 3, NX, NX + 1, NX + 2, NX + 3):
            dgrad_pad[d, x] = jnp.zeros((ROWS, NZ), f32)

    def out(d, x, value):
        dgrad_pad[d, x + 2, pl.ds(LOW, NY), :] = value

    for x in (0, NX - 1):
        gradient_plane(x, adj_pad, fluid_pad, grad, dgrad_in, out)
    for x in inner:
        for d in range(3):
            out(d, x, dgrad_inner[d, x])
    values = [plane_adjoint(dgrad_pad, x + 1) * wall[x] for x in (0, 1, NX - 2, NX - 1)]
    total = acc_in[...]
    for k, start in enumerate((0, NX - 2)):
        nodes = pl.ds(start * NY * NZ, 2 * NY * NZ)
        total = total + table_sum(weighted(hits[:, nodes], values[2 * k : 2 * k + 2]), rights[:, nodes])
    values = [plane_adjoint(dgrad_pad, x) * wall_face[k] for k, x in enumerate((0, WX - 1))]
    flat = dgrad_pad.reshape(3 * (WX + 2) * ROWS, NZ)
    for side, (row, sign) in enumerate(((LOW, 1.0), (LOW + NY - 1, -1.0))):
        for d in range(3):
            rows[d] = flat[pl.ds(d * (WX + 2) * ROWS + row, WX + 2, stride=ROWS), :]
        values.append(side_adjoint(rows, sign) * wall_side[side])
    total = total + table_sum(weighted(halo_hits[...], values), halo_rights[...])
    both = total[:64] + total[64:]
    total_out[...] = jnp.concatenate([both[:32], both[32:]], axis=1)


SHARE = 4


def first_adjoint_kernel(
    start, speed, phase, adj, fluid_pad, ya, yb, xa, xb, *refs
):
    out, adj_pad, part, sem = refs[-4:]
    (x_low, x_high), (y_low, y_high) = sides("pipe", xa, xb), sides("cross", ya, yb)
    planes = range(max(start - 1, 0), min(start + SHARE + 1, NX))
    fill_pops(adj_pad, adj, planes, y_low, y_high)
    if start == 0 or start + SHARE == NX:
        fill_pops_outer(adj_pad, x_low, x_high, 5)

    def plane(k, carry):
        step_plane(start + k, adj_pad, fluid_pad, speed, phase, part, None, start)
        return carry

    lax.fori_loop(0, SHARE, plane, 0)
    (copy,) = fetch([(part, out.at[:, pl.ds(start, SHARE)])], sem)
    copy.wait()


def first_adjoint(start, args, after, before):
    args = (*args, after) if before is None else (*args, after, before)
    specs = [pl.BlockSpec(memory_space=pltpu.VMEM)] * 8 + [pl.BlockSpec(memory_space=pl.ANY)] * (len(args) - 8)
    return pl.pallas_call(
        functools.partial(first_adjoint_kernel, start),
        out_shape=jax.ShapeDtypeStruct(*block),
        in_specs=specs,
        out_specs=pl.BlockSpec(memory_space=pl.ANY),
        scratch_shapes=[
            pltpu.VMEM((19, WX, ROWS, NZ), f32),
            pltpu.VMEM((19, SHARE, NY, NZ), f32),
            pltpu.SemaphoreType.DMA((1,)),
        ],
        input_output_aliases={} if before is None else {9: 0},
        compiler_params=pltpu.CompilerParams(vmem_limit_bytes=24 * 1024 * 1024),
        name="first_adjoint",
    )(*args)


def swap(axis, a, b):
    count = lax.axis_size(axis)
    near = lax.ppermute(a, axis, [(i, i ^ 1) for i in range(count)])
    far = lax.ppermute(b, axis, [(i, (i + 2 * (i % 2) - 1) % count) for i in range(count)])
    return near, far


def mirror(index, low, size):
    digit = index // low % size
    return index + (size - 1 - 2 * digit) * low


def sum_rounds():
    return (
        lambda p, c: (p ^ 1, c),
        lambda p, c: (p ^ 3, c),
        lambda p, c: (mirror(p, 2, 4) ^ 1, c),
        lambda p, c: (p ^ 1, c ^ 1),
        lambda p, c: (p ^ 1, mirror(c, 1, 4)),
        lambda p, c: (p ^ 1, c ^ 4),
        lambda p, c: (p ^ 1, mirror(c, 4, 4)),
    )


def exchange(value, place):
    pipe, cross = lax.axis_size("pipe"), lax.axis_size("cross")
    pairs = []
    for p in range(pipe):
        for c in range(cross):
            q, d = place(p, c)
            pairs.append((p * cross + c, q * cross + d))
    return lax.ppermute(value, ("pipe", "cross"), pairs)


def pack_pairs(packed):
    return packed[:2], packed[2:]


def shards(
    pops_first,
    pops_second,
    phase_first,
    phase_second,
    adjoint_last,
    wettability,
    fluid,
    wall,
    patch,
):
    table = wettability.reshape(32, NZ)
    fields = (phase_first, phase_second, fluid, wall, patch)
    x_swap, y_swap = pack_pairs(pack(adjoint_last, fields))
    y_halo = swap("cross", *y_swap)
    phi, hits, rights, wall_own, speed = own_terms(table, *fields, pops_second)
    x_halo = swap("pipe", *pack_edges(x_swap, y_halo, FIELDS, phi))
    given = (speed, phase_second, adjoint_last, fluid, *y_halo)
    adjoint, mom = whole_call(
        second_inner_kernel, "second_inner", [block, seven], given, pad_scratch()
    )
    face, side = ((7, NY, NZ), f32), ((5 * NX, NZ), f32)
    adjoint, mom, *packed = whole_call(
        second_outer_kernel,
        "second_outer",
        [block, seven, face, face, side, side],
        given + x_halo + (adjoint, mom),
        pad_scratch(),
        {8: 0, 9: 1},
    )
    x_swap, y_swap = pack_pairs(packed)
    y_halo2 = swap("cross", *y_swap)
    dgrad, grad, fluid_pad, wall_face, wall_side, halo_hits, halo_rights, speed = middle(
        phi, table, fluid, mom, *y_halo, *x_halo, pops_first
    )
    x_halo2 = swap("pipe", *pack_edges(x_swap, y_halo2, 0, wall_side))
    given = (adjoint, fluid_pad, grad, dgrad, *y_halo2)
    nodes = (wall_own, hits, rights)
    adj_scratch = pad_scratch()[:1]
    dgrad_scratch = adj_scratch + [pltpu.VMEM((3, WX + 2, ROWS, NZ), f32)]
    dgrad_inner, acc = whole_call(
        first_inner_kernel, "first_inner", [vector, ((128, 64), f32)], given + nodes, dgrad_scratch
    )
    (total,) = whole_call(
        first_outer_kernel,
        "first_outer",
        [((32, NZ), f32)],
        given + x_halo2 + (dgrad_inner, acc) + nodes + (wall_face, wall_side, halo_hits, halo_rights),
        dgrad_scratch + [pltpu.VMEM((3, WX + 2, NZ), f32)],
    )
    args = (speed, phase_first, adjoint, fluid_pad, *y_halo2, *x_halo2)
    result = None
    for k, place in enumerate(sum_rounds()):
        got = exchange(total, place)
        share = k - 2
        if 0 <= share < NX // SHARE:
            result = first_adjoint(share * SHARE, args, total, result)
            got, result = lax.optimization_barrier((got, result))
        total = total + got
    return result, total.reshape(wettability.shape)


def solution(mesh):
    return jax.shard_map(
        shards,
        mesh=mesh,
        in_specs=(
            P(None, "pipe", "cross", None),
            P(None, "pipe", "cross", None),
            P("pipe", "cross", None),
            P("pipe", "cross", None),
            P(None, "pipe", "cross", None),
            P(),
            P("pipe", "cross", None),
            P("pipe", "cross", None),
            P("pipe", "cross", None),
        ),
        out_specs=(P(None, "pipe", "cross", None), P()),
        check_vma=False,
    )
```

```python
import functools

import jax
import jax.numpy as jnp
from jax import lax
from jax.experimental import pallas as pl
from jax.experimental.pallas import tpu as pltpu
from jax.sharding import PartitionSpec as P

lattice_vel = (
    (0, 0, 0),
    (1, 0, 0),
    (-1, 0, 0),
    (0, 1, 0),
    (0, -1, 0),
    (0, 0, 1),
    (0, 0, -1),
    (1, 1, 0),
    (-1, -1, 0),
    (1, -1, 0),
    (-1, 1, 0),
    (1, 0, 1),
    (-1, 0, -1),
    (1, 0, -1),
    (-1, 0, 1),
    (0, 1, 1),
    (0, -1, -1),
    (0, 1, -1),
    (0, -1, 1),
)
opposite = (0, 2, 1, 4, 3, 6, 5, 8, 7, 10, 9, 12, 11, 14, 13, 16, 15, 18, 17)
relax_heavy = 1.0
relax_light = 0.7

x_plus = (1, 7, 9, 11, 13)
x_minus = (2, 8, 10, 12, 14)
y_plus = (3, 7, 10, 15, 17)
y_minus = (4, 8, 9, 16, 18)

NX = 16
NY = 8
NZ = 128
WX = NX + 2
LOW = 8
ROWS = 24
EXTRA = 33
OWN_EXTRA = 5
FIELDS = 5
f32 = jnp.float32


def tile(ref, lead, x, move, low=LOW):
    index = lead + (x + 1 + move[0], pl.ds(low + move[1], NY), slice(None))
    value = ref[index]
    if move[2]:
        value = pltpu.roll(value, (-move[2]) % NZ, 1)
    return value


def look_up(table, index):
    high = lax.shift_right_logical(index, 7)
    low = index & 127
    result = jnp.zeros(index.shape, f32)
    for r in range(32):
        row = jnp.broadcast_to(table[pl.ds(r, 1), :], index.shape)
        picked = jnp.take_along_axis(row, low, axis=1, mode="promise_in_bounds")
        result = jnp.where(high == r, picked, result)
    return result


def roll_z(value, step):
    return pltpu.roll(value, (-step) % NZ, 1)


def gradient(view):
    sixth, twelfth = 1.0 / 6.0, 1.0 / 12.0
    east, west, north, south = view(1, 0), view(-1, 0), view(0, 1), view(0, -1)
    dx, dy = east - west, north - south
    xy = view(1, 1) - view(-1, -1)
    xmy = view(1, -1) - view(-1, 1)
    along = sixth * view(0, 0) + twelfth * (east + west + north + south)
    gx = sixth * dx + twelfth * (xy + xmy + roll_z(dx, 1) + roll_z(dx, -1))
    gy = sixth * dy + twelfth * (xy - xmy + roll_z(dy, 1) + roll_z(dy, -1))
    return gx, gy, roll_z(along, 1) - roll_z(along, -1)


def moments(q):
    a, b = 1.0 / 18.0, 1.0 / 36.0

    def pair(i):
        return q[i] + q[i + 1], q[i] - q[i + 1]

    (sx, dx), (sy, dy), (sz, dz) = pair(1), pair(3), pair(5)
    (s7, d7), (s9, d9), (s11, d11) = pair(7), pair(9), pair(11)
    (s13, d13), (s15, d15), (s17, d17) = pair(13), pair(15), pair(17)
    xy, xz, yz = s7 + s9, s11 + s13, s15 + s17
    m0 = (1.0 / 3.0) * q[0] + a * (sx + sy + sz) + b * (xy + xz + yz)
    mx = a * dx + b * (d7 + d9 + d11 + d13)
    my = a * dy + b * (d7 - d9 + d15 + d17)
    mz = a * dz + b * (d11 - d13 + d15 - d17)
    mxx = a * sx + b * (xy + xz)
    myy = a * sy + b * (xy + yz)
    mzz = a * sz + b * (xz + yz)
    return m0, (mx, my, mz), (mxx, myy, mzz, b * (s7 - s9), b * (s11 - s13), b * (s15 - s17))


def velocity(f):
    density = f[0]
    for i in range(1, 19):
        density = density + f[i]
    d = {i: f[i] - f[i + 1] for i in range(1, 19, 2)}
    inv = 1.0 / density
    ux = (d[1] + d[7] + d[9] + d[11] + d[13]) * inv
    uy = (d[3] + d[7] - d[9] + d[15] + d[17]) * inv
    uz = (d[5] + d[11] - d[13] + d[15] - d[17]) * inv
    return ux, uy, uz


def apply_second(second, v):
    mxx, myy, mzz, mxy, mxz, myz = second
    x, y, z = v
    return (
        mxx * x + mxy * y + mxz * z,
        mxy * x + myy * y + myz * z,
        mxz * x + myz * y + mzz * z,
    )


def dot3(a, b):
    return a[0] * b[0] + a[1] * b[1] + a[2] * b[2]


def collide_back(post, q, u, phase, store):
    q0, q1, q2 = q
    omega = 1.0 / (relax_heavy * (1.0 + phase) * 0.5 + relax_light * (1.0 - phase) * 0.5)
    q2u = apply_second(q2, u)
    along = q0 - 4.5 * dot3(u, q2u) + 1.5 * dot3(u, u) * q0
    base = omega * along
    bx, by, bz = [omega * (3.0 * q1[d] + 9.0 * q2u[d] - 3.0 * u[d] * q0) for d in range(3)]
    keep = 1.0 - omega
    store(0, keep * post[0] + base)
    slopes = (bx, by, bz, bx + by, bx - by, bx + bz, bx - bz, by + bz, by - bz)
    for k, slope in enumerate(slopes):
        i = 1 + 2 * k
        store(i, keep * post[i] + (base + slope))
        store(i + 1, keep * post[i + 1] + (base - slope))


def gradient_back(q0, q2, n):
    nsq = dot3(n, n)
    root = 1.0 / jnp.sqrt(1.0 + nsq)
    q2n = apply_second(q2, n)
    energy = dot3(n, q2n) - (1.0 / 3.0) * nsq * q0
    third = (4.0 / 3.0) * q0
    tail = 2.0 * energy * root * root * root
    return [root * (4.0 * q2n[d] - third * n[d]) - tail * n[d] for d in range(3)]


def gradient_adjoint(view):
    sixth, twelfth = 1.0 / 6.0, 1.0 / 12.0
    xe, xw, yn, ys = view(0, 1, 0), view(0, -1, 0), view(1, 0, 1), view(1, 0, -1)
    zc = sixth * view(2, 0, 0)
    around = view(2, 1, 0) + view(2, -1, 0) + view(2, 0, 1) + view(2, 0, -1)
    across = xe - xw + yn - ys
    flat = sixth * across + twelfth * (
        view(0, 1, 1) + view(1, 1, 1) - view(0, -1, -1) - view(1, -1, -1)
        + view(0, 1, -1) - view(1, 1, -1) - view(0, -1, 1) + view(1, -1, 1)
    )
    ahead = zc + twelfth * (across + around)
    behind = twelfth * (across - around) - zc
    return -(flat + roll_z(ahead, 1) + roll_z(behind, -1))


def side_adjoint(rows, sign):
    sixth, twelfth = 1.0 / 6.0, 1.0 / 12.0
    gx, gy, gz = [lambda move, d=d: rows[d, pl.ds(1 + move, WX), :] for d in range(3)]
    flat = sixth * sign * gy(0) + twelfth * (sign * (gy(1) + gy(-1)) + gx(1) - gx(-1))
    return -(flat + twelfth * (roll_z(sign * gy(0) + gz(0), 1) + roll_z(sign * gy(0) - gz(0), -1)))


def whole_call(kernel, name, out_shape, args, scratch=(), aliases=None, in_hbm=False, specs=None):
    options = {}
    if in_hbm:
        options["in_specs"] = [pl.BlockSpec(memory_space=pl.ANY)] * len(args)
    else:
        if specs:
            options["in_specs"] = specs
        options["compiler_params"] = pltpu.CompilerParams(vmem_limit_bytes=24 * 1024 * 1024)
    return pl.pallas_call(
        kernel,
        out_shape=[
            pltpu.VMEM(shape, kind) if in_hbm else jax.ShapeDtypeStruct(shape, kind) for shape, kind in out_shape
        ],
        scratch_shapes=scratch,
        input_output_aliases=aliases or {},
        name=name,
        **options,
    )(*args)


class Pick:
    def __init__(self, first, a, b):
        self.first, self.a, self.b = first, a, b

    def __getitem__(self, index):
        return jnp.where(self.first, self.a[index], self.b[index])


def is_odd(axis):
    return lax.axis_index(axis) % 2 == 1


def sides(axis, a, b):
    odd = is_odd(axis)
    return Pick(odd, a, b), Pick(odd, b, a)


def put(odd, outs, index, up, down):
    outs[0][index] = jnp.where(odd, up, down)
    outs[1][index] = jnp.where(odd, down, up)


def put_rows(odd, outs, slot, flat, up, down):
    rows = [flat[pl.ds(start, NX, stride=NY), :].astype(f32) for start in (up, down)]
    put(odd, outs, (pl.ds(slot * NX, NX), slice(None)), *rows)


def put_pops(adj, x_outs, y_outs):
    odd_x, odd_y = is_odd("pipe"), is_odd("cross")
    flat = adj.reshape(19 * NX * NY, NZ)
    for k in range(5):
        put(odd_x, x_outs, k, adj[x_plus[k], 0], adj[x_minus[k], NX - 1])
        put_rows(odd_y, y_outs, k, flat, y_plus[k] * NX * NY, y_minus[k] * NX * NY + NY - 1)


def fetch(pairs, sem):
    copies = [pltpu.make_async_copy(a, b, sem.at[k]) for k, (a, b) in enumerate(pairs)]
    for copy in copies:
        copy.start()
    return copies


def along(x, y):
    return [i for i in range(19) if lattice_vel[i][:2] == (x, y)]


def corner_rows(adj, fluid, speed, side, sign):
    x, step = ((0, 1), (NX - 1, -1))[side]
    y = 0 if sign > 0 else NY - 1
    flat = adj.reshape(19 * NX * NY, NZ)
    rows = [flat[pl.ds(x * NY + y, 19, stride=NX * NY), :]]
    rows += [speed[d][y : y + 1, :] for d in range(3)]

    def row(ref, lead, a, b):
        return ref[lead + (a, pl.ds(b, 1), slice(None))].astype(f32)

    rows += [row(adj, (p,), x + step, y) for p in along(step, 0)]
    rows += [row(adj, (p,), x, y + sign) for p in along(0, sign)]
    (diagonal,) = along(step, sign)
    rows += [row(adj, (diagonal,), x + step, y + sign), row(adj, (diagonal,), x, y + sign)]
    return rows + [row(fluid, (), x, y + sign), row(fluid, (), x + step, y + sign), row(fluid, (), x + step, y)]


def pack_kernel(adj_hbm, *refs):
    hbm, pops_hbm, (xa, xb, ya, yb) = refs[:FIELDS], refs[FIELDS], refs[FIELDS + 1 : FIELDS + 5]
    adj, *fields = refs[FIELDS + 5 : -2]
    pops, sem = refs[-2:]
    pairs = [(adj_hbm, adj), *zip(hbm, fields)]
    pairs += [(pops_hbm.at[:, x], pops.at[:, k]) for k, x in enumerate((0, NX - 1))]
    for copy in fetch(pairs, sem):
        copy.wait()
    put_pops(adj, (xa, xb), (ya, yb))
    odd_x, odd_y = is_odd("pipe"), is_odd("cross")
    for k in range(FIELDS):
        put(odd_x, (xa, xb), 5 + k, fields[k][0].astype(f32), fields[k][NX - 1].astype(f32))
        put_rows(odd_y, (ya, yb), 5 + k, fields[k].reshape(NX * NY, NZ), 0, NY - 1)
    fluid = fields[2]
    for side in range(2):
        speed = velocity([pops[i, side] for i in range(19)])
        at = (5 + FIELDS) * NX + side * EXTRA
        for up, down in zip(*[corner_rows(adj, fluid, speed, side, sign) for sign in (1, -1)]):
            put(odd_y, (ya, yb), (pl.ds(at, up.shape[0]), slice(None)), up, down)
            at += up.shape[0]
    flats = [ref.reshape(X_PLANES * NY, NZ) for ref in (xa, xb)]
    for e, sign in enumerate((1, -1)):
        y = NY - 1 if sign > 0 else 0
        both = []
        for x, step in ((0, 1), (NX - 1, -1)):
            rows = [adj[p, x, pl.ds(y, 1), :] for p in along(0, -sign)]
            rows += [adj[p, x + step, pl.ds(y, 1), :] for p in along(step, -sign)]
            both.append(rows + [fluid[x + step, pl.ds(y, 1), :].astype(f32)])
        for k, (up, down) in enumerate(zip(*both)):
            put(odd_x, flats, (pl.ds(corner_at(e) + EXTRA + k, 1), slice(None)), up, down)


X_PLANES = 5 + FIELDS + 2 + 10


def corner_at(e):
    return (5 + FIELDS + 2 + 5 * e) * NY


def pack(adjoint, fields, pops):
    face, side = ((X_PLANES, NY, NZ), f32), (((5 + FIELDS) * NX + 2 * EXTRA, NZ), f32)
    scratch = [pltpu.VMEM((19, NX, NY, NZ), f32)]
    scratch += [pltpu.VMEM((NX, NY, NZ), field.dtype) for field in fields]
    scratch.append(pltpu.VMEM((19, 2, NY, NZ), f32))
    scratch.append(pltpu.SemaphoreType.DMA((3 + FIELDS,)))
    return whole_call(pack_kernel, "pack", [face, face, side, side], (adjoint, *fields, pops), scratch, in_hbm=True)


edge_plus = (7, 9)
edge_minus = (10, 8)


def pack_edges_kernel(xa, xb, ya, yb, _, xa_out, xb_out):
    planes = 5 + FIELDS
    for k in [*range(planes), *range(planes + 2, X_PLANES)]:
        xa_out[k] = xa[k]
        xb_out[k] = xb[k]
    low, high = sides("cross", ya, yb)
    odd = is_odd("pipe")
    flats = [ref.reshape(X_PLANES * NY, NZ) for ref in (xa_out, xb_out)]
    for e, (rows, pops) in enumerate(((high, y_plus), (low, y_minus))):
        xa_out[planes + e] = jnp.zeros((NY, NZ), f32)
        xb_out[planes + e] = jnp.zeros((NY, NZ), f32)
        starts = [(pops.index(edge_plus[e]), pops.index(edge_minus[e]))] + [(5 + k, 5 + k) for k in range(FIELDS)]
        for r, (up, down) in enumerate(starts):
            up_row = rows[pl.ds(up * NX, 1), :]
            down_row = rows[pl.ds(down * NX + NX - 1, 1), :]
            put(odd, (xa_out, xb_out), (planes + e, pl.ds(r, 1), slice(None)), up_row, down_row)
        up, down = [rows[pl.ds(planes * NX + side * EXTRA, EXTRA), :] for side in range(2)]
        put(odd, flats, (pl.ds(corner_at(e), EXTRA), slice(None)), up, down)


def pack_edges(x_pair, y_halo, after):
    out = ((X_PLANES, NY, NZ), f32)
    return whole_call(pack_edges_kernel, "pack_edges", [out, out], (*x_pair, *y_halo, after))


def fill_sides(pad, lead, y_low, low_slot, y_high, high_slot):
    for x in range(NX):
        pad[lead + (x + 1, pl.ds(LOW - 1, 1), slice(None))] = y_low[pl.ds(low_slot * NX + x, 1), :]
        pad[lead + (x + 1, pl.ds(LOW + NY, 1), slice(None))] = y_high[pl.ds(high_slot * NX + x, 1), :]


def fill_pops(pad, adj, planes, y_low, y_high):
    for p in range(19):
        for x in planes:
            pad[p, x + 1, pl.ds(LOW, NY), :] = adj[p, x]
    for k in range(5):
        for x in planes:
            pad[y_minus[k], x + 1, pl.ds(LOW - 1, 1), :] = y_low[pl.ds(k * NX + x, 1), :]
            pad[y_plus[k], x + 1, pl.ds(LOW + NY, 1), :] = y_high[pl.ds(k * NX + x, 1), :]


def fill_pops_outer(pad, x_low, x_high, edge):
    for k in range(5):
        pad[x_minus[k], 0, pl.ds(LOW, NY), :] = x_low[k]
        pad[x_plus[k], WX - 1, pl.ds(LOW, NY), :] = x_high[k]
    for e, row in enumerate((LOW + NY, LOW - 1)):
        pad[edge_minus[e], 0, pl.ds(row, 1), :] = edge(0, e)
        pad[edge_plus[e], WX - 1, pl.ds(row, 1), :] = edge(1, e)


def edge_of(edges):
    return lambda side, e: edges[pl.ds(2 * side + e, 1), :]


def fill_field(pad, lead, own, slot, y_low, y_high):
    for x in range(NX):
        pad[lead + (x + 1, pl.ds(LOW, NY), slice(None))] = own[x].astype(f32)
    fill_sides(pad, lead, y_low, 5 + slot, y_high, 5 + slot)


def fill_field_outer(pad, lead, slot, x_low, x_high):
    for x, face in ((0, x_low), (WX - 1, x_high)):
        pad[lead + (x, pl.ds(LOW, NY), slice(None))] = face[5 + slot]
        for e, row in enumerate((LOW + NY, LOW - 1)):
            pad[lead + (x, pl.ds(row, 1), slice(None))] = face[5 + FIELDS + e, pl.ds(1 + slot, 1), :]


def propagate_back(adj_pad, fluid_pad, x, low=LOW):
    here = tile(fluid_pad, (), x, (0, 0, 0), low)
    post = [here * adj_pad[0, x + 1, pl.ds(low, NY), :]]
    for i in range(1, 19):
        ahead = tile(fluid_pad, (), x, lattice_vel[i], low)
        moved = tile(adj_pad, (i,), x, lattice_vel[i], low)
        back = adj_pad[opposite[i], x + 1, pl.ds(low, NY), :]
        post.append(here * jnp.where(ahead != 0.0, moved, back))
    return post


def step_plane(x, adj_pad, fluid_pad, speed, phase, adj_out, mom_out, at=0):
    post = propagate_back(adj_pad, fluid_pad, x)
    q = moments(post)

    def store(i, value):
        adj_out[i, x - at] = value

    collide_back(post, q, [speed[d, x] for d in range(3)], phase[x], store)
    if mom_out is not None:
        mom_out[0, x] = q[0]
        for k in range(6):
            mom_out[1 + k, x] = q[2][k]


inner = range(1, NX - 1)


def second_inner_kernel(speed, phase, adj, fluid, ya, yb, adj_out, mom_out, adj_pad, fluid_pad):
    y_low, y_high = sides("cross", ya, yb)
    fill_field(fluid_pad, (), fluid, 2, y_low, y_high)
    fill_pops(adj_pad, adj, range(NX), y_low, y_high)

    def plane(x, carry):
        step_plane(x, adj_pad, fluid_pad, speed, phase, adj_out, mom_out)
        return carry

    lax.fori_loop(1, NX - 1, plane, 0, unroll=2)


block = ((19, NX, NY, NZ), f32)
seven = ((7, NX, NY, NZ), f32)
vector = ((3, NX, NY, NZ), f32)


def pad_scratch():
    return [pltpu.VMEM((19, WX, ROWS, NZ), f32), pltpu.VMEM((WX, ROWS, NZ), f32)]


def corner_edges(adj, fluid, y_sides, x_sides, edges_out, corner_pad, corner_fluid):
    base = (5 + FIELDS) * NX
    for side, face in enumerate(x_sides):
        sx = (-1, 1)[side]
        x = (0, NX - 1)[side]
        near, far = 1 - sx, 1 + sx
        pad, wet = corner_pad.at[side], corner_fluid.at[side]
        flat = Pick(face.first, *[ref.reshape(X_PLANES * NY, NZ) for ref in (face.a, face.b)])
        for e, (rows, sy) in enumerate(zip(y_sides, (1, -1))):
            at = LOW + NY if sy > 0 else LOW - 1
            inner_y = NY - 1 if sy > 0 else 0
            first = corner_at(e)

            def got(r):
                return flat[pl.ds(first + r, 1), :]

            def beside(r):
                return rows[pl.ds(base + side * EXTRA + r, 1), :]

            def set_pops(pops, plane, row, values):
                for p, value in zip(pops, values):
                    pad[p, plane, pl.ds(row, 1), :] = value

            set_pops(range(19), 1, at, [got(r) for r in range(19)])
            set_pops(along(sx, 0), far, at, [got(22 + r) for r in range(3)])
            set_pops(along(0, sy), 1, at + sy, [got(25 + r) for r in range(3)])
            set_pops(along(sx, sy), far, at + sy, [got(28)])
            set_pops(along(-sx, 0), near, at, [beside(p) for p in along(-sx, 0)])
            set_pops(along(-sx, sy), near, at + sy, [beside(29)])
            set_pops(along(0, -sy), 1, at - sy, [got(EXTRA + r) for r in range(3)])
            set_pops(along(sx, -sy), far, at - sy, [got(EXTRA + 3)])
            set_pops(along(-sx, -sy), near, at - sy, [adj[p, x, pl.ds(inner_y, 1), :] for p in along(-sx, -sy)])
            for plane, row, value in (
                (1, at, face[5 + FIELDS + e, pl.ds(3, 1), :]),
                (far, at, got(32)),
                (1, at + sy, got(30)),
                (far, at + sy, got(31)),
                (near, at, rows[pl.ds((5 + 2) * NX + x, 1), :]),
                (near, at + sy, beside(30)),
                (1, at - sy, face[5 + 2, pl.ds(inner_y, 1), :]),
                (far, at - sy, got(EXTRA + 4)),
                (near, at - sy, fluid[x, pl.ds(inner_y, 1), :].astype(f32)),
            ):
                wet[plane, pl.ds(row, 1), :] = value
            low = LOW + 1 if sy > 0 else LOW - 1
            post = propagate_back(pad, wet, 0, low)
            u = [jnp.broadcast_to(got(19 + d), (NY, NZ)) for d in range(3)]
            phase = jnp.broadcast_to(face[5 + FIELDS + e, pl.ds(2, 1), :], (NY, NZ))
            kept = {}
            collide_back(post, moments(post), u, phase, kept.__setitem__)
            (crossing,) = along(sx, sy)
            edges_out[pl.ds(2 * side + e, 1), :] = kept[crossing][at - low : at - low + 1, :]
    edges_out[pl.ds(4, 4), :] = jnp.zeros((4, NZ), f32)


def second_outer_kernel(
    speed, phase, adj, fluid, ya, yb, xa, xb, adj_in, mom_in, _,
    adj_out, mom_out, xa_out, xb_out, ya_out, yb_out, edges_out,
    adj_pad, fluid_pad, corner_pad, corner_fluid,
):
    (x_low, x_high), (y_low, y_high) = sides("pipe", xa, xb), sides("cross", ya, yb)
    fill_field(fluid_pad, (), fluid, 2, y_low, y_high)
    fill_field_outer(fluid_pad, (), 2, x_low, x_high)
    fill_pops(adj_pad, adj, (0, 1, NX - 2, NX - 1), y_low, y_high)
    faces = (x_low, x_high)
    fill_pops_outer(adj_pad, x_low, x_high, lambda side, e: faces[side][5 + FIELDS + e, pl.ds(0, 1), :])
    for x in (0, NX - 1):
        step_plane(x, adj_pad, fluid_pad, speed, phase, adj_out, mom_out)
    put_pops(adj_out, (xa_out, xb_out), (ya_out, yb_out))
    corner_edges(adj, fluid, (y_high, y_low), faces, edges_out, corner_pad, corner_fluid)


def one_hots(index, row, hit_out, right_out, at):
    row_iota = lax.broadcasted_iota(jnp.int32, (64, NZ), 0)
    key = (lax.shift_right_logical(index, 6) & 1) * 32 + lax.shift_right_logical(index, 7)
    low = index & 63
    hit = jnp.where(row_iota == key[row : row + 1, :], 1.0, 0.0)
    hit_out[:, pl.ds(at, NZ)] = hit.astype(jnp.bfloat16)
    right = jnp.where(row_iota == low[row : row + 1, :], 1.0, 0.0)
    right_out[:, pl.ds(at, NZ)] = right.astype(jnp.bfloat16)


OWN = NX * NY * NZ
SIDES = 2 * NX * NZ
FACES = (2 * NY + 4) * NZ


def store_velocity(pops, out):
    def plane(x, carry):
        u = velocity([pops[i, x] for i in range(19)])
        for d in range(3):
            out[d, x] = u[d]
        return carry

    lax.fori_loop(0, NX, plane, 0, unroll=2)


def own_kernel(
    table_hbm, phase_a_hbm, phase_b_hbm, fluid_hbm, wall_hbm, patch_hbm, pops_hbm,
    phi_out, hit_out, right_out, wall_out, speed_out,
    table, phase_a, phase_b, fluid, wall, patch, pops, sem,
):
    hbm = (table_hbm, phase_a_hbm, phase_b_hbm, fluid_hbm, wall_hbm, patch_hbm, pops_hbm)
    copies = fetch(zip(hbm, (table, phase_a, phase_b, fluid, wall, patch, pops)), sem)
    for copy in copies[:-1]:
        copy.wait()

    def plane(x, carry):
        index = patch[x] & 4095
        wall_out[x] = wall[x].astype(f32)
        contact = wall[x].astype(f32) * look_up(table, index)
        wet = fluid[x].astype(f32)
        phi_out[0, x] = wet * phase_a[x] + contact
        phi_out[1, x] = wet * phase_b[x] + contact
        for r in range(NY):
            one_hots(index, r, hit_out, right_out, pl.multiple_of((x * NY + r) * NZ, NZ))
        return carry

    lax.fori_loop(0, NX, plane, 0, unroll=2)
    copies[-1].wait()
    store_velocity(pops, speed_out)


def imposed(table, slot):
    index = slot(4).astype(jnp.int32) & 4095
    contact = slot(3) * look_up(table, index)
    return index, [slot(2) * slot(t) + contact for t in range(2)]


def side_kernel(table, ya, yb, phi_out, wall_out, hit_out, right_out):
    for side, rows in enumerate(sides("cross", ya, yb)):
        index, values = imposed(table, lambda k: rows[pl.ds((5 + k) * NX, NX), :])
        wall_out[side] = rows[pl.ds(8 * NX, NX), :]
        for t in range(2):
            phi_out[side, t] = values[t]
        for x in range(NX):
            one_hots(index, x, hit_out, right_out, (side * NX + x) * NZ)


def middle_kernel(
    phi, table, fluid, mom, ya, yb, xa, xb, phi_side, wall_beside,
    dgrad_out, grad_out, fluid_out, wall_face, wall_side, hit_out, right_out,
    phi_pad,
):
    (x_low, x_high), (y_low, y_high) = sides("pipe", xa, xb), sides("cross", ya, yb)
    fill_field(fluid_out, (), fluid, 2, y_low, y_high)
    fill_field_outer(fluid_out, (), 2, x_low, x_high)
    for x in range(NX):
        for t in range(2):
            phi_pad[t, x + 1, pl.ds(LOW, NY), :] = phi[t, x]
            for side, y in enumerate((LOW - 1, LOW + NY)):
                phi_pad[t, x + 1, pl.ds(y, 1), :] = phi_side[side, t, pl.ds(x, 1), :]
    for side, (face, x) in enumerate(((x_low, 0), (x_high, WX - 1))):
        index, values = imposed(table, lambda k: face[5 + k])
        wall_face[side] = face[8]
        wall_side[side, pl.ds(1, NX), :] = wall_beside[side]
        for t in range(2):
            phi_pad[t, x, pl.ds(LOW, NY), :] = values[t]
        for r in range(NY):
            one_hots(index, r, hit_out, right_out, (side * NY + r) * NZ)

    def corner_tile(k):
        rows = [face[5 + FIELDS + 1 - e, pl.ds(1 + k, 1), :] for e in range(2) for face in (x_low, x_high)]
        return jnp.concatenate(rows + rows, axis=0)

    index, values = imposed(table, corner_tile)
    on_wall = corner_tile(3)
    for r in range(4):
        side, x, y = r // 2, (WX - 1) * (r % 2), (LOW - 1, LOW + NY)[r // 2]
        wall_side[side, pl.ds(x, 1), :] = on_wall[r : r + 1, :]
        for t in range(2):
            phi_pad[t, x, pl.ds(y, 1), :] = values[t][r : r + 1, :]
        one_hots(index, r, hit_out, right_out, (2 * NY + r) * NZ)

    def plane(x, carry):
        def view(t):
            return lambda a, b: tile(phi_pad, (t,), x, (a, b, 0))

        first, n = gradient(view(0)), gradient(view(1))
        for d in range(3):
            grad_out[d, x] = first[d]
        dgrad = gradient_back(mom[0, x], [mom[1 + k, x] for k in range(6)], n)
        for d in range(3):
            dgrad_out[d, x] = dgrad[d]
        return carry

    lax.fori_loop(0, NX, plane, 0, unroll=2)


def speed_kernel(pops_hbm, _, out, pops, sem):
    for copy in fetch([(pops_hbm, pops)], sem):
        copy.wait()
    store_velocity(pops, out)


def own_terms(*args):
    hots = ((64, OWN), jnp.bfloat16)
    scratch = [pltpu.VMEM(arg.shape, arg.dtype) for arg in args] + [pltpu.SemaphoreType.DMA((len(args),))]
    shapes = [((2, NX, NY, NZ), f32), hots, hots, ((NX, NY, NZ), f32), vector]
    return whole_call(own_kernel, "own_terms", shapes, args, scratch, specs=[pl.BlockSpec(memory_space=pl.ANY)] * len(args))


def side_terms(*args):
    shapes = [((2, 2, NX, NZ), f32), ((2, NX, NZ), f32)] + [((64, SIDES), jnp.bfloat16)] * 2
    return whole_call(side_kernel, "side_terms", shapes, args)


def middle(*args):
    shapes = [vector, vector, ((WX, ROWS, NZ), f32), ((2, NY, NZ), f32), ((2, WX, NZ), f32)]
    shapes += [((64, FACES), jnp.bfloat16)] * 2
    return whole_call(middle_kernel, "middle", shapes, args, [pltpu.VMEM((2, WX, ROWS, NZ), f32)])


def first_speed(pops, after):
    scratch = [pltpu.VMEM((19, NX, NY, NZ), f32), pltpu.SemaphoreType.DMA((1,))]
    specs = [pl.BlockSpec(memory_space=pl.ANY)] * 2
    return whole_call(speed_kernel, "first_speed", [vector], (pops, after), scratch, specs=specs)[0]


def weighted(hit, values):
    bigs, smalls = [], []
    for value in values:
        big = value.astype(jnp.bfloat16).astype(f32)
        for r in range(value.shape[0]):
            for rows, source in ((bigs, big), (smalls, value - big)):
                row = jnp.broadcast_to(source[r : r + 1, :], (16, NZ)).astype(jnp.bfloat16)
                rows.append(jnp.concatenate([row] * 4, axis=0))
    return jnp.concatenate(
        [hit * jnp.concatenate(bigs, axis=1), hit * jnp.concatenate(smalls, axis=1)], axis=0
    )


def table_sum(left, right):
    return lax.dot_general(left, right, (((1,), (1,)), ((), ())), preferred_element_type=f32)


def gradient_plane(x, adj_pad, fluid_pad, grad, dgrad_in, out):
    q0, _, q2 = moments(propagate_back(adj_pad, fluid_pad, x))
    dgrad = gradient_back(q0, q2, [grad[d, x] for d in range(3)])
    for d in range(3):
        out(d, x, dgrad[d] + dgrad_in[d, x])


def plane_adjoint(pad, x):
    return gradient_adjoint(lambda d, a, b: pad[d, x + 1 + a, pl.ds(LOW + b, NY), :])


GROUP = 4


def own_group(start, dgrad_pad, wall, hits, rights):
    values = [plane_adjoint(dgrad_pad, start + k + 1) * wall[start + k] for k in range(GROUP)]
    nodes = pl.ds(pl.multiple_of(start * NY * NZ, NY * NZ), GROUP * NY * NZ)
    return table_sum(weighted(hits[:, nodes], values), rights[:, nodes])


def first_inner_kernel(
    adj, fluid_pad, grad, dgrad_in, ya, yb, wall, hits, rights,
    dgrad_out, acc_out,
    adj_pad, dgrad_pad,
):
    y_low, y_high = sides("cross", ya, yb)
    fill_pops(adj_pad, adj, range(NX), y_low, y_high)
    dgrad_pad[...] = jnp.zeros_like(dgrad_pad)

    def out(d, x, value):
        dgrad_out[d, x] = value
        dgrad_pad[d, x + 2, pl.ds(LOW, NY), :] = value

    def plane(x, carry):
        gradient_plane(x, adj_pad, fluid_pad, grad, dgrad_in, out)
        return carry

    lax.fori_loop(1, NX - 1, plane, 0, unroll=2)
    acc_out[...] = jnp.zeros_like(acc_out)

    def group(g, carry):
        acc_out[...] += own_group(2 + g * GROUP, dgrad_pad, wall, hits, rights)
        return carry

    lax.fori_loop(0, (NX - 4) // GROUP, group, 0)


def first_outer_kernel(
    adj, fluid_pad, grad, dgrad_in, ya, yb, xa, xb, edges, dgrad_inner, acc_in,
    wall, hits, rights, wall_face, wall_side, face_hits, face_rights, side_hits, side_rights,
    total_out,
    adj_pad, dgrad_pad, rows,
):
    (x_low, x_high), (y_low, y_high) = sides("pipe", xa, xb), sides("cross", ya, yb)
    fill_pops(adj_pad, adj, (0, 1, NX - 2, NX - 1), y_low, y_high)
    fill_pops_outer(adj_pad, x_low, x_high, edge_of(edges))
    for d in range(3):
        for x in (0, 1, 2, 3, NX, NX + 1, NX + 2, NX + 3):
            dgrad_pad[d, x] = jnp.zeros((ROWS, NZ), f32)

    def out(d, x, value):
        dgrad_pad[d, x + 2, pl.ds(LOW, NY), :] = value

    for x in (0, NX - 1):
        gradient_plane(x, adj_pad, fluid_pad, grad, dgrad_in, out)
    for x in inner:
        for d in range(3):
            out(d, x, dgrad_inner[d, x])
    values = [plane_adjoint(dgrad_pad, x + 1) * wall[x] for x in (0, 1, NX - 2, NX - 1)]
    total = acc_in[...]
    for k, start in enumerate((0, NX - 2)):
        nodes = pl.ds(start * NY * NZ, 2 * NY * NZ)
        total = total + table_sum(weighted(hits[:, nodes], values[2 * k : 2 * k + 2]), rights[:, nodes])
    values = [plane_adjoint(dgrad_pad, x) * wall_face[k] for k, x in enumerate((0, WX - 1))]
    flat = dgrad_pad.reshape(3 * (WX + 2) * ROWS, NZ)
    beside, corners = [], []
    for side, (row, sign) in enumerate(((LOW, 1.0), (LOW + NY - 1, -1.0))):
        for d in range(3):
            rows[d] = flat[pl.ds(d * (WX + 2) * ROWS + row, WX + 2, stride=ROWS), :]
        value = side_adjoint(rows, sign) * wall_side[side]
        beside.append(value[1 : WX - 1])
        corners += [value[:1], value[WX - 1 :]]
    values.append(jnp.concatenate(corners, axis=0))
    total = total + table_sum(weighted(face_hits[...], values), face_rights[...])
    total = total + table_sum(weighted(side_hits[...], beside), side_rights[...])
    both = total[:64] + total[64:]
    total_out[...] = jnp.concatenate([both[:32], both[32:]], axis=1)


shares = ((0, 6), (6, 5), (11, 5))


def first_adjoint_kernel(
    start, count, speed, phase, adj, fluid_pad, ya, yb, xa, xb, edges, *refs
):
    out, adj_pad, part, sem = refs[-4:]
    (x_low, x_high), (y_low, y_high) = sides("pipe", xa, xb), sides("cross", ya, yb)
    planes = range(max(start - 1, 0), min(start + count + 1, NX))
    fill_pops(adj_pad, adj, planes, y_low, y_high)
    if start == 0 or start + count == NX:
        fill_pops_outer(adj_pad, x_low, x_high, edge_of(edges))

    def plane(k, carry):
        step_plane(start + k, adj_pad, fluid_pad, speed, phase, part, None, start)
        return carry

    lax.fori_loop(0, count, plane, 0)
    (copy,) = fetch([(part, out.at[:, pl.ds(start, count)])], sem)
    copy.wait()


def first_adjoint(start, count, args, after, before):
    args = (*args, after) if before is None else (*args, after, before)
    specs = [pl.BlockSpec(memory_space=pltpu.VMEM)] * 9 + [pl.BlockSpec(memory_space=pl.ANY)] * (len(args) - 9)
    return pl.pallas_call(
        functools.partial(first_adjoint_kernel, start, count),
        out_shape=jax.ShapeDtypeStruct(*block),
        in_specs=specs,
        out_specs=pl.BlockSpec(memory_space=pl.ANY),
        scratch_shapes=[
            pltpu.VMEM((19, WX, ROWS, NZ), f32),
            pltpu.VMEM((19, count, NY, NZ), f32),
            pltpu.SemaphoreType.DMA((1,)),
        ],
        input_output_aliases={} if before is None else {10: 0},
        compiler_params=pltpu.CompilerParams(vmem_limit_bytes=24 * 1024 * 1024),
        name="first_adjoint",
    )(*args)


def swap(axis, a, b):
    count = lax.axis_size(axis)
    near = lax.ppermute(a, axis, [(i, i ^ 1) for i in range(count)])
    far = lax.ppermute(b, axis, [(i, (i + 2 * (i % 2) - 1) % count) for i in range(count)])
    return near, far


def mirror(index, low, size):
    digit = index // low % size
    return index + (size - 1 - 2 * digit) * low


def sum_rounds():
    return (
        (lambda p, c: (p ^ 1, c),),
        (
            lambda p, c: (mirror(p, 2, 4) ^ 1, c),
            lambda p, c: (p ^ 3, c),
            lambda p, c: (mirror(p, 2, 4) ^ 3, c),
        ),
        (
            lambda p, c: (p ^ 1, mirror(c, 1, 4)),
            lambda p, c: (p ^ 1, c ^ 1),
            lambda p, c: (p ^ 1, mirror(c, 1, 4) ^ 1),
        ),
        (
            lambda p, c: (p ^ 1, mirror(c, 4, 4)),
            lambda p, c: (p ^ 1, c ^ 4),
            lambda p, c: (p ^ 1, mirror(c, 4, 4) ^ 4),
        ),
    )


def exchange(value, place):
    pipe, cross = lax.axis_size("pipe"), lax.axis_size("cross")
    pairs = []
    for p in range(pipe):
        for c in range(cross):
            q, d = place(p, c)
            pairs.append((p * cross + c, q * cross + d))
    return lax.ppermute(value, ("pipe", "cross"), pairs)


def pack_pairs(packed):
    return packed[:2], packed[2:]


def shards(
    pops_first,
    pops_second,
    phase_first,
    phase_second,
    adjoint_last,
    wettability,
    fluid,
    wall,
    patch,
):
    table = wettability.reshape(32, NZ)
    fields = (phase_first, phase_second, fluid, wall, patch)
    x_swap, y_swap = pack_pairs(pack(adjoint_last, fields, pops_second))
    y_halo = swap("cross", *y_swap)
    phi, hits, rights, wall_own, speed = own_terms(table, *fields, pops_second)
    x_halo = swap("pipe", *pack_edges(x_swap, y_halo, phi))
    phi_side, wall_beside, side_hits, side_rights = side_terms(table, *y_halo)
    given = (speed, phase_second, adjoint_last, fluid, *y_halo)
    adjoint, mom = whole_call(
        second_inner_kernel, "second_inner", [block, seven], given, pad_scratch()
    )
    face, side = ((5, NY, NZ), f32), ((5 * NX, NZ), f32)
    adjoint, mom, *packed, edges = whole_call(
        second_outer_kernel,
        "second_outer",
        [block, seven, face, face, side, side, ((8, NZ), f32)],
        given + x_halo + (adjoint, mom, phi_side),
        pad_scratch() + [pltpu.VMEM((2, 19, 3, ROWS, NZ), f32), pltpu.VMEM((2, 3, ROWS, NZ), f32)],
        {8: 0, 9: 1},
    )
    x_swap, y_swap = pack_pairs(packed)
    y_halo2, x_halo2 = swap("cross", *y_swap), swap("pipe", *x_swap)
    dgrad, grad, fluid_pad, wall_face, wall_side, face_hits, face_rights = middle(
        phi, table, fluid, mom, *y_halo, *x_halo, phi_side, wall_beside
    )
    given = (adjoint, fluid_pad, grad, dgrad, *y_halo2)
    nodes = (wall_own, hits, rights)
    adj_scratch = pad_scratch()[:1]
    dgrad_scratch = adj_scratch + [pltpu.VMEM((3, WX + 2, ROWS, NZ), f32)]
    dgrad_inner, acc = whole_call(
        first_inner_kernel, "first_inner", [vector, ((128, 64), f32)], given + nodes, dgrad_scratch
    )
    (total,) = whole_call(
        first_outer_kernel,
        "first_outer",
        [((32, NZ), f32)],
        given + x_halo2 + (edges, dgrad_inner, acc) + nodes + (wall_face, wall_side, face_hits, face_rights, side_hits, side_rights),
        dgrad_scratch + [pltpu.VMEM((3, WX + 2, NZ), f32)],
    )
    args = (first_speed(pops_first, total), phase_first, adjoint, fluid_pad, *y_halo2, *x_halo2, edges)
    result = None
    for k, places in enumerate(sum_rounds()):
        got = [exchange(total, place) for place in places]
        if k:
            result = first_adjoint(*shares[k - 1], args, total, result)
            *got, result = lax.optimization_barrier((*got, result))
        for part in got:
            total = total + part
    return result, total.reshape(wettability.shape)


def solution(mesh):
    return jax.shard_map(
        shards,
        mesh=mesh,
        in_specs=(
            P(None, "pipe", "cross", None),
            P(None, "pipe", "cross", None),
            P("pipe", "cross", None),
            P("pipe", "cross", None),
            P(None, "pipe", "cross", None),
            P(),
            P("pipe", "cross", None),
            P("pipe", "cross", None),
            P("pipe", "cross", None),
        ),
        out_specs=(P(None, "pipe", "cross", None), P()),
        check_vma=False,
    )
```

```python
import functools

import jax
import jax.numpy as jnp
from jax import lax
from jax.experimental import pallas as pl
from jax.experimental.pallas import tpu as pltpu
from jax.sharding import PartitionSpec as P

lattice_vel = (
    (0, 0, 0),
    (1, 0, 0),
    (-1, 0, 0),
    (0, 1, 0),
    (0, -1, 0),
    (0, 0, 1),
    (0, 0, -1),
    (1, 1, 0),
    (-1, -1, 0),
    (1, -1, 0),
    (-1, 1, 0),
    (1, 0, 1),
    (-1, 0, -1),
    (1, 0, -1),
    (-1, 0, 1),
    (0, 1, 1),
    (0, -1, -1),
    (0, 1, -1),
    (0, -1, 1),
)
opposite = (0, 2, 1, 4, 3, 6, 5, 8, 7, 10, 9, 12, 11, 14, 13, 16, 15, 18, 17)
relax_heavy = 1.0
relax_light = 0.7

x_plus = (1, 7, 9, 11, 13)
x_minus = (2, 8, 10, 12, 14)
y_plus = (3, 7, 10, 15, 17)
y_minus = (4, 8, 9, 16, 18)

NX = 16
NY = 8
NZ = 128
WX = NX + 2
LOW = 8
ROWS = 24
EXTRA = 33
OWN_EXTRA = 5
FIELDS = 5
f32 = jnp.float32


def tile(ref, lead, x, move, low=LOW):
    index = lead + (x + 1 + move[0], pl.ds(low + move[1], NY), slice(None))
    value = ref[index]
    if move[2]:
        value = pltpu.roll(value, (-move[2]) % NZ, 1)
    return value


def look_up(table, index):
    high = lax.shift_right_logical(index, 7)
    low = index & 127
    result = jnp.zeros(index.shape, f32)
    for r in range(32):
        row = jnp.broadcast_to(table[pl.ds(r, 1), :], index.shape)
        picked = jnp.take_along_axis(row, low, axis=1, mode="promise_in_bounds")
        result = jnp.where(high == r, picked, result)
    return result


def roll_z(value, step):
    return pltpu.roll(value, (-step) % NZ, 1)


def gradient(view):
    sixth, twelfth = 1.0 / 6.0, 1.0 / 12.0
    east, west, north, south = view(1, 0), view(-1, 0), view(0, 1), view(0, -1)
    dx, dy = east - west, north - south
    xy = view(1, 1) - view(-1, -1)
    xmy = view(1, -1) - view(-1, 1)
    along = sixth * view(0, 0) + twelfth * (east + west + north + south)
    gx = sixth * dx + twelfth * (xy + xmy + roll_z(dx, 1) + roll_z(dx, -1))
    gy = sixth * dy + twelfth * (xy - xmy + roll_z(dy, 1) + roll_z(dy, -1))
    return gx, gy, roll_z(along, 1) - roll_z(along, -1)


def moments(q):
    a, b = 1.0 / 18.0, 1.0 / 36.0

    def pair(i):
        return q[i] + q[i + 1], q[i] - q[i + 1]

    (sx, dx), (sy, dy), (sz, dz) = pair(1), pair(3), pair(5)
    (s7, d7), (s9, d9), (s11, d11) = pair(7), pair(9), pair(11)
    (s13, d13), (s15, d15), (s17, d17) = pair(13), pair(15), pair(17)
    xy, xz, yz = s7 + s9, s11 + s13, s15 + s17
    m0 = (1.0 / 3.0) * q[0] + a * (sx + sy + sz) + b * (xy + xz + yz)
    mx = a * dx + b * (d7 + d9 + d11 + d13)
    my = a * dy + b * (d7 - d9 + d15 + d17)
    mz = a * dz + b * (d11 - d13 + d15 - d17)
    mxx = a * sx + b * (xy + xz)
    myy = a * sy + b * (xy + yz)
    mzz = a * sz + b * (xz + yz)
    return m0, (mx, my, mz), (mxx, myy, mzz, b * (s7 - s9), b * (s11 - s13), b * (s15 - s17))


def velocity(f):
    density = f[0]
    for i in range(1, 19):
        density = density + f[i]
    d = {i: f[i] - f[i + 1] for i in range(1, 19, 2)}
    inv = 1.0 / density
    ux = (d[1] + d[7] + d[9] + d[11] + d[13]) * inv
    uy = (d[3] + d[7] - d[9] + d[15] + d[17]) * inv
    uz = (d[5] + d[11] - d[13] + d[15] - d[17]) * inv
    return ux, uy, uz


def apply_second(second, v):
    mxx, myy, mzz, mxy, mxz, myz = second
    x, y, z = v
    return (
        mxx * x + mxy * y + mxz * z,
        mxy * x + myy * y + myz * z,
        mxz * x + myz * y + mzz * z,
    )


def dot3(a, b):
    return a[0] * b[0] + a[1] * b[1] + a[2] * b[2]


def collide_back(post, q, u, phase, store):
    q0, q1, q2 = q
    omega = 1.0 / (relax_heavy * (1.0 + phase) * 0.5 + relax_light * (1.0 - phase) * 0.5)
    q2u = apply_second(q2, u)
    along = q0 - 4.5 * dot3(u, q2u) + 1.5 * dot3(u, u) * q0
    base = omega * along
    bx, by, bz = [omega * (3.0 * q1[d] + 9.0 * q2u[d] - 3.0 * u[d] * q0) for d in range(3)]
    keep = 1.0 - omega
    store(0, keep * post[0] + base)
    slopes = (bx, by, bz, bx + by, bx - by, bx + bz, bx - bz, by + bz, by - bz)
    for k, slope in enumerate(slopes):
        i = 1 + 2 * k
        store(i, keep * post[i] + (base + slope))
        store(i + 1, keep * post[i + 1] + (base - slope))


def gradient_back(q0, q2, n):
    nsq = dot3(n, n)
    root = 1.0 / jnp.sqrt(1.0 + nsq)
    q2n = apply_second(q2, n)
    energy = dot3(n, q2n) - (1.0 / 3.0) * nsq * q0
    third = (4.0 / 3.0) * q0
    tail = 2.0 * energy * root * root * root
    return [root * (4.0 * q2n[d] - third * n[d]) - tail * n[d] for d in range(3)]


def gradient_adjoint(view):
    sixth, twelfth = 1.0 / 6.0, 1.0 / 12.0
    xe, xw, yn, ys = view(0, 1, 0), view(0, -1, 0), view(1, 0, 1), view(1, 0, -1)
    zc = sixth * view(2, 0, 0)
    around = view(2, 1, 0) + view(2, -1, 0) + view(2, 0, 1) + view(2, 0, -1)
    across = xe - xw + yn - ys
    flat = sixth * across + twelfth * (
        view(0, 1, 1) + view(1, 1, 1) - view(0, -1, -1) - view(1, -1, -1)
        + view(0, 1, -1) - view(1, 1, -1) - view(0, -1, 1) + view(1, -1, 1)
    )
    ahead = zc + twelfth * (across + around)
    behind = twelfth * (across - around) - zc
    return -(flat + roll_z(ahead, 1) + roll_z(behind, -1))


def side_adjoint(rows, sign):
    sixth, twelfth = 1.0 / 6.0, 1.0 / 12.0
    gx, gy, gz = [lambda move, d=d: rows[d, pl.ds(1 + move, WX), :] for d in range(3)]
    flat = sixth * sign * gy(0) + twelfth * (sign * (gy(1) + gy(-1)) + gx(1) - gx(-1))
    return -(flat + twelfth * (roll_z(sign * gy(0) + gz(0), 1) + roll_z(sign * gy(0) - gz(0), -1)))


def whole_call(kernel, name, out_shape, args, scratch=(), aliases=None, in_hbm=False, specs=None):
    options = {}
    if in_hbm:
        options["in_specs"] = [pl.BlockSpec(memory_space=pl.ANY)] * len(args)
    else:
        if specs:
            options["in_specs"] = specs
        options["compiler_params"] = pltpu.CompilerParams(vmem_limit_bytes=24 * 1024 * 1024)
    return pl.pallas_call(
        kernel,
        out_shape=[
            pltpu.VMEM(shape, kind) if in_hbm else jax.ShapeDtypeStruct(shape, kind) for shape, kind in out_shape
        ],
        scratch_shapes=scratch,
        input_output_aliases=aliases or {},
        name=name,
        **options,
    )(*args)


class Pick:
    def __init__(self, first, a, b):
        self.first, self.a, self.b = first, a, b

    def __getitem__(self, index):
        return jnp.where(self.first, self.a[index], self.b[index])


def is_odd(axis):
    return lax.axis_index(axis) % 2 == 1


def sides(axis, a, b):
    odd = is_odd(axis)
    return Pick(odd, a, b), Pick(odd, b, a)


def put(odd, outs, index, up, down):
    outs[0][index] = jnp.where(odd, up, down)
    outs[1][index] = jnp.where(odd, down, up)


def put_rows(odd, outs, slot, flat, up, down):
    rows = [flat[pl.ds(start, NX, stride=NY), :].astype(f32) for start in (up, down)]
    put(odd, outs, (pl.ds(slot * NX, NX), slice(None)), *rows)


def put_pops(adj, x_outs, y_outs):
    odd_x, odd_y = is_odd("pipe"), is_odd("cross")
    flat = adj.reshape(19 * NX * NY, NZ)
    for k in range(5):
        put(odd_x, x_outs, k, adj[x_plus[k], 0], adj[x_minus[k], NX - 1])
        put_rows(odd_y, y_outs, k, flat, y_plus[k] * NX * NY, y_minus[k] * NX * NY + NY - 1)


def fetch(pairs, sem):
    copies = [pltpu.make_async_copy(a, b, sem.at[k]) for k, (a, b) in enumerate(pairs)]
    for copy in copies:
        copy.start()
    return copies


def along(x, y):
    return [i for i in range(19) if lattice_vel[i][:2] == (x, y)]


def corner_rows(adj, fluid, speed, side, sign):
    x, step = ((0, 1), (NX - 1, -1))[side]
    y = 0 if sign > 0 else NY - 1
    flat = adj.reshape(19 * NX * NY, NZ)
    rows = [flat[pl.ds(x * NY + y, 19, stride=NX * NY), :]]
    rows += [speed[d][y : y + 1, :] for d in range(3)]

    def row(ref, lead, a, b):
        return ref[lead + (a, pl.ds(b, 1), slice(None))].astype(f32)

    rows += [row(adj, (p,), x + step, y) for p in along(step, 0)]
    rows += [row(adj, (p,), x, y + sign) for p in along(0, sign)]
    (diagonal,) = along(step, sign)
    rows += [row(adj, (diagonal,), x + step, y + sign), row(adj, (diagonal,), x, y + sign)]
    return rows + [row(fluid, (), x, y + sign), row(fluid, (), x + step, y + sign), row(fluid, (), x + step, y)]


def pack_kernel(adj_hbm, *refs):
    hbm, pops_hbm, (xa, xb, ya, yb) = refs[:FIELDS], refs[FIELDS], refs[FIELDS + 1 : FIELDS + 5]
    adj, *fields = refs[FIELDS + 5 : -2]
    pops, sem = refs[-2:]
    pairs = [(adj_hbm, adj), *zip(hbm, fields)]
    pairs += [(pops_hbm.at[:, x], pops.at[:, k]) for k, x in enumerate((0, NX - 1))]
    for copy in fetch(pairs, sem):
        copy.wait()
    put_pops(adj, (xa, xb), (ya, yb))
    odd_x, odd_y = is_odd("pipe"), is_odd("cross")
    for k in range(FIELDS):
        put(odd_x, (xa, xb), 5 + k, fields[k][0].astype(f32), fields[k][NX - 1].astype(f32))
        put_rows(odd_y, (ya, yb), 5 + k, fields[k].reshape(NX * NY, NZ), 0, NY - 1)
    fluid = fields[2]
    for side in range(2):
        speed = velocity([pops[i, side] for i in range(19)])
        at = (5 + FIELDS) * NX + side * EXTRA
        for up, down in zip(*[corner_rows(adj, fluid, speed, side, sign) for sign in (1, -1)]):
            put(odd_y, (ya, yb), (pl.ds(at, up.shape[0]), slice(None)), up, down)
            at += up.shape[0]
    flats = [ref.reshape(X_PLANES * NY, NZ) for ref in (xa, xb)]
    for e, sign in enumerate((1, -1)):
        y = NY - 1 if sign > 0 else 0
        both = []
        for x, step in ((0, 1), (NX - 1, -1)):
            rows = [adj[p, x, pl.ds(y, 1), :] for p in along(0, -sign)]
            rows += [adj[p, x + step, pl.ds(y, 1), :] for p in along(step, -sign)]
            both.append(rows + [fluid[x + step, pl.ds(y, 1), :].astype(f32)])
        for k, (up, down) in enumerate(zip(*both)):
            put(odd_x, flats, (pl.ds(corner_at(e) + EXTRA + k, 1), slice(None)), up, down)


X_PLANES = 5 + FIELDS + 2 + 10


def corner_at(e):
    return (5 + FIELDS + 2 + 5 * e) * NY


def pack(adjoint, fields, pops):
    face, side = ((X_PLANES, NY, NZ), f32), (((5 + FIELDS) * NX + 2 * EXTRA, NZ), f32)
    scratch = [pltpu.VMEM((19, NX, NY, NZ), f32)]
    scratch += [pltpu.VMEM((NX, NY, NZ), field.dtype) for field in fields]
    scratch.append(pltpu.VMEM((19, 2, NY, NZ), f32))
    scratch.append(pltpu.SemaphoreType.DMA((3 + FIELDS,)))
    return whole_call(pack_kernel, "pack", [face, face, side, side], (adjoint, *fields, pops), scratch, in_hbm=True)


edge_plus = (7, 9)
edge_minus = (10, 8)


def pack_edges_kernel(xa, xb, ya, yb, _, xa_out, xb_out):
    planes = 5 + FIELDS
    for k in [*range(planes), *range(planes + 2, X_PLANES)]:
        xa_out[k] = xa[k]
        xb_out[k] = xb[k]
    low, high = sides("cross", ya, yb)
    odd = is_odd("pipe")
    flats = [ref.reshape(X_PLANES * NY, NZ) for ref in (xa_out, xb_out)]
    for e, (rows, pops) in enumerate(((high, y_plus), (low, y_minus))):
        xa_out[planes + e] = jnp.zeros((NY, NZ), f32)
        xb_out[planes + e] = jnp.zeros((NY, NZ), f32)
        starts = [(pops.index(edge_plus[e]), pops.index(edge_minus[e]))] + [(5 + k, 5 + k) for k in range(FIELDS)]
        for r, (up, down) in enumerate(starts):
            up_row = rows[pl.ds(up * NX, 1), :]
            down_row = rows[pl.ds(down * NX + NX - 1, 1), :]
            put(odd, (xa_out, xb_out), (planes + e, pl.ds(r, 1), slice(None)), up_row, down_row)
        up, down = [rows[pl.ds(planes * NX + side * EXTRA, EXTRA), :] for side in range(2)]
        put(odd, flats, (pl.ds(corner_at(e), EXTRA), slice(None)), up, down)


def pack_edges(x_pair, y_halo, after):
    out = ((X_PLANES, NY, NZ), f32)
    return whole_call(pack_edges_kernel, "pack_edges", [out, out], (*x_pair, *y_halo, after))


def fill_sides(pad, lead, y_low, low_slot, y_high, high_slot):
    for x in range(NX):
        pad[lead + (x + 1, pl.ds(LOW - 1, 1), slice(None))] = y_low[pl.ds(low_slot * NX + x, 1), :]
        pad[lead + (x + 1, pl.ds(LOW + NY, 1), slice(None))] = y_high[pl.ds(high_slot * NX + x, 1), :]


def fill_pops(pad, adj, planes, y_low, y_high):
    for p in range(19):
        for x in planes:
            pad[p, x + 1, pl.ds(LOW, NY), :] = adj[p, x]
    for k in range(5):
        for x in planes:
            pad[y_minus[k], x + 1, pl.ds(LOW - 1, 1), :] = y_low[pl.ds(k * NX + x, 1), :]
            pad[y_plus[k], x + 1, pl.ds(LOW + NY, 1), :] = y_high[pl.ds(k * NX + x, 1), :]


def fill_pops_outer(pad, x_low, x_high, edge):
    for k in range(5):
        pad[x_minus[k], 0, pl.ds(LOW, NY), :] = x_low[k]
        pad[x_plus[k], WX - 1, pl.ds(LOW, NY), :] = x_high[k]
    for e, row in enumerate((LOW + NY, LOW - 1)):
        pad[edge_minus[e], 0, pl.ds(row, 1), :] = edge(0, e)
        pad[edge_plus[e], WX - 1, pl.ds(row, 1), :] = edge(1, e)


def edge_of(edges):
    return lambda side, e: edges[pl.ds(2 * side + e, 1), :]


def fill_field(pad, lead, own, slot, y_low, y_high):
    for x in range(NX):
        pad[lead + (x + 1, pl.ds(LOW, NY), slice(None))] = own[x].astype(f32)
    fill_sides(pad, lead, y_low, 5 + slot, y_high, 5 + slot)


def fill_field_outer(pad, lead, slot, x_low, x_high):
    for x, face in ((0, x_low), (WX - 1, x_high)):
        pad[lead + (x, pl.ds(LOW, NY), slice(None))] = face[5 + slot]
        for e, row in enumerate((LOW + NY, LOW - 1)):
            pad[lead + (x, pl.ds(row, 1), slice(None))] = face[5 + FIELDS + e, pl.ds(1 + slot, 1), :]


def propagate_back(adj_pad, fluid_pad, x, low=LOW):
    here = tile(fluid_pad, (), x, (0, 0, 0), low)
    post = [here * adj_pad[0, x + 1, pl.ds(low, NY), :]]
    for i in range(1, 19):
        ahead = tile(fluid_pad, (), x, lattice_vel[i], low)
        moved = tile(adj_pad, (i,), x, lattice_vel[i], low)
        back = adj_pad[opposite[i], x + 1, pl.ds(low, NY), :]
        post.append(here * jnp.where(ahead != 0.0, moved, back))
    return post


def step_plane(x, adj_pad, fluid_pad, speed, phase, adj_out, mom_out, at=0):
    post = propagate_back(adj_pad, fluid_pad, x)
    q = moments(post)

    def store(i, value):
        adj_out[i, x - at] = value

    collide_back(post, q, [speed[d, x] for d in range(3)], phase[x], store)
    if mom_out is not None:
        mom_out[0, x] = q[0]
        for k in range(6):
            mom_out[1 + k, x] = q[2][k]


inner = range(1, NX - 1)


def second_inner_kernel(speed, phase, adj, fluid, ya, yb, adj_out, mom_out, adj_pad, fluid_pad):
    y_low, y_high = sides("cross", ya, yb)
    fill_field(fluid_pad, (), fluid, 2, y_low, y_high)
    fill_pops(adj_pad, adj, range(NX), y_low, y_high)

    def plane(x, carry):
        step_plane(x, adj_pad, fluid_pad, speed, phase, adj_out, mom_out)
        return carry

    lax.fori_loop(1, NX - 1, plane, 0, unroll=7)


block = ((19, NX, NY, NZ), f32)
seven = ((7, NX, NY, NZ), f32)
vector = ((3, NX, NY, NZ), f32)


def pad_scratch():
    return [pltpu.VMEM((19, WX, ROWS, NZ), f32), pltpu.VMEM((WX, ROWS, NZ), f32)]


def corner_edges(adj, fluid, y_sides, x_sides, edges_out, corner_pad, corner_fluid):
    base = (5 + FIELDS) * NX
    for side, face in enumerate(x_sides):
        sx = (-1, 1)[side]
        x = (0, NX - 1)[side]
        near, far = 1 - sx, 1 + sx
        pad, wet = corner_pad.at[side], corner_fluid.at[side]
        flat = Pick(face.first, *[ref.reshape(X_PLANES * NY, NZ) for ref in (face.a, face.b)])
        for e, (rows, sy) in enumerate(zip(y_sides, (1, -1))):
            at = LOW + NY if sy > 0 else LOW - 1
            inner_y = NY - 1 if sy > 0 else 0
            first = corner_at(e)

            def got(r):
                return flat[pl.ds(first + r, 1), :]

            def beside(r):
                return rows[pl.ds(base + side * EXTRA + r, 1), :]

            def set_pops(pops, plane, row, values):
                for p, value in zip(pops, values):
                    pad[p, plane, pl.ds(row, 1), :] = value

            set_pops(range(19), 1, at, [got(r) for r in range(19)])
            set_pops(along(sx, 0), far, at, [got(22 + r) for r in range(3)])
            set_pops(along(0, sy), 1, at + sy, [got(25 + r) for r in range(3)])
            set_pops(along(sx, sy), far, at + sy, [got(28)])
            set_pops(along(-sx, 0), near, at, [beside(p) for p in along(-sx, 0)])
            set_pops(along(-sx, sy), near, at + sy, [beside(29)])
            set_pops(along(0, -sy), 1, at - sy, [got(EXTRA + r) for r in range(3)])
            set_pops(along(sx, -sy), far, at - sy, [got(EXTRA + 3)])
            set_pops(along(-sx, -sy), near, at - sy, [adj[p, x, pl.ds(inner_y, 1), :] for p in along(-sx, -sy)])
            for plane, row, value in (
                (1, at, face[5 + FIELDS + e, pl.ds(3, 1), :]),
                (far, at, got(32)),
                (1, at + sy, got(30)),
                (far, at + sy, got(31)),
                (near, at, rows[pl.ds((5 + 2) * NX + x, 1), :]),
                (near, at + sy, beside(30)),
                (1, at - sy, face[5 + 2, pl.ds(inner_y, 1), :]),
                (far, at - sy, got(EXTRA + 4)),
                (near, at - sy, fluid[x, pl.ds(inner_y, 1), :].astype(f32)),
            ):
                wet[plane, pl.ds(row, 1), :] = value
            low = LOW + 1 if sy > 0 else LOW - 1
            post = propagate_back(pad, wet, 0, low)
            u = [jnp.broadcast_to(got(19 + d), (NY, NZ)) for d in range(3)]
            phase = jnp.broadcast_to(face[5 + FIELDS + e, pl.ds(2, 1), :], (NY, NZ))
            kept = {}
            collide_back(post, moments(post), u, phase, kept.__setitem__)
            (crossing,) = along(sx, sy)
            edges_out[pl.ds(2 * side + e, 1), :] = kept[crossing][at - low : at - low + 1, :]
    edges_out[pl.ds(4, 4), :] = jnp.zeros((4, NZ), f32)


def second_outer_kernel(
    speed, phase, adj, fluid, ya, yb, xa, xb, adj_in, mom_in, _,
    adj_out, mom_out, xa_out, xb_out, ya_out, yb_out, edges_out,
    adj_pad, fluid_pad, corner_pad, corner_fluid,
):
    (x_low, x_high), (y_low, y_high) = sides("pipe", xa, xb), sides("cross", ya, yb)
    fill_field(fluid_pad, (), fluid, 2, y_low, y_high)
    fill_field_outer(fluid_pad, (), 2, x_low, x_high)
    fill_pops(adj_pad, adj, (0, 1, NX - 2, NX - 1), y_low, y_high)
    faces = (x_low, x_high)
    fill_pops_outer(adj_pad, x_low, x_high, lambda side, e: faces[side][5 + FIELDS + e, pl.ds(0, 1), :])
    for x in (0, NX - 1):
        step_plane(x, adj_pad, fluid_pad, speed, phase, adj_out, mom_out)
    put_pops(adj_out, (xa_out, xb_out), (ya_out, yb_out))
    corner_edges(adj, fluid, (y_high, y_low), faces, edges_out, corner_pad, corner_fluid)


def one_hots(index, row, hit_out, right_out, at):
    row_iota = lax.broadcasted_iota(jnp.int32, (64, NZ), 0)
    key = (lax.shift_right_logical(index, 6) & 1) * 32 + lax.shift_right_logical(index, 7)
    low = index & 63
    hit = jnp.where(row_iota == key[row : row + 1, :], 1.0, 0.0)
    hit_out[:, pl.ds(at, NZ)] = hit.astype(jnp.bfloat16)
    right = jnp.where(row_iota == low[row : row + 1, :], 1.0, 0.0)
    right_out[:, pl.ds(at, NZ)] = right.astype(jnp.bfloat16)


OWN = NX * NY * NZ
SIDES = 2 * NX * NZ
FACES = (2 * NY + 4) * NZ


def store_velocity(pops, out):
    def plane(x, carry):
        u = velocity([pops[i, x] for i in range(19)])
        for d in range(3):
            out[d, x] = u[d]
        return carry

    lax.fori_loop(0, NX, plane, 0, unroll=4)


def own_kernel(
    table_hbm, phase_a_hbm, phase_b_hbm, fluid_hbm, wall_hbm, patch_hbm, pops_hbm,
    phi_out, hit_out, right_out, wall_out, speed_out,
    table, phase_a, phase_b, fluid, wall, patch, pops, sem,
):
    hbm = (table_hbm, phase_a_hbm, phase_b_hbm, fluid_hbm, wall_hbm, patch_hbm, pops_hbm)
    copies = fetch(zip(hbm, (table, phase_a, phase_b, fluid, wall, patch, pops)), sem)
    for copy in copies[:-1]:
        copy.wait()

    def plane(x, carry):
        index = patch[x] & 4095
        wall_out[x] = wall[x].astype(f32)
        contact = wall[x].astype(f32) * look_up(table, index)
        wet = fluid[x].astype(f32)
        phi_out[0, x] = wet * phase_a[x] + contact
        phi_out[1, x] = wet * phase_b[x] + contact
        for r in range(NY):
            one_hots(index, r, hit_out, right_out, pl.multiple_of((x * NY + r) * NZ, NZ))
        return carry

    lax.fori_loop(0, NX, plane, 0, unroll=4)
    copies[-1].wait()
    store_velocity(pops, speed_out)


def imposed(table, slot):
    index = slot(4).astype(jnp.int32) & 4095
    contact = slot(3) * look_up(table, index)
    return index, [slot(2) * slot(t) + contact for t in range(2)]


def side_kernel(table, ya, yb, phi_out, wall_out, hit_out, right_out):
    for side, rows in enumerate(sides("cross", ya, yb)):
        index, values = imposed(table, lambda k: rows[pl.ds((5 + k) * NX, NX), :])
        wall_out[side] = rows[pl.ds(8 * NX, NX), :]
        for t in range(2):
            phi_out[side, t] = values[t]
        for x in range(NX):
            one_hots(index, x, hit_out, right_out, (side * NX + x) * NZ)


def middle_kernel(
    phi, table, fluid, mom, ya, yb, xa, xb, phi_side, wall_beside,
    dgrad_out, grad_out, fluid_out, wall_face, wall_side, hit_out, right_out,
    phi_pad,
):
    (x_low, x_high), (y_low, y_high) = sides("pipe", xa, xb), sides("cross", ya, yb)
    fill_field(fluid_out, (), fluid, 2, y_low, y_high)
    fill_field_outer(fluid_out, (), 2, x_low, x_high)
    for x in range(NX):
        for t in range(2):
            phi_pad[t, x + 1, pl.ds(LOW, NY), :] = phi[t, x]
            for side, y in enumerate((LOW - 1, LOW + NY)):
                phi_pad[t, x + 1, pl.ds(y, 1), :] = phi_side[side, t, pl.ds(x, 1), :]
    for side, (face, x) in enumerate(((x_low, 0), (x_high, WX - 1))):
        index, values = imposed(table, lambda k: face[5 + k])
        wall_face[side] = face[8]
        wall_side[side, pl.ds(1, NX), :] = wall_beside[side]
        for t in range(2):
            phi_pad[t, x, pl.ds(LOW, NY), :] = values[t]
        for r in range(NY):
            one_hots(index, r, hit_out, right_out, (side * NY + r) * NZ)

    def corner_tile(k):
        rows = [face[5 + FIELDS + 1 - e, pl.ds(1 + k, 1), :] for e in range(2) for face in (x_low, x_high)]
        return jnp.concatenate(rows + rows, axis=0)

    index, values = imposed(table, corner_tile)
    on_wall = corner_tile(3)
    for r in range(4):
        side, x, y = r // 2, (WX - 1) * (r % 2), (LOW - 1, LOW + NY)[r // 2]
        wall_side[side, pl.ds(x, 1), :] = on_wall[r : r + 1, :]
        for t in range(2):
            phi_pad[t, x, pl.ds(y, 1), :] = values[t][r : r + 1, :]
        one_hots(index, r, hit_out, right_out, (2 * NY + r) * NZ)

    def plane(x, carry):
        def view(t):
            return lambda a, b: tile(phi_pad, (t,), x, (a, b, 0))

        first, n = gradient(view(0)), gradient(view(1))
        for d in range(3):
            grad_out[d, x] = first[d]
        dgrad = gradient_back(mom[0, x], [mom[1 + k, x] for k in range(6)], n)
        for d in range(3):
            dgrad_out[d, x] = dgrad[d]
        return carry

    lax.fori_loop(0, NX, plane, 0, unroll=4)


def speed_kernel(pops_hbm, _, out, pops, sem):
    for copy in fetch([(pops_hbm, pops)], sem):
        copy.wait()
    store_velocity(pops, out)


def own_terms(*args):
    hots = ((64, OWN), jnp.bfloat16)
    scratch = [pltpu.VMEM(arg.shape, arg.dtype) for arg in args] + [pltpu.SemaphoreType.DMA((len(args),))]
    shapes = [((2, NX, NY, NZ), f32), hots, hots, ((NX, NY, NZ), f32), vector]
    return whole_call(own_kernel, "own_terms", shapes, args, scratch, specs=[pl.BlockSpec(memory_space=pl.ANY)] * len(args))


def side_terms(*args):
    shapes = [((2, 2, NX, NZ), f32), ((2, NX, NZ), f32)] + [((64, SIDES), jnp.bfloat16)] * 2
    return whole_call(side_kernel, "side_terms", shapes, args)


def middle(*args):
    shapes = [vector, vector, ((WX, ROWS, NZ), f32), ((2, NY, NZ), f32), ((2, WX, NZ), f32)]
    shapes += [((64, FACES), jnp.bfloat16)] * 2
    return whole_call(middle_kernel, "middle", shapes, args, [pltpu.VMEM((2, WX, ROWS, NZ), f32)])


def first_speed(pops, after):
    scratch = [pltpu.VMEM((19, NX, NY, NZ), f32), pltpu.SemaphoreType.DMA((1,))]
    specs = [pl.BlockSpec(memory_space=pl.ANY)] * 2
    return whole_call(speed_kernel, "first_speed", [vector], (pops, after), scratch, specs=specs)[0]


def weighted(hit, values):
    bigs, smalls = [], []
    for value in values:
        big = value.astype(jnp.bfloat16).astype(f32)
        for r in range(value.shape[0]):
            for rows, source in ((bigs, big), (smalls, value - big)):
                row = jnp.broadcast_to(source[r : r + 1, :], (16, NZ)).astype(jnp.bfloat16)
                rows.append(jnp.concatenate([row] * 4, axis=0))
    return jnp.concatenate(
        [hit * jnp.concatenate(bigs, axis=1), hit * jnp.concatenate(smalls, axis=1)], axis=0
    )


def table_sum(left, right):
    return lax.dot_general(left, right, (((1,), (1,)), ((), ())), preferred_element_type=f32)


def gradient_plane(x, adj_pad, fluid_pad, grad, dgrad_in, out):
    q0, _, q2 = moments(propagate_back(adj_pad, fluid_pad, x))
    dgrad = gradient_back(q0, q2, [grad[d, x] for d in range(3)])
    for d in range(3):
        out(d, x, dgrad[d] + dgrad_in[d, x])


def plane_adjoint(pad, x):
    return gradient_adjoint(lambda d, a, b: pad[d, x + 1 + a, pl.ds(LOW + b, NY), :])


GROUP = 4


def own_group(start, dgrad_pad, wall, hits, rights):
    values = [plane_adjoint(dgrad_pad, start + k + 1) * wall[start + k] for k in range(GROUP)]
    nodes = pl.ds(pl.multiple_of(start * NY * NZ, NY * NZ), GROUP * NY * NZ)
    return table_sum(weighted(hits[:, nodes], values), rights[:, nodes])


def first_inner_kernel(
    adj, fluid_pad, grad, dgrad_in, ya, yb, wall, hits, rights,
    dgrad_out, acc_out,
    adj_pad, dgrad_pad,
):
    y_low, y_high = sides("cross", ya, yb)
    fill_pops(adj_pad, adj, range(NX), y_low, y_high)
    dgrad_pad[...] = jnp.zeros_like(dgrad_pad)

    def out(d, x, value):
        dgrad_out[d, x] = value
        dgrad_pad[d, x + 2, pl.ds(LOW, NY), :] = value

    def plane(x, carry):
        gradient_plane(x, adj_pad, fluid_pad, grad, dgrad_in, out)
        return carry

    lax.fori_loop(1, NX - 1, plane, 0, unroll=7)
    acc_out[...] = jnp.zeros_like(acc_out)

    def group(g, carry):
        acc_out[...] += own_group(2 + g * GROUP, dgrad_pad, wall, hits, rights)
        return carry

    lax.fori_loop(0, (NX - 4) // GROUP, group, 0)


def first_outer_kernel(
    adj, fluid_pad, grad, dgrad_in, ya, yb, xa, xb, edges, dgrad_inner, acc_in,
    wall, hits, rights, wall_face, wall_side, face_hits, face_rights, side_hits, side_rights,
    total_out,
    adj_pad, dgrad_pad, rows,
):
    (x_low, x_high), (y_low, y_high) = sides("pipe", xa, xb), sides("cross", ya, yb)
    fill_pops(adj_pad, adj, (0, 1, NX - 2, NX - 1), y_low, y_high)
    fill_pops_outer(adj_pad, x_low, x_high, edge_of(edges))
    for d in range(3):
        for x in (0, 1, 2, 3, NX, NX + 1, NX + 2, NX + 3):
            dgrad_pad[d, x] = jnp.zeros((ROWS, NZ), f32)

    def out(d, x, value):
        dgrad_pad[d, x + 2, pl.ds(LOW, NY), :] = value

    for x in (0, NX - 1):
        gradient_plane(x, adj_pad, fluid_pad, grad, dgrad_in, out)
    for x in inner:
        for d in range(3):
            out(d, x, dgrad_inner[d, x])
    values = [plane_adjoint(dgrad_pad, x + 1) * wall[x] for x in (0, 1, NX - 2, NX - 1)]
    total = acc_in[...]
    for k, start in enumerate((0, NX - 2)):
        nodes = pl.ds(start * NY * NZ, 2 * NY * NZ)
        total = total + table_sum(weighted(hits[:, nodes], values[2 * k : 2 * k + 2]), rights[:, nodes])
    values = [plane_adjoint(dgrad_pad, x) * wall_face[k] for k, x in enumerate((0, WX - 1))]
    flat = dgrad_pad.reshape(3 * (WX + 2) * ROWS, NZ)
    beside, corners = [], []
    for side, (row, sign) in enumerate(((LOW, 1.0), (LOW + NY - 1, -1.0))):
        for d in range(3):
            rows[d] = flat[pl.ds(d * (WX + 2) * ROWS + row, WX + 2, stride=ROWS), :]
        value = side_adjoint(rows, sign) * wall_side[side]
        beside.append(value[1 : WX - 1])
        corners += [value[:1], value[WX - 1 :]]
    values.append(jnp.concatenate(corners, axis=0))
    total = total + table_sum(weighted(face_hits[...], values), face_rights[...])
    total = total + table_sum(weighted(side_hits[...], beside), side_rights[...])
    both = total[:64] + total[64:]
    total_out[...] = jnp.concatenate([both[:32], both[32:]], axis=1)


shares = ((0, 6), (6, 5), (11, 5))


def first_adjoint_kernel(
    start, count, speed, phase, adj, fluid_pad, ya, yb, xa, xb, edges, *refs
):
    out, adj_pad, part, sem = refs[-4:]
    (x_low, x_high), (y_low, y_high) = sides("pipe", xa, xb), sides("cross", ya, yb)
    planes = range(max(start - 1, 0), min(start + count + 1, NX))
    fill_pops(adj_pad, adj, planes, y_low, y_high)
    if start == 0 or start + count == NX:
        fill_pops_outer(adj_pad, x_low, x_high, edge_of(edges))

    def plane(k, carry):
        step_plane(start + k, adj_pad, fluid_pad, speed, phase, part, None, start)
        return carry

    lax.fori_loop(0, count, plane, 0)
    (copy,) = fetch([(part, out.at[:, pl.ds(start, count)])], sem)
    copy.wait()


def first_adjoint(start, count, args, after, before):
    args = (*args, after) if before is None else (*args, after, before)
    specs = [pl.BlockSpec(memory_space=pltpu.VMEM)] * 9 + [pl.BlockSpec(memory_space=pl.ANY)] * (len(args) - 9)
    return pl.pallas_call(
        functools.partial(first_adjoint_kernel, start, count),
        out_shape=jax.ShapeDtypeStruct(*block),
        in_specs=specs,
        out_specs=pl.BlockSpec(memory_space=pl.ANY),
        scratch_shapes=[
            pltpu.VMEM((19, WX, ROWS, NZ), f32),
            pltpu.VMEM((19, count, NY, NZ), f32),
            pltpu.SemaphoreType.DMA((1,)),
        ],
        input_output_aliases={} if before is None else {10: 0},
        compiler_params=pltpu.CompilerParams(vmem_limit_bytes=24 * 1024 * 1024),
        name="first_adjoint",
    )(*args)


def swap(axis, a, b):
    count = lax.axis_size(axis)
    near = lax.ppermute(a, axis, [(i, i ^ 1) for i in range(count)])
    far = lax.ppermute(b, axis, [(i, (i + 2 * (i % 2) - 1) % count) for i in range(count)])
    return near, far


def mirror(index, low, size):
    digit = index // low % size
    return index + (size - 1 - 2 * digit) * low


def sum_rounds():
    return (
        (lambda p, c: (p ^ 1, c),),
        (
            lambda p, c: (p ^ 3, c),
            lambda p, c: (mirror(p, 2, 4) ^ 1, c),
            lambda p, c: (mirror(p, 2, 4) ^ 3, c),
        ),
        (
            lambda p, c: (p ^ 1, c ^ 1),
            lambda p, c: (p ^ 1, mirror(c, 1, 4)),
            lambda p, c: (p ^ 1, mirror(c, 1, 4) ^ 1),
        ),
        (
            lambda p, c: (p ^ 1, c ^ 4),
            lambda p, c: (p ^ 1, mirror(c, 4, 4)),
            lambda p, c: (p ^ 1, mirror(c, 4, 4) ^ 4),
        ),
    )


def exchange(value, place):
    pipe, cross = lax.axis_size("pipe"), lax.axis_size("cross")
    pairs = []
    for p in range(pipe):
        for c in range(cross):
            q, d = place(p, c)
            pairs.append((p * cross + c, q * cross + d))
    return lax.ppermute(value, ("pipe", "cross"), pairs)


def pack_pairs(packed):
    return packed[:2], packed[2:]


def shards(
    pops_first,
    pops_second,
    phase_first,
    phase_second,
    adjoint_last,
    wettability,
    fluid,
    wall,
    patch,
):
    table = wettability.reshape(32, NZ)
    fields = (phase_first, phase_second, fluid, wall, patch)
    x_swap, y_swap = pack_pairs(pack(adjoint_last, fields, pops_second))
    y_halo = swap("cross", *y_swap)
    phi, hits, rights, wall_own, speed = own_terms(table, *fields, pops_second)
    x_halo = swap("pipe", *pack_edges(x_swap, y_halo, phi))
    phi_side, wall_beside, side_hits, side_rights = side_terms(table, *y_halo)
    given = (speed, phase_second, adjoint_last, fluid, *y_halo)
    adjoint, mom = whole_call(
        second_inner_kernel, "second_inner", [block, seven], given, pad_scratch()
    )
    face, side = ((5, NY, NZ), f32), ((5 * NX, NZ), f32)
    adjoint, mom, *packed, edges = whole_call(
        second_outer_kernel,
        "second_outer",
        [block, seven, face, face, side, side, ((8, NZ), f32)],
        given + x_halo + (adjoint, mom, phi_side),
        pad_scratch() + [pltpu.VMEM((2, 19, 3, ROWS, NZ), f32), pltpu.VMEM((2, 3, ROWS, NZ), f32)],
        {8: 0, 9: 1},
    )
    x_swap, y_swap = pack_pairs(packed)
    y_halo2, x_halo2 = swap("cross", *y_swap), swap("pipe", *x_swap)
    dgrad, grad, fluid_pad, wall_face, wall_side, face_hits, face_rights = middle(
        phi, table, fluid, mom, *y_halo, *x_halo, phi_side, wall_beside
    )
    given = (adjoint, fluid_pad, grad, dgrad, *y_halo2)
    nodes = (wall_own, hits, rights)
    adj_scratch = pad_scratch()[:1]
    dgrad_scratch = adj_scratch + [pltpu.VMEM((3, WX + 2, ROWS, NZ), f32)]
    dgrad_inner, acc = whole_call(
        first_inner_kernel, "first_inner", [vector, ((128, 64), f32)], given + nodes, dgrad_scratch
    )
    (total,) = whole_call(
        first_outer_kernel,
        "first_outer",
        [((32, NZ), f32)],
        given + x_halo2 + (edges, dgrad_inner, acc) + nodes + (wall_face, wall_side, face_hits, face_rights, side_hits, side_rights),
        dgrad_scratch + [pltpu.VMEM((3, WX + 2, NZ), f32)],
    )
    args = (first_speed(pops_first, total), phase_first, adjoint, fluid_pad, *y_halo2, *x_halo2, edges)
    result = None
    for k, places in enumerate(sum_rounds()):
        got = [exchange(total, place) for place in places]
        if k:
            result = first_adjoint(*shares[k - 1], args, total, result)
            *got, result = lax.optimization_barrier((*got, result))
        for part in got:
            total = total + part
    return result, total.reshape(wettability.shape)


def solution(mesh):
    return jax.shard_map(
        shards,
        mesh=mesh,
        in_specs=(
            P(None, "pipe", "cross", None),
            P(None, "pipe", "cross", None),
            P("pipe", "cross", None),
            P("pipe", "cross", None),
            P(None, "pipe", "cross", None),
            P(),
            P("pipe", "cross", None),
            P("pipe", "cross", None),
            P("pipe", "cross", None),
        ),
        out_specs=(P(None, "pipe", "cross", None), P()),
        check_vma=False,
    )
```

```python
import functools

import jax
import jax.numpy as jnp
from jax import lax
from jax.experimental import pallas as pl
from jax.experimental.pallas import tpu as pltpu
from jax.sharding import PartitionSpec as P

lattice_vel = (
    (0, 0, 0),
    (1, 0, 0),
    (-1, 0, 0),
    (0, 1, 0),
    (0, -1, 0),
    (0, 0, 1),
    (0, 0, -1),
    (1, 1, 0),
    (-1, -1, 0),
    (1, -1, 0),
    (-1, 1, 0),
    (1, 0, 1),
    (-1, 0, -1),
    (1, 0, -1),
    (-1, 0, 1),
    (0, 1, 1),
    (0, -1, -1),
    (0, 1, -1),
    (0, -1, 1),
)
opposite = (0, 2, 1, 4, 3, 6, 5, 8, 7, 10, 9, 12, 11, 14, 13, 16, 15, 18, 17)
relax_heavy = 1.0
relax_light = 0.7

x_plus = (1, 7, 9, 11, 13)
x_minus = (2, 8, 10, 12, 14)
y_plus = (3, 7, 10, 15, 17)
y_minus = (4, 8, 9, 16, 18)

NX = 16
NY = 8
NZ = 128
WX = NX + 2
LOW = 8
ROWS = 24
EXTRA = 33
OWN_EXTRA = 5
FIELDS = 5
f32 = jnp.float32


def tile(ref, lead, x, move, low=LOW):
    index = lead + (x + 1 + move[0], pl.ds(low + move[1], NY), slice(None))
    value = ref[index]
    if move[2]:
        value = pltpu.roll(value, (-move[2]) % NZ, 1)
    return value


def look_up(table, index):
    high = lax.shift_right_logical(index, 7)
    low = index & 127
    result = jnp.zeros(index.shape, f32)
    for r in range(32):
        row = jnp.broadcast_to(table[pl.ds(r, 1), :], index.shape)
        picked = jnp.take_along_axis(row, low, axis=1, mode="promise_in_bounds")
        result = jnp.where(high == r, picked, result)
    return result


def roll_z(value, step):
    return pltpu.roll(value, (-step) % NZ, 1)


def gradient(view):
    sixth, twelfth = 1.0 / 6.0, 1.0 / 12.0
    east, west, north, south = view(1, 0), view(-1, 0), view(0, 1), view(0, -1)
    dx, dy = east - west, north - south
    xy = view(1, 1) - view(-1, -1)
    xmy = view(1, -1) - view(-1, 1)
    along = sixth * view(0, 0) + twelfth * (east + west + north + south)
    gx = sixth * dx + twelfth * (xy + xmy + roll_z(dx, 1) + roll_z(dx, -1))
    gy = sixth * dy + twelfth * (xy - xmy + roll_z(dy, 1) + roll_z(dy, -1))
    return gx, gy, roll_z(along, 1) - roll_z(along, -1)


def moments(q):
    a, b = 1.0 / 18.0, 1.0 / 36.0

    def pair(i):
        return q[i] + q[i + 1], q[i] - q[i + 1]

    (sx, dx), (sy, dy), (sz, dz) = pair(1), pair(3), pair(5)
    (s7, d7), (s9, d9), (s11, d11) = pair(7), pair(9), pair(11)
    (s13, d13), (s15, d15), (s17, d17) = pair(13), pair(15), pair(17)
    xy, xz, yz = s7 + s9, s11 + s13, s15 + s17
    m0 = (1.0 / 3.0) * q[0] + a * (sx + sy + sz) + b * (xy + xz + yz)
    mx = a * dx + b * (d7 + d9 + d11 + d13)
    my = a * dy + b * (d7 - d9 + d15 + d17)
    mz = a * dz + b * (d11 - d13 + d15 - d17)
    mxx = a * sx + b * (xy + xz)
    myy = a * sy + b * (xy + yz)
    mzz = a * sz + b * (xz + yz)
    return m0, (mx, my, mz), (mxx, myy, mzz, b * (s7 - s9), b * (s11 - s13), b * (s15 - s17))


def velocity(f):
    density = f[0]
    for i in range(1, 19):
        density = density + f[i]
    d = {i: f[i] - f[i + 1] for i in range(1, 19, 2)}
    inv = 1.0 / density
    ux = (d[1] + d[7] + d[9] + d[11] + d[13]) * inv
    uy = (d[3] + d[7] - d[9] + d[15] + d[17]) * inv
    uz = (d[5] + d[11] - d[13] + d[15] - d[17]) * inv
    return ux, uy, uz


def apply_second(second, v):
    mxx, myy, mzz, mxy, mxz, myz = second
    x, y, z = v
    return (
        mxx * x + mxy * y + mxz * z,
        mxy * x + myy * y + myz * z,
        mxz * x + myz * y + mzz * z,
    )


def dot3(a, b):
    return a[0] * b[0] + a[1] * b[1] + a[2] * b[2]


def collide_back(post, q, u, phase, store):
    q0, q1, q2 = q
    omega = 1.0 / (relax_heavy * (1.0 + phase) * 0.5 + relax_light * (1.0 - phase) * 0.5)
    q2u = apply_second(q2, u)
    along = q0 - 4.5 * dot3(u, q2u) + 1.5 * dot3(u, u) * q0
    base = omega * along
    bx, by, bz = [omega * (3.0 * q1[d] + 9.0 * q2u[d] - 3.0 * u[d] * q0) for d in range(3)]
    keep = 1.0 - omega
    store(0, keep * post[0] + base)
    slopes = (bx, by, bz, bx + by, bx - by, bx + bz, bx - bz, by + bz, by - bz)
    for k, slope in enumerate(slopes):
        i = 1 + 2 * k
        store(i, keep * post[i] + (base + slope))
        store(i + 1, keep * post[i + 1] + (base - slope))


def gradient_back(q0, q2, n):
    nsq = dot3(n, n)
    root = 1.0 / jnp.sqrt(1.0 + nsq)
    q2n = apply_second(q2, n)
    energy = dot3(n, q2n) - (1.0 / 3.0) * nsq * q0
    third = (4.0 / 3.0) * q0
    tail = 2.0 * energy * root * root * root
    return [root * (4.0 * q2n[d] - third * n[d]) - tail * n[d] for d in range(3)]


def gradient_adjoint(view):
    sixth, twelfth = 1.0 / 6.0, 1.0 / 12.0
    xe, xw, yn, ys = view(0, 1, 0), view(0, -1, 0), view(1, 0, 1), view(1, 0, -1)
    zc = sixth * view(2, 0, 0)
    around = view(2, 1, 0) + view(2, -1, 0) + view(2, 0, 1) + view(2, 0, -1)
    across = xe - xw + yn - ys
    flat = sixth * across + twelfth * (
        view(0, 1, 1) + view(1, 1, 1) - view(0, -1, -1) - view(1, -1, -1)
        + view(0, 1, -1) - view(1, 1, -1) - view(0, -1, 1) + view(1, -1, 1)
    )
    ahead = zc + twelfth * (across + around)
    behind = twelfth * (across - around) - zc
    return -(flat + roll_z(ahead, 1) + roll_z(behind, -1))


def side_adjoint(rows, sign):
    sixth, twelfth = 1.0 / 6.0, 1.0 / 12.0
    gx, gy, gz = [lambda move, d=d: rows[d, pl.ds(1 + move, WX), :] for d in range(3)]
    flat = sixth * sign * gy(0) + twelfth * (sign * (gy(1) + gy(-1)) + gx(1) - gx(-1))
    return -(flat + twelfth * (roll_z(sign * gy(0) + gz(0), 1) + roll_z(sign * gy(0) - gz(0), -1)))


def whole_call(kernel, name, out_shape, args, scratch=(), aliases=None, in_hbm=False, specs=None):
    options = {}
    if in_hbm:
        options["in_specs"] = [pl.BlockSpec(memory_space=pl.ANY)] * len(args)
    else:
        if specs:
            options["in_specs"] = specs
        options["compiler_params"] = pltpu.CompilerParams(vmem_limit_bytes=24 * 1024 * 1024)
    return pl.pallas_call(
        kernel,
        out_shape=[
            pltpu.VMEM(shape, kind) if in_hbm else jax.ShapeDtypeStruct(shape, kind) for shape, kind in out_shape
        ],
        scratch_shapes=scratch,
        input_output_aliases=aliases or {},
        name=name,
        **options,
    )(*args)


class Pick:
    def __init__(self, first, a, b):
        self.first, self.a, self.b = first, a, b

    def __getitem__(self, index):
        return jnp.where(self.first, self.a[index], self.b[index])


def is_odd(axis):
    return lax.axis_index(axis) % 2 == 1


def sides(axis, a, b):
    odd = is_odd(axis)
    return Pick(odd, a, b), Pick(odd, b, a)


def put(odd, outs, index, up, down):
    outs[0][index] = jnp.where(odd, up, down)
    outs[1][index] = jnp.where(odd, down, up)


def put_rows(odd, outs, slot, flat, up, down):
    rows = [flat[pl.ds(start, NX, stride=NY), :].astype(f32) for start in (up, down)]
    put(odd, outs, (pl.ds(slot * NX, NX), slice(None)), *rows)


def put_pops(adj, x_outs, y_outs):
    odd_x, odd_y = is_odd("pipe"), is_odd("cross")
    flat = adj.reshape(19 * NX * NY, NZ)
    for k in range(5):
        put(odd_x, x_outs, k, adj[x_plus[k], 0], adj[x_minus[k], NX - 1])
        put_rows(odd_y, y_outs, k, flat, y_plus[k] * NX * NY, y_minus[k] * NX * NY + NY - 1)


def fetch(pairs, sem):
    copies = [pltpu.make_async_copy(a, b, sem.at[k]) for k, (a, b) in enumerate(pairs)]
    for copy in copies:
        copy.start()
    return copies


def along(x, y):
    return [i for i in range(19) if lattice_vel[i][:2] == (x, y)]


def corner_rows(adj, fluid, speed, side, sign):
    x, step = ((0, 1), (NX - 1, -1))[side]
    y = 0 if sign > 0 else NY - 1
    flat = adj.reshape(19 * NX * NY, NZ)
    rows = [flat[pl.ds(x * NY + y, 19, stride=NX * NY), :]]
    rows += [speed[d][y : y + 1, :] for d in range(3)]

    def row(ref, lead, a, b):
        return ref[lead + (a, pl.ds(b, 1), slice(None))].astype(f32)

    rows += [row(adj, (p,), x + step, y) for p in along(step, 0)]
    rows += [row(adj, (p,), x, y + sign) for p in along(0, sign)]
    (diagonal,) = along(step, sign)
    rows += [row(adj, (diagonal,), x + step, y + sign), row(adj, (diagonal,), x, y + sign)]
    return rows + [row(fluid, (), x, y + sign), row(fluid, (), x + step, y + sign), row(fluid, (), x + step, y)]


def pack_kernel(adj_hbm, *refs):
    hbm, pops_hbm, (xa, xb, ya, yb) = refs[:FIELDS], refs[FIELDS], refs[FIELDS + 1 : FIELDS + 5]
    adj, *fields = refs[FIELDS + 5 : -2]
    pops, sem = refs[-2:]
    pairs = [(adj_hbm, adj), *zip(hbm, fields)]
    pairs += [(pops_hbm.at[:, x], pops.at[:, k]) for k, x in enumerate((0, NX - 1))]
    for copy in fetch(pairs, sem):
        copy.wait()
    put_pops(adj, (xa, xb), (ya, yb))
    odd_x, odd_y = is_odd("pipe"), is_odd("cross")
    for k in range(FIELDS):
        put(odd_x, (xa, xb), 5 + k, fields[k][0].astype(f32), fields[k][NX - 1].astype(f32))
        put_rows(odd_y, (ya, yb), 5 + k, fields[k].reshape(NX * NY, NZ), 0, NY - 1)
    fluid = fields[2]
    for side in range(2):
        speed = velocity([pops[i, side] for i in range(19)])
        at = (5 + FIELDS) * NX + side * EXTRA
        for up, down in zip(*[corner_rows(adj, fluid, speed, side, sign) for sign in (1, -1)]):
            put(odd_y, (ya, yb), (pl.ds(at, up.shape[0]), slice(None)), up, down)
            at += up.shape[0]
    flats = [ref.reshape(X_PLANES * NY, NZ) for ref in (xa, xb)]
    for e, sign in enumerate((1, -1)):
        y = NY - 1 if sign > 0 else 0
        both = []
        for x, step in ((0, 1), (NX - 1, -1)):
            rows = [adj[p, x, pl.ds(y, 1), :] for p in along(0, -sign)]
            rows += [adj[p, x + step, pl.ds(y, 1), :] for p in along(step, -sign)]
            both.append(rows + [fluid[x + step, pl.ds(y, 1), :].astype(f32)])
        for k, (up, down) in enumerate(zip(*both)):
            put(odd_x, flats, (pl.ds(corner_at(e) + EXTRA + k, 1), slice(None)), up, down)


X_PLANES = 5 + FIELDS + 2 + 10


def corner_at(e):
    return (5 + FIELDS + 2 + 5 * e) * NY


def pack(adjoint, fields, pops):
    face, side = ((X_PLANES, NY, NZ), f32), (((5 + FIELDS) * NX + 2 * EXTRA, NZ), f32)
    scratch = [pltpu.VMEM((19, NX, NY, NZ), f32)]
    scratch += [pltpu.VMEM((NX, NY, NZ), field.dtype) for field in fields]
    scratch.append(pltpu.VMEM((19, 2, NY, NZ), f32))
    scratch.append(pltpu.SemaphoreType.DMA((3 + FIELDS,)))
    return whole_call(pack_kernel, "pack", [face, face, side, side], (adjoint, *fields, pops), scratch, in_hbm=True)


edge_plus = (7, 9)
edge_minus = (10, 8)


def pack_edges_kernel(xa, xb, yb, ya, _, xa_out, xb_out):
    planes = 5 + FIELDS
    for k in [*range(planes), *range(planes + 2, X_PLANES)]:
        xa_out[k] = xa[k]
        xb_out[k] = xb[k]
    low, high = sides("cross", ya, yb)
    odd = is_odd("pipe")
    flats = [ref.reshape(X_PLANES * NY, NZ) for ref in (xa_out, xb_out)]
    for e, (rows, pops) in enumerate(((high, y_plus), (low, y_minus))):
        xa_out[planes + e] = jnp.zeros((NY, NZ), f32)
        xb_out[planes + e] = jnp.zeros((NY, NZ), f32)
        starts = [(pops.index(edge_plus[e]), pops.index(edge_minus[e]))] + [(5 + k, 5 + k) for k in range(FIELDS)]
        for r, (up, down) in enumerate(starts):
            up_row = rows[pl.ds(up * NX, 1), :]
            down_row = rows[pl.ds(down * NX + NX - 1, 1), :]
            put(odd, (xa_out, xb_out), (planes + e, pl.ds(r, 1), slice(None)), up_row, down_row)
        up, down = [rows[pl.ds(planes * NX + side * EXTRA, EXTRA), :] for side in range(2)]
        put(odd, flats, (pl.ds(corner_at(e), EXTRA), slice(None)), up, down)


def pack_edges(x_pair, y_halo, after):
    out = ((X_PLANES, NY, NZ), f32)
    return whole_call(pack_edges_kernel, "pack_edges", [out, out], (*x_pair, *y_halo[::-1], after))


def fill_sides(pad, lead, y_low, low_slot, y_high, high_slot):
    for x in range(NX):
        pad[lead + (x + 1, pl.ds(LOW - 1, 1), slice(None))] = y_low[pl.ds(low_slot * NX + x, 1), :]
        pad[lead + (x + 1, pl.ds(LOW + NY, 1), slice(None))] = y_high[pl.ds(high_slot * NX + x, 1), :]


def fill_pops(pad, adj, planes, y_low, y_high):
    for p in range(19):
        for x in planes:
            pad[p, x + 1, pl.ds(LOW, NY), :] = adj[p, x]
    for k in range(5):
        for x in planes:
            pad[y_minus[k], x + 1, pl.ds(LOW - 1, 1), :] = y_low[pl.ds(k * NX + x, 1), :]
            pad[y_plus[k], x + 1, pl.ds(LOW + NY, 1), :] = y_high[pl.ds(k * NX + x, 1), :]


def fill_pops_outer(pad, x_low, x_high, edge):
    for k in range(5):
        pad[x_minus[k], 0, pl.ds(LOW, NY), :] = x_low[k]
        pad[x_plus[k], WX - 1, pl.ds(LOW, NY), :] = x_high[k]
    for e, row in enumerate((LOW + NY, LOW - 1)):
        pad[edge_minus[e], 0, pl.ds(row, 1), :] = edge(0, e)
        pad[edge_plus[e], WX - 1, pl.ds(row, 1), :] = edge(1, e)


def edge_of(edges):
    return lambda side, e: edges[pl.ds(2 * side + e, 1), :]


def fill_field(pad, lead, own, slot, y_low, y_high):
    for x in range(NX):
        pad[lead + (x + 1, pl.ds(LOW, NY), slice(None))] = own[x].astype(f32)
    fill_sides(pad, lead, y_low, 5 + slot, y_high, 5 + slot)


def fill_field_outer(pad, lead, slot, x_low, x_high):
    for x, face in ((0, x_low), (WX - 1, x_high)):
        pad[lead + (x, pl.ds(LOW, NY), slice(None))] = face[5 + slot]
        for e, row in enumerate((LOW + NY, LOW - 1)):
            pad[lead + (x, pl.ds(row, 1), slice(None))] = face[5 + FIELDS + e, pl.ds(1 + slot, 1), :]


def propagate_back(adj_pad, fluid_pad, x, low=LOW):
    here = tile(fluid_pad, (), x, (0, 0, 0), low)
    post = [here * adj_pad[0, x + 1, pl.ds(low, NY), :]]
    for i in range(1, 19):
        ahead = tile(fluid_pad, (), x, lattice_vel[i], low)
        moved = tile(adj_pad, (i,), x, lattice_vel[i], low)
        back = adj_pad[opposite[i], x + 1, pl.ds(low, NY), :]
        post.append(here * jnp.where(ahead != 0.0, moved, back))
    return post


def step_plane(x, adj_pad, fluid_pad, speed, phase, adj_out, mom_out, at=0):
    post = propagate_back(adj_pad, fluid_pad, x)
    q = moments(post)

    def store(i, value):
        adj_out[i, x - at] = value

    collide_back(post, q, [speed[d, x] for d in range(3)], phase[x], store)
    if mom_out is not None:
        mom_out[0, x] = q[0]
        for k in range(6):
            mom_out[1 + k, x] = q[2][k]


inner = range(1, NX - 1)


def second_inner_kernel(speed, phase, adj, fluid, yb, ya, adj_out, mom_out, adj_pad, fluid_pad):
    y_low, y_high = sides("cross", ya, yb)
    fill_field(fluid_pad, (), fluid, 2, y_low, y_high)
    fill_pops(adj_pad, adj, range(NX), y_low, y_high)

    def plane(x, carry):
        step_plane(x, adj_pad, fluid_pad, speed, phase, adj_out, mom_out)
        return carry

    lax.fori_loop(1, NX - 1, plane, 0, unroll=7)


block = ((19, NX, NY, NZ), f32)
seven = ((7, NX, NY, NZ), f32)
vector = ((3, NX, NY, NZ), f32)


def pad_scratch():
    return [pltpu.VMEM((19, WX, ROWS, NZ), f32), pltpu.VMEM((WX, ROWS, NZ), f32)]


def corner_edges(adj, fluid, y_sides, x_sides, edges_out, corner_pad, corner_fluid):
    base = (5 + FIELDS) * NX
    for side, face in enumerate(x_sides):
        sx = (-1, 1)[side]
        x = (0, NX - 1)[side]
        near, far = 1 - sx, 1 + sx
        pad, wet = corner_pad.at[side], corner_fluid.at[side]
        flat = Pick(face.first, *[ref.reshape(X_PLANES * NY, NZ) for ref in (face.a, face.b)])
        for e, (rows, sy) in enumerate(zip(y_sides, (1, -1))):
            at = LOW + NY if sy > 0 else LOW - 1
            inner_y = NY - 1 if sy > 0 else 0
            first = corner_at(e)

            def got(r):
                return flat[pl.ds(first + r, 1), :]

            def beside(r):
                return rows[pl.ds(base + side * EXTRA + r, 1), :]

            def set_pops(pops, plane, row, values):
                for p, value in zip(pops, values):
                    pad[p, plane, pl.ds(row, 1), :] = value

            set_pops(range(19), 1, at, [got(r) for r in range(19)])
            set_pops(along(sx, 0), far, at, [got(22 + r) for r in range(3)])
            set_pops(along(0, sy), 1, at + sy, [got(25 + r) for r in range(3)])
            set_pops(along(sx, sy), far, at + sy, [got(28)])
            set_pops(along(-sx, 0), near, at, [beside(p) for p in along(-sx, 0)])
            set_pops(along(-sx, sy), near, at + sy, [beside(29)])
            set_pops(along(0, -sy), 1, at - sy, [got(EXTRA + r) for r in range(3)])
            set_pops(along(sx, -sy), far, at - sy, [got(EXTRA + 3)])
            set_pops(along(-sx, -sy), near, at - sy, [adj[p, x, pl.ds(inner_y, 1), :] for p in along(-sx, -sy)])
            for plane, row, value in (
                (1, at, face[5 + FIELDS + e, pl.ds(3, 1), :]),
                (far, at, got(32)),
                (1, at + sy, got(30)),
                (far, at + sy, got(31)),
                (near, at, rows[pl.ds((5 + 2) * NX + x, 1), :]),
                (near, at + sy, beside(30)),
                (1, at - sy, face[5 + 2, pl.ds(inner_y, 1), :]),
                (far, at - sy, got(EXTRA + 4)),
                (near, at - sy, fluid[x, pl.ds(inner_y, 1), :].astype(f32)),
            ):
                wet[plane, pl.ds(row, 1), :] = value
            low = LOW + 1 if sy > 0 else LOW - 1
            post = propagate_back(pad, wet, 0, low)
            u = [jnp.broadcast_to(got(19 + d), (NY, NZ)) for d in range(3)]
            phase = jnp.broadcast_to(face[5 + FIELDS + e, pl.ds(2, 1), :], (NY, NZ))
            kept = {}
            collide_back(post, moments(post), u, phase, kept.__setitem__)
            (crossing,) = along(sx, sy)
            edges_out[pl.ds(2 * side + e, 1), :] = kept[crossing][at - low : at - low + 1, :]
    edges_out[pl.ds(4, 4), :] = jnp.zeros((4, NZ), f32)


def second_outer_kernel(
    speed, phase, adj, fluid, yb, ya, xa, xb, adj_in, mom_in, _,
    adj_out, mom_out, xa_out, xb_out, ya_out, yb_out, edges_out,
    adj_pad, fluid_pad, corner_pad, corner_fluid,
):
    (x_low, x_high), (y_low, y_high) = sides("pipe", xa, xb), sides("cross", ya, yb)
    fill_field(fluid_pad, (), fluid, 2, y_low, y_high)
    fill_field_outer(fluid_pad, (), 2, x_low, x_high)
    fill_pops(adj_pad, adj, (0, 1, NX - 2, NX - 1), y_low, y_high)
    faces = (x_low, x_high)
    fill_pops_outer(adj_pad, x_low, x_high, lambda side, e: faces[side][5 + FIELDS + e, pl.ds(0, 1), :])
    for x in (0, NX - 1):
        step_plane(x, adj_pad, fluid_pad, speed, phase, adj_out, mom_out)
    put_pops(adj_out, (xa_out, xb_out), (ya_out, yb_out))
    corner_edges(adj, fluid, (y_high, y_low), faces, edges_out, corner_pad, corner_fluid)


def one_hots(index, row, hit_out, right_out, at):
    row_iota = lax.broadcasted_iota(jnp.int32, (64, NZ), 0)
    key = (lax.shift_right_logical(index, 6) & 1) * 32 + lax.shift_right_logical(index, 7)
    low = index & 63
    hit = jnp.where(row_iota == key[row : row + 1, :], 1.0, 0.0)
    hit_out[:, pl.ds(at, NZ)] = hit.astype(jnp.bfloat16)
    right = jnp.where(row_iota == low[row : row + 1, :], 1.0, 0.0)
    right_out[:, pl.ds(at, NZ)] = right.astype(jnp.bfloat16)


OWN = NX * NY * NZ
SIDES = 2 * NX * NZ
FACES = (2 * NY + 4) * NZ


def store_velocity(pops, out):
    def plane(x, carry):
        u = velocity([pops[i, x] for i in range(19)])
        for d in range(3):
            out[d, x] = u[d]
        return carry

    lax.fori_loop(0, NX, plane, 0, unroll=4)


def own_kernel(
    table_hbm, phase_a_hbm, phase_b_hbm, fluid_hbm, wall_hbm, patch_hbm, pops_hbm,
    phi_out, hit_out, right_out, wall_out, speed_out,
    table, phase_a, phase_b, fluid, wall, patch, pops, sem,
):
    hbm = (table_hbm, phase_a_hbm, phase_b_hbm, fluid_hbm, wall_hbm, patch_hbm, pops_hbm)
    copies = fetch(zip(hbm, (table, phase_a, phase_b, fluid, wall, patch, pops)), sem)
    for copy in copies[:-1]:
        copy.wait()

    def plane(x, carry):
        index = patch[x] & 4095
        wall_out[x] = wall[x].astype(f32)
        contact = wall[x].astype(f32) * look_up(table, index)
        wet = fluid[x].astype(f32)
        phi_out[0, x] = wet * phase_a[x] + contact
        phi_out[1, x] = wet * phase_b[x] + contact
        for r in range(NY):
            one_hots(index, r, hit_out, right_out, pl.multiple_of((x * NY + r) * NZ, NZ))
        return carry

    lax.fori_loop(0, NX, plane, 0, unroll=4)
    copies[-1].wait()
    store_velocity(pops, speed_out)


def imposed(table, slot):
    index = slot(4).astype(jnp.int32) & 4095
    contact = slot(3) * look_up(table, index)
    return index, [slot(2) * slot(t) + contact for t in range(2)]


def side_kernel(table, yb, ya, phi_out, wall_out, hit_out, right_out):
    for side, rows in enumerate(sides("cross", ya, yb)):
        index, values = imposed(table, lambda k: rows[pl.ds((5 + k) * NX, NX), :])
        wall_out[side] = rows[pl.ds(8 * NX, NX), :]
        for t in range(2):
            phi_out[side, t] = values[t]
        for x in range(NX):
            one_hots(index, x, hit_out, right_out, (side * NX + x) * NZ)


def middle_kernel(
    phi, table, fluid, mom, ya, yb, xa, xb, phi_side, wall_beside,
    dgrad_out, grad_out, fluid_out, wall_face, wall_side, hit_out, right_out,
    phi_pad,
):
    (x_low, x_high), (y_low, y_high) = sides("pipe", xa, xb), sides("cross", ya, yb)
    fill_field(fluid_out, (), fluid, 2, y_low, y_high)
    fill_field_outer(fluid_out, (), 2, x_low, x_high)
    for x in range(NX):
        for t in range(2):
            phi_pad[t, x + 1, pl.ds(LOW, NY), :] = phi[t, x]
            for side, y in enumerate((LOW - 1, LOW + NY)):
                phi_pad[t, x + 1, pl.ds(y, 1), :] = phi_side[side, t, pl.ds(x, 1), :]
    for side, (face, x) in enumerate(((x_low, 0), (x_high, WX - 1))):
        index, values = imposed(table, lambda k: face[5 + k])
        wall_face[side] = face[8]
        wall_side[side, pl.ds(1, NX), :] = wall_beside[side]
        for t in range(2):
            phi_pad[t, x, pl.ds(LOW, NY), :] = values[t]
        for r in range(NY):
            one_hots(index, r, hit_out, right_out, (side * NY + r) * NZ)

    def corner_tile(k):
        rows = [face[5 + FIELDS + 1 - e, pl.ds(1 + k, 1), :] for e in range(2) for face in (x_low, x_high)]
        return jnp.concatenate(rows + rows, axis=0)

    index, values = imposed(table, corner_tile)
    on_wall = corner_tile(3)
    for r in range(4):
        side, x, y = r // 2, (WX - 1) * (r % 2), (LOW - 1, LOW + NY)[r // 2]
        wall_side[side, pl.ds(x, 1), :] = on_wall[r : r + 1, :]
        for t in range(2):
            phi_pad[t, x, pl.ds(y, 1), :] = values[t][r : r + 1, :]
        one_hots(index, r, hit_out, right_out, (2 * NY + r) * NZ)

    def plane(x, carry):
        def view(t):
            return lambda a, b: tile(phi_pad, (t,), x, (a, b, 0))

        first, n = gradient(view(0)), gradient(view(1))
        for d in range(3):
            grad_out[d, x] = first[d]
        dgrad = gradient_back(mom[0, x], [mom[1 + k, x] for k in range(6)], n)
        for d in range(3):
            dgrad_out[d, x] = dgrad[d]
        return carry

    lax.fori_loop(0, NX, plane, 0, unroll=4)


def speed_kernel(pops_hbm, _, out, pops, sem):
    for copy in fetch([(pops_hbm, pops)], sem):
        copy.wait()
    store_velocity(pops, out)


def own_terms(*args):
    hots = ((64, OWN), jnp.bfloat16)
    scratch = [pltpu.VMEM(arg.shape, arg.dtype) for arg in args] + [pltpu.SemaphoreType.DMA((len(args),))]
    shapes = [((2, NX, NY, NZ), f32), hots, hots, ((NX, NY, NZ), f32), vector]
    return whole_call(own_kernel, "own_terms", shapes, args, scratch, specs=[pl.BlockSpec(memory_space=pl.ANY)] * len(args))


def side_terms(*args):
    shapes = [((2, 2, NX, NZ), f32), ((2, NX, NZ), f32)] + [((64, SIDES), jnp.bfloat16)] * 2
    return whole_call(side_kernel, "side_terms", shapes, args)


def middle(*args):
    shapes = [vector, vector, ((WX, ROWS, NZ), f32), ((2, NY, NZ), f32), ((2, WX, NZ), f32)]
    shapes += [((64, FACES), jnp.bfloat16)] * 2
    return whole_call(middle_kernel, "middle", shapes, args, [pltpu.VMEM((2, WX, ROWS, NZ), f32)])


def first_speed(pops, after):
    scratch = [pltpu.VMEM((19, NX, NY, NZ), f32), pltpu.SemaphoreType.DMA((1,))]
    specs = [pl.BlockSpec(memory_space=pl.ANY)] * 2
    return whole_call(speed_kernel, "first_speed", [vector], (pops, after), scratch, specs=specs)[0]


def weighted(hit, values):
    bigs, smalls = [], []
    for value in values:
        big = value.astype(jnp.bfloat16).astype(f32)
        for r in range(value.shape[0]):
            for rows, source in ((bigs, big), (smalls, value - big)):
                row = jnp.broadcast_to(source[r : r + 1, :], (16, NZ)).astype(jnp.bfloat16)
                rows.append(jnp.concatenate([row] * 4, axis=0))
    return jnp.concatenate(
        [hit * jnp.concatenate(bigs, axis=1), hit * jnp.concatenate(smalls, axis=1)], axis=0
    )


def table_sum(left, right):
    return lax.dot_general(left, right, (((1,), (1,)), ((), ())), preferred_element_type=f32)


def gradient_plane(x, adj_pad, fluid_pad, grad, dgrad_in, out):
    q0, _, q2 = moments(propagate_back(adj_pad, fluid_pad, x))
    dgrad = gradient_back(q0, q2, [grad[d, x] for d in range(3)])
    for d in range(3):
        out(d, x, dgrad[d] + dgrad_in[d, x])


def plane_adjoint(pad, x):
    return gradient_adjoint(lambda d, a, b: pad[d, x + 1 + a, pl.ds(LOW + b, NY), :])


GROUP = 6


def own_group(start, dgrad_pad, wall, hits, rights):
    values = [plane_adjoint(dgrad_pad, start + k + 1) * wall[start + k] for k in range(GROUP)]
    nodes = pl.ds(start * NY * NZ, GROUP * NY * NZ)
    return table_sum(weighted(hits[:, nodes], values), rights[:, nodes])


def first_inner_kernel(
    adj, fluid_pad, grad, dgrad_in, ya, yb, wall, hits, rights,
    dgrad_out, acc_out,
    adj_pad, dgrad_pad,
):
    y_low, y_high = sides("cross", ya, yb)
    fill_pops(adj_pad, adj, range(NX), y_low, y_high)
    dgrad_pad[...] = jnp.zeros_like(dgrad_pad)

    def out(d, x, value):
        dgrad_out[d, x] = value
        dgrad_pad[d, x + 2, pl.ds(LOW, NY), :] = value

    def plane(x, carry):
        gradient_plane(x, adj_pad, fluid_pad, grad, dgrad_in, out)
        return carry

    lax.fori_loop(1, NX - 1, plane, 0, unroll=7)
    total = own_group(2, dgrad_pad, wall, hits, rights)
    for start in range(2 + GROUP, NX - 2, GROUP):
        total = total + own_group(start, dgrad_pad, wall, hits, rights)
    acc_out[...] = total


def first_outer_kernel(
    adj, fluid_pad, grad, dgrad_in, ya, yb, xa, xb, edges, dgrad_inner, acc_in,
    wall, hits, rights, wall_face, wall_side, face_hits, face_rights, side_hits, side_rights,
    total_out,
    adj_pad, dgrad_pad, rows,
):
    (x_low, x_high), (y_low, y_high) = sides("pipe", xa, xb), sides("cross", ya, yb)
    fill_pops(adj_pad, adj, (0, 1, NX - 2, NX - 1), y_low, y_high)
    fill_pops_outer(adj_pad, x_low, x_high, edge_of(edges))
    for d in range(3):
        for x in (0, 1, 2, 3, NX, NX + 1, NX + 2, NX + 3):
            dgrad_pad[d, x] = jnp.zeros((ROWS, NZ), f32)

    def out(d, x, value):
        dgrad_pad[d, x + 2, pl.ds(LOW, NY), :] = value

    for x in (0, NX - 1):
        gradient_plane(x, adj_pad, fluid_pad, grad, dgrad_in, out)
    for x in inner:
        for d in range(3):
            out(d, x, dgrad_inner[d, x])
    values = [plane_adjoint(dgrad_pad, x + 1) * wall[x] for x in (0, 1, NX - 2, NX - 1)]
    total = acc_in[...]
    for k, start in enumerate((0, NX - 2)):
        nodes = pl.ds(start * NY * NZ, 2 * NY * NZ)
        total = total + table_sum(weighted(hits[:, nodes], values[2 * k : 2 * k + 2]), rights[:, nodes])
    values = [plane_adjoint(dgrad_pad, x) * wall_face[k] for k, x in enumerate((0, WX - 1))]
    flat = dgrad_pad.reshape(3 * (WX + 2) * ROWS, NZ)
    beside, corners = [], []
    for side, (row, sign) in enumerate(((LOW, 1.0), (LOW + NY - 1, -1.0))):
        for d in range(3):
            rows[d] = flat[pl.ds(d * (WX + 2) * ROWS + row, WX + 2, stride=ROWS), :]
        value = side_adjoint(rows, sign) * wall_side[side]
        beside.append(value[1 : WX - 1])
        corners += [value[:1], value[WX - 1 :]]
    values.append(jnp.concatenate(corners, axis=0))
    total = total + table_sum(weighted(face_hits[...], values), face_rights[...])
    total = total + table_sum(weighted(side_hits[...], beside), side_rights[...])
    both = total[:64] + total[64:]
    total_out[...] = jnp.concatenate([both[:32], both[32:]], axis=1)


shares = ((0, 6), (6, 5), (11, 5))


def first_adjoint_kernel(
    start, count, speed, phase, adj, fluid_pad, ya, yb, xa, xb, edges, *refs
):
    out, adj_pad, part, sem = refs[-4:]
    (x_low, x_high), (y_low, y_high) = sides("pipe", xa, xb), sides("cross", ya, yb)
    planes = range(max(start - 1, 0), min(start + count + 1, NX))
    fill_pops(adj_pad, adj, planes, y_low, y_high)
    if start == 0 or start + count == NX:
        fill_pops_outer(adj_pad, x_low, x_high, edge_of(edges))

    def plane(k, carry):
        step_plane(start + k, adj_pad, fluid_pad, speed, phase, part, None, start)
        return carry

    lax.fori_loop(0, count, plane, 0)
    (copy,) = fetch([(part, out.at[:, pl.ds(start, count)])], sem)
    copy.wait()


def first_adjoint(start, count, args, after, before):
    args = (*args, after) if before is None else (*args, after, before)
    specs = [pl.BlockSpec(memory_space=pltpu.VMEM)] * 9 + [pl.BlockSpec(memory_space=pl.ANY)] * (len(args) - 9)
    return pl.pallas_call(
        functools.partial(first_adjoint_kernel, start, count),
        out_shape=jax.ShapeDtypeStruct(*block),
        in_specs=specs,
        out_specs=pl.BlockSpec(memory_space=pl.ANY),
        scratch_shapes=[
            pltpu.VMEM((19, WX, ROWS, NZ), f32),
            pltpu.VMEM((19, count, NY, NZ), f32),
            pltpu.SemaphoreType.DMA((1,)),
        ],
        input_output_aliases={} if before is None else {10: 0},
        compiler_params=pltpu.CompilerParams(vmem_limit_bytes=24 * 1024 * 1024),
        name="first_adjoint",
    )(*args)


def swap(axis, a, b):
    count = lax.axis_size(axis)
    near = lax.ppermute(a, axis, [(i, i ^ 1) for i in range(count)])
    far = lax.ppermute(b, axis, [(i, (i + 2 * (i % 2) - 1) % count) for i in range(count)])
    return near, far


def mirror(index, low, size):
    digit = index // low % size
    return index + (size - 1 - 2 * digit) * low


def sum_rounds():
    return (
        (lambda p, c: (p ^ 1, c),),
        (
            lambda p, c: (p ^ 3, c),
            lambda p, c: (mirror(p, 2, 4) ^ 1, c),
            lambda p, c: (mirror(p, 2, 4) ^ 3, c),
        ),
        (
            lambda p, c: (p ^ 1, c ^ 1),
            lambda p, c: (p ^ 1, mirror(c, 1, 4)),
            lambda p, c: (p ^ 1, mirror(c, 1, 4) ^ 1),
        ),
        (
            lambda p, c: (p ^ 1, c ^ 4),
            lambda p, c: (p ^ 1, mirror(c, 4, 4)),
            lambda p, c: (p ^ 1, mirror(c, 4, 4) ^ 4),
        ),
    )


def exchange(value, place):
    pipe, cross = lax.axis_size("pipe"), lax.axis_size("cross")
    pairs = []
    for p in range(pipe):
        for c in range(cross):
            q, d = place(p, c)
            pairs.append((p * cross + c, q * cross + d))
    return lax.ppermute(value, ("pipe", "cross"), pairs)


def pack_pairs(packed):
    return packed[:2], packed[2:]


def shards(
    pops_first,
    pops_second,
    phase_first,
    phase_second,
    adjoint_last,
    wettability,
    fluid,
    wall,
    patch,
):
    table = wettability.reshape(32, NZ)
    fields = (phase_first, phase_second, fluid, wall, patch)
    x_swap, y_swap = pack_pairs(pack(adjoint_last, fields, pops_second))
    y_halo = swap("cross", *y_swap)
    phi, hits, rights, wall_own, speed = own_terms(table, *fields, pops_second)
    x_halo = swap("pipe", *pack_edges(x_swap, y_halo, phi))
    phi_side, wall_beside, side_hits, side_rights = side_terms(table, *y_halo[::-1])
    given = (speed, phase_second, adjoint_last, fluid, *y_halo[::-1])
    adjoint, mom = whole_call(
        second_inner_kernel, "second_inner", [block, seven], given, pad_scratch()
    )
    face, side = ((5, NY, NZ), f32), ((5 * NX, NZ), f32)
    adjoint, mom, *packed, edges = whole_call(
        second_outer_kernel,
        "second_outer",
        [block, seven, face, face, side, side, ((8, NZ), f32)],
        given + x_halo + (adjoint, mom, phi_side),
        pad_scratch() + [pltpu.VMEM((2, 19, 3, ROWS, NZ), f32), pltpu.VMEM((2, 3, ROWS, NZ), f32)],
        {8: 0, 9: 1},
    )
    x_swap, y_swap = pack_pairs(packed)
    y_halo2, x_halo2 = swap("cross", *y_swap), swap("pipe", *x_swap)
    dgrad, grad, fluid_pad, wall_face, wall_side, face_hits, face_rights = middle(
        phi, table, fluid, mom, *y_halo, *x_halo, phi_side, wall_beside
    )
    given = (adjoint, fluid_pad, grad, dgrad, *y_halo2)
    nodes = (wall_own, hits, rights)
    adj_scratch = pad_scratch()[:1]
    dgrad_scratch = adj_scratch + [pltpu.VMEM((3, WX + 2, ROWS, NZ), f32)]
    dgrad_inner, acc = whole_call(
        first_inner_kernel, "first_inner", [vector, ((128, 64), f32)], given + nodes, dgrad_scratch
    )
    (total,) = whole_call(
        first_outer_kernel,
        "first_outer",
        [((32, NZ), f32)],
        given + x_halo2 + (edges, dgrad_inner, acc) + nodes + (wall_face, wall_side, face_hits, face_rights, side_hits, side_rights),
        dgrad_scratch + [pltpu.VMEM((3, WX + 2, NZ), f32)],
    )
    args = (first_speed(pops_first, total), phase_first, adjoint, fluid_pad, *y_halo2, *x_halo2, edges)
    result = None
    for k, places in enumerate(sum_rounds()):
        got = [exchange(total, place) for place in places]
        if k:
            result = first_adjoint(*shares[k - 1], args, total, result)
            *got, result = lax.optimization_barrier((*got, result))
        for part in got:
            total = total + part
    return result, total.reshape(wettability.shape)


def solution(mesh):
    return jax.shard_map(
        shards,
        mesh=mesh,
        in_specs=(
            P(None, "pipe", "cross", None),
            P(None, "pipe", "cross", None),
            P("pipe", "cross", None),
            P("pipe", "cross", None),
            P(None, "pipe", "cross", None),
            P(),
            P("pipe", "cross", None),
            P("pipe", "cross", None),
            P("pipe", "cross", None),
        ),
        out_specs=(P(None, "pipe", "cross", None), P()),
        check_vma=False,
    )
```

```python
import functools

import jax
import jax.numpy as jnp
from jax import lax
from jax.experimental import pallas as pl
from jax.experimental.pallas import tpu as pltpu
from jax.sharding import PartitionSpec as P

lattice_vel = (
    (0, 0, 0),
    (1, 0, 0),
    (-1, 0, 0),
    (0, 1, 0),
    (0, -1, 0),
    (0, 0, 1),
    (0, 0, -1),
    (1, 1, 0),
    (-1, -1, 0),
    (1, -1, 0),
    (-1, 1, 0),
    (1, 0, 1),
    (-1, 0, -1),
    (1, 0, -1),
    (-1, 0, 1),
    (0, 1, 1),
    (0, -1, -1),
    (0, 1, -1),
    (0, -1, 1),
)
opposite = (0, 2, 1, 4, 3, 6, 5, 8, 7, 10, 9, 12, 11, 14, 13, 16, 15, 18, 17)
relax_heavy = 1.0
relax_light = 0.7

x_plus = (1, 7, 9, 11, 13)
x_minus = (2, 8, 10, 12, 14)
y_plus = (3, 7, 10, 15, 17)
y_minus = (4, 8, 9, 16, 18)

NX = 16
NY = 8
NZ = 128
WX = NX + 2
LOW = 8
ROWS = 24
EXTRA = 33
OWN_EXTRA = 5
FIELDS = 5
f32 = jnp.float32


def tile(ref, lead, x, move, low=LOW):
    index = lead + (x + 1 + move[0], pl.ds(low + move[1], NY), slice(None))
    value = ref[index]
    if move[2]:
        value = pltpu.roll(value, (-move[2]) % NZ, 1)
    return value


def look_up(table, index):
    high = lax.shift_right_logical(index, 7)
    low = index & 127
    result = jnp.zeros(index.shape, f32)
    for r in range(32):
        row = jnp.broadcast_to(table[pl.ds(r, 1), :], index.shape)
        picked = jnp.take_along_axis(row, low, axis=1, mode="promise_in_bounds")
        result = jnp.where(high == r, picked, result)
    return result


def roll_z(value, step):
    return pltpu.roll(value, (-step) % NZ, 1)


def gradient(view):
    sixth, twelfth = 1.0 / 6.0, 1.0 / 12.0
    east, west, north, south = view(1, 0), view(-1, 0), view(0, 1), view(0, -1)
    dx, dy = east - west, north - south
    xy = view(1, 1) - view(-1, -1)
    xmy = view(1, -1) - view(-1, 1)
    along = sixth * view(0, 0) + twelfth * (east + west + north + south)
    gx = sixth * dx + twelfth * (xy + xmy + roll_z(dx, 1) + roll_z(dx, -1))
    gy = sixth * dy + twelfth * (xy - xmy + roll_z(dy, 1) + roll_z(dy, -1))
    return gx, gy, roll_z(along, 1) - roll_z(along, -1)


def moments(q):
    a, b = 1.0 / 18.0, 1.0 / 36.0

    def pair(i):
        return q[i] + q[i + 1], q[i] - q[i + 1]

    (sx, dx), (sy, dy), (sz, dz) = pair(1), pair(3), pair(5)
    (s7, d7), (s9, d9), (s11, d11) = pair(7), pair(9), pair(11)
    (s13, d13), (s15, d15), (s17, d17) = pair(13), pair(15), pair(17)
    xy, xz, yz = s7 + s9, s11 + s13, s15 + s17
    m0 = (1.0 / 3.0) * q[0] + a * (sx + sy + sz) + b * (xy + xz + yz)
    mx = a * dx + b * (d7 + d9 + d11 + d13)
    my = a * dy + b * (d7 - d9 + d15 + d17)
    mz = a * dz + b * (d11 - d13 + d15 - d17)
    mxx = a * sx + b * (xy + xz)
    myy = a * sy + b * (xy + yz)
    mzz = a * sz + b * (xz + yz)
    return m0, (mx, my, mz), (mxx, myy, mzz, b * (s7 - s9), b * (s11 - s13), b * (s15 - s17))


def velocity(f):
    density = f[0]
    for i in range(1, 19):
        density = density + f[i]
    d = {i: f[i] - f[i + 1] for i in range(1, 19, 2)}
    inv = 1.0 / density
    ux = (d[1] + d[7] + d[9] + d[11] + d[13]) * inv
    uy = (d[3] + d[7] - d[9] + d[15] + d[17]) * inv
    uz = (d[5] + d[11] - d[13] + d[15] - d[17]) * inv
    return ux, uy, uz


def apply_second(second, v):
    mxx, myy, mzz, mxy, mxz, myz = second
    x, y, z = v
    return (
        mxx * x + mxy * y + mxz * z,
        mxy * x + myy * y + myz * z,
        mxz * x + myz * y + mzz * z,
    )


def dot3(a, b):
    return a[0] * b[0] + a[1] * b[1] + a[2] * b[2]


def collide_back(post, q, u, phase, store):
    q0, q1, q2 = q
    omega = 1.0 / (relax_heavy * (1.0 + phase) * 0.5 + relax_light * (1.0 - phase) * 0.5)
    q2u = apply_second(q2, u)
    along = q0 - 4.5 * dot3(u, q2u) + 1.5 * dot3(u, u) * q0
    base = omega * along
    bx, by, bz = [omega * (3.0 * q1[d] + 9.0 * q2u[d] - 3.0 * u[d] * q0) for d in range(3)]
    keep = 1.0 - omega
    store(0, keep * post[0] + base)
    slopes = (bx, by, bz, bx + by, bx - by, bx + bz, bx - bz, by + bz, by - bz)
    for k, slope in enumerate(slopes):
        i = 1 + 2 * k
        store(i, keep * post[i] + (base + slope))
        store(i + 1, keep * post[i + 1] + (base - slope))


def gradient_back(q0, q2, n):
    nsq = dot3(n, n)
    root = 1.0 / jnp.sqrt(1.0 + nsq)
    q2n = apply_second(q2, n)
    energy = dot3(n, q2n) - (1.0 / 3.0) * nsq * q0
    third = (4.0 / 3.0) * q0
    tail = 2.0 * energy * root * root * root
    return [root * (4.0 * q2n[d] - third * n[d]) - tail * n[d] for d in range(3)]


def gradient_adjoint(view):
    sixth, twelfth = 1.0 / 6.0, 1.0 / 12.0
    xe, xw, yn, ys = view(0, 1, 0), view(0, -1, 0), view(1, 0, 1), view(1, 0, -1)
    zc = sixth * view(2, 0, 0)
    around = view(2, 1, 0) + view(2, -1, 0) + view(2, 0, 1) + view(2, 0, -1)
    across = xe - xw + yn - ys
    flat = sixth * across + twelfth * (
        view(0, 1, 1) + view(1, 1, 1) - view(0, -1, -1) - view(1, -1, -1)
        + view(0, 1, -1) - view(1, 1, -1) - view(0, -1, 1) + view(1, -1, 1)
    )
    ahead = zc + twelfth * (across + around)
    behind = twelfth * (across - around) - zc
    return -(flat + roll_z(ahead, 1) + roll_z(behind, -1))


def side_adjoint(rows, sign):
    sixth, twelfth = 1.0 / 6.0, 1.0 / 12.0
    gx, gy, gz = [lambda move, d=d: rows[d, pl.ds(1 + move, WX), :] for d in range(3)]
    flat = sixth * sign * gy(0) + twelfth * (sign * (gy(1) + gy(-1)) + gx(1) - gx(-1))
    return -(flat + twelfth * (roll_z(sign * gy(0) + gz(0), 1) + roll_z(sign * gy(0) - gz(0), -1)))


def whole_call(kernel, name, out_shape, args, scratch=(), aliases=None, in_hbm=False, specs=None):
    options = {}
    if in_hbm:
        options["in_specs"] = [pl.BlockSpec(memory_space=pl.ANY)] * len(args)
    else:
        if specs:
            options["in_specs"] = specs
        options["compiler_params"] = pltpu.CompilerParams(vmem_limit_bytes=24 * 1024 * 1024)
    return pl.pallas_call(
        kernel,
        out_shape=[
            pltpu.VMEM(shape, kind) if in_hbm else jax.ShapeDtypeStruct(shape, kind) for shape, kind in out_shape
        ],
        scratch_shapes=scratch,
        input_output_aliases=aliases or {},
        name=name,
        **options,
    )(*args)


class Pick:
    def __init__(self, first, a, b):
        self.first, self.a, self.b = first, a, b

    def __getitem__(self, index):
        return jnp.where(self.first, self.a[index], self.b[index])


def is_odd(axis):
    return lax.axis_index(axis) % 2 == 1


def sides(axis, a, b):
    odd = is_odd(axis)
    return Pick(odd, a, b), Pick(odd, b, a)


def put(odd, outs, index, up, down):
    outs[0][index] = jnp.where(odd, up, down)
    outs[1][index] = jnp.where(odd, down, up)


def put_rows(odd, outs, slot, flat, up, down):
    rows = [flat[pl.ds(start, NX, stride=NY), :].astype(f32) for start in (up, down)]
    put(odd, outs, (pl.ds(slot * NX, NX), slice(None)), *rows)


def put_pops(adj, x_outs, y_outs):
    odd_x, odd_y = is_odd("pipe"), is_odd("cross")
    flat = adj.reshape(adj.shape[0] * NX * NY, NZ)
    for k in range(5):
        put(odd_x, x_outs, k, adj[x_plus[k], 0], adj[x_minus[k], NX - 1])
        put_rows(odd_y, y_outs, k, flat, y_plus[k] * NX * NY, y_minus[k] * NX * NY + NY - 1)


def fetch(pairs, sem):
    copies = [pltpu.make_async_copy(a, b, sem.at[k]) for k, (a, b) in enumerate(pairs)]
    for copy in copies:
        copy.start()
    return copies


def along(x, y):
    return [i for i in range(19) if lattice_vel[i][:2] == (x, y)]


def corner_rows(adj, fluid, speed, side, sign):
    x, step = ((0, 1), (NX - 1, -1))[side]
    y = 0 if sign > 0 else NY - 1
    flat = adj.reshape(adj.shape[0] * NX * NY, NZ)
    rows = [flat[pl.ds(x * NY + y, 19, stride=NX * NY), :]]
    rows += [speed[d][y : y + 1, :] for d in range(3)]

    def row(ref, lead, a, b):
        return ref[lead + (a, pl.ds(b, 1), slice(None))].astype(f32)

    rows += [row(adj, (p,), x + step, y) for p in along(step, 0)]
    rows += [row(adj, (p,), x, y + sign) for p in along(0, sign)]
    (diagonal,) = along(step, sign)
    rows += [row(adj, (diagonal,), x + step, y + sign), row(adj, (diagonal,), x, y + sign)]
    return rows + [row(fluid, (), x, y + sign), row(fluid, (), x + step, y + sign), row(fluid, (), x + step, y)]


def pack_kernel(adj_hbm, *refs):
    hbm, pops_hbm, (xa, xb, ya, yb) = refs[:FIELDS], refs[FIELDS], refs[FIELDS + 1 : FIELDS + 5]
    adj, *fields = refs[FIELDS + 5 : -2]
    pops, sem = refs[-2:]
    pairs = [(adj_hbm, adj.at[pl.ds(0, 19)]), *zip(hbm, fields)]
    pairs += [(pops_hbm.at[:, x], pops.at[:, k]) for k, x in enumerate((0, NX - 1))]
    for copy in fetch(pairs, sem):
        copy.wait()
    put_pops(adj, (xa, xb), (ya, yb))
    odd_x, odd_y = is_odd("pipe"), is_odd("cross")
    for k in range(FIELDS):
        put(odd_x, (xa, xb), 5 + k, fields[k][0].astype(f32), fields[k][NX - 1].astype(f32))
        put_rows(odd_y, (ya, yb), 5 + k, fields[k].reshape(NX * NY, NZ), 0, NY - 1)
    fluid = fields[2]
    for side in range(2):
        speed = velocity([pops[i, side] for i in range(19)])
        at = (5 + FIELDS) * NX + side * EXTRA
        for up, down in zip(*[corner_rows(adj, fluid, speed, side, sign) for sign in (1, -1)]):
            put(odd_y, (ya, yb), (pl.ds(at, up.shape[0]), slice(None)), up, down)
            at += up.shape[0]
    flats = [ref.reshape(X_PLANES * NY, NZ) for ref in (xa, xb)]
    for e, sign in enumerate((1, -1)):
        y = NY - 1 if sign > 0 else 0
        both = []
        for x, step in ((0, 1), (NX - 1, -1)):
            rows = [adj[p, x, pl.ds(y, 1), :] for p in along(0, -sign)]
            rows += [adj[p, x + step, pl.ds(y, 1), :] for p in along(step, -sign)]
            both.append(rows + [fluid[x + step, pl.ds(y, 1), :].astype(f32)])
        for k, (up, down) in enumerate(zip(*both)):
            put(odd_x, flats, (pl.ds(corner_at(e) + EXTRA + k, 1), slice(None)), up, down)


Y_ROWS = (5 + FIELDS) * NX + 80
X_PLANES = 5 + FIELDS + 2 + 10


def corner_at(e):
    return (5 + FIELDS + 2 + 5 * e) * NY


def pack(adjoint, fields, pops):
    face, side = ((X_PLANES, NY, NZ), f32), ((Y_ROWS, NZ), f32)
    scratch = [pltpu.VMEM((24, NX, NY, NZ), f32)]
    scratch += [pltpu.VMEM((NX, NY, NZ), field.dtype) for field in fields]
    scratch.append(pltpu.VMEM((19, 2, NY, NZ), f32))
    scratch.append(pltpu.SemaphoreType.DMA((3 + FIELDS,)))
    return whole_call(pack_kernel, "pack", [face, face, side, side], (adjoint, *fields, pops), scratch, in_hbm=True)


edge_plus = (7, 9)
edge_minus = (10, 8)


def pack_edges_kernel(xa, xb, yb, ya, _, xa_out, xb_out):
    planes = 5 + FIELDS
    for k in [*range(planes), *range(planes + 2, X_PLANES)]:
        xa_out[k] = xa[k]
        xb_out[k] = xb[k]
    low, high = sides("cross", ya, yb)
    odd = is_odd("pipe")
    flats = [ref.reshape(X_PLANES * NY, NZ) for ref in (xa_out, xb_out)]
    for e, (rows, pops) in enumerate(((high, y_plus), (low, y_minus))):
        xa_out[planes + e] = jnp.zeros((NY, NZ), f32)
        xb_out[planes + e] = jnp.zeros((NY, NZ), f32)
        starts = [(pops.index(edge_plus[e]), pops.index(edge_minus[e]))] + [(5 + k, 5 + k) for k in range(FIELDS)]
        for r, (up, down) in enumerate(starts):
            up_row = rows[pl.ds(up * NX, 1), :]
            down_row = rows[pl.ds(down * NX + NX - 1, 1), :]
            put(odd, (xa_out, xb_out), (planes + e, pl.ds(r, 1), slice(None)), up_row, down_row)
        up, down = [rows[pl.ds(planes * NX + side * EXTRA, EXTRA), :] for side in range(2)]
        put(odd, flats, (pl.ds(corner_at(e), EXTRA), slice(None)), up, down)


def pack_edges(x_pair, y_halo, after):
    out = ((X_PLANES, NY, NZ), f32)
    return whole_call(pack_edges_kernel, "pack_edges", [out, out], (*x_pair, *y_halo[::-1], after))


def fill_sides(pad, lead, y_low, low_slot, y_high, high_slot):
    for x in range(NX):
        pad[lead + (x + 1, pl.ds(LOW - 1, 1), slice(None))] = y_low[pl.ds(low_slot * NX + x, 1), :]
        pad[lead + (x + 1, pl.ds(LOW + NY, 1), slice(None))] = y_high[pl.ds(high_slot * NX + x, 1), :]


def fill_pops(pad, adj, planes, y_low, y_high):
    for p in range(19):
        for x in planes:
            pad[p, x + 1, pl.ds(LOW, NY), :] = adj[p, x]
    for k in range(5):
        for x in planes:
            pad[y_minus[k], x + 1, pl.ds(LOW - 1, 1), :] = y_low[pl.ds(k * NX + x, 1), :]
            pad[y_plus[k], x + 1, pl.ds(LOW + NY, 1), :] = y_high[pl.ds(k * NX + x, 1), :]


def fill_pops_outer(pad, x_low, x_high, edge):
    for k in range(5):
        pad[x_minus[k], 0, pl.ds(LOW, NY), :] = x_low[k]
        pad[x_plus[k], WX - 1, pl.ds(LOW, NY), :] = x_high[k]
    for e, row in enumerate((LOW + NY, LOW - 1)):
        pad[edge_minus[e], 0, pl.ds(row, 1), :] = edge(0, e)
        pad[edge_plus[e], WX - 1, pl.ds(row, 1), :] = edge(1, e)


def edge_of(edges):
    return lambda side, e: edges[pl.ds(2 * side + e, 1), :]


def fill_field(pad, lead, own, slot, y_low, y_high):
    for x in range(NX):
        pad[lead + (x + 1, pl.ds(LOW, NY), slice(None))] = own[x].astype(f32)
    fill_sides(pad, lead, y_low, 5 + slot, y_high, 5 + slot)


def fill_field_outer(pad, lead, slot, x_low, x_high):
    for x, face in ((0, x_low), (WX - 1, x_high)):
        pad[lead + (x, pl.ds(LOW, NY), slice(None))] = face[5 + slot]
        for e, row in enumerate((LOW + NY, LOW - 1)):
            pad[lead + (x, pl.ds(row, 1), slice(None))] = face[5 + FIELDS + e, pl.ds(1 + slot, 1), :]


def propagate_back(adj_pad, fluid_pad, x, low=LOW):
    here = tile(fluid_pad, (), x, (0, 0, 0), low)
    post = [here * adj_pad[0, x + 1, pl.ds(low, NY), :]]
    for i in range(1, 19):
        ahead = tile(fluid_pad, (), x, lattice_vel[i], low)
        moved = tile(adj_pad, (i,), x, lattice_vel[i], low)
        back = adj_pad[opposite[i], x + 1, pl.ds(low, NY), :]
        post.append(here * jnp.where(ahead != 0.0, moved, back))
    return post


def step_plane(x, adj_pad, fluid_pad, speed, phase, adj_out, mom_out, at=0):
    post = propagate_back(adj_pad, fluid_pad, x)
    q = moments(post)

    def store(i, value):
        adj_out[i, x - at] = value

    collide_back(post, q, [speed[d, x] for d in range(3)], phase[x], store)
    if mom_out is not None:
        mom_out[0, x] = q[0]
        for k in range(6):
            mom_out[1 + k, x] = q[2][k]


inner = range(1, NX - 1)


def second_inner_kernel(speed, phase, adj, fluid, yb, ya, adj_out, mom_out, adj_pad, fluid_pad):
    y_low, y_high = sides("cross", ya, yb)
    fill_field(fluid_pad, (), fluid, 2, y_low, y_high)
    fill_pops(adj_pad, adj, range(NX), y_low, y_high)

    def plane(x, carry):
        step_plane(x, adj_pad, fluid_pad, speed, phase, adj_out, mom_out)
        return carry

    lax.fori_loop(1, NX - 1, plane, 0, unroll=7)


block = ((19, NX, NY, NZ), f32)
seven = ((7, NX, NY, NZ), f32)
vector = ((3, NX, NY, NZ), f32)


def pad_scratch():
    return [pltpu.VMEM((19, WX, ROWS, NZ), f32), pltpu.VMEM((WX, ROWS, NZ), f32)]


def corner_edges(adj, fluid, y_sides, x_sides, edges_out, corner_pad, corner_fluid):
    base = (5 + FIELDS) * NX
    for side, face in enumerate(x_sides):
        sx = (-1, 1)[side]
        x = (0, NX - 1)[side]
        near, far = 1 - sx, 1 + sx
        pad, wet = corner_pad.at[side], corner_fluid.at[side]
        flat = Pick(face.first, *[ref.reshape(X_PLANES * NY, NZ) for ref in (face.a, face.b)])
        for e, (rows, sy) in enumerate(zip(y_sides, (1, -1))):
            at = LOW + NY if sy > 0 else LOW - 1
            inner_y = NY - 1 if sy > 0 else 0
            first = corner_at(e)

            def got(r):
                return flat[pl.ds(first + r, 1), :]

            def beside(r):
                return rows[pl.ds(base + side * EXTRA + r, 1), :]

            def set_pops(pops, plane, row, values):
                for p, value in zip(pops, values):
                    pad[p, plane, pl.ds(row, 1), :] = value

            set_pops(range(19), 1, at, [got(r) for r in range(19)])
            set_pops(along(sx, 0), far, at, [got(22 + r) for r in range(3)])
            set_pops(along(0, sy), 1, at + sy, [got(25 + r) for r in range(3)])
            set_pops(along(sx, sy), far, at + sy, [got(28)])
            set_pops(along(-sx, 0), near, at, [beside(p) for p in along(-sx, 0)])
            set_pops(along(-sx, sy), near, at + sy, [beside(29)])
            set_pops(along(0, -sy), 1, at - sy, [got(EXTRA + r) for r in range(3)])
            set_pops(along(sx, -sy), far, at - sy, [got(EXTRA + 3)])
            set_pops(along(-sx, -sy), near, at - sy, [adj[p, x, pl.ds(inner_y, 1), :] for p in along(-sx, -sy)])
            for plane, row, value in (
                (1, at, face[5 + FIELDS + e, pl.ds(3, 1), :]),
                (far, at, got(32)),
                (1, at + sy, got(30)),
                (far, at + sy, got(31)),
                (near, at, rows[pl.ds((5 + 2) * NX + x, 1), :]),
                (near, at + sy, beside(30)),
                (1, at - sy, face[5 + 2, pl.ds(inner_y, 1), :]),
                (far, at - sy, got(EXTRA + 4)),
                (near, at - sy, fluid[x, pl.ds(inner_y, 1), :].astype(f32)),
            ):
                wet[plane, pl.ds(row, 1), :] = value
            low = LOW + 1 if sy > 0 else LOW - 1
            post = propagate_back(pad, wet, 0, low)
            u = [jnp.broadcast_to(got(19 + d), (NY, NZ)) for d in range(3)]
            phase = jnp.broadcast_to(face[5 + FIELDS + e, pl.ds(2, 1), :], (NY, NZ))
            kept = {}
            collide_back(post, moments(post), u, phase, kept.__setitem__)
            (crossing,) = along(sx, sy)
            edges_out[pl.ds(2 * side + e, 1), :] = kept[crossing][at - low : at - low + 1, :]
    edges_out[pl.ds(4, 4), :] = jnp.zeros((4, NZ), f32)


def second_outer_kernel(
    speed, phase, adj, fluid, yb, ya, xa, xb, adj_in, mom_in, _,
    adj_out, mom_out, xa_out, xb_out, ya_out, yb_out, edges_out,
    adj_pad, fluid_pad, corner_pad, corner_fluid,
):
    (x_low, x_high), (y_low, y_high) = sides("pipe", xa, xb), sides("cross", ya, yb)
    fill_field(fluid_pad, (), fluid, 2, y_low, y_high)
    fill_field_outer(fluid_pad, (), 2, x_low, x_high)
    fill_pops(adj_pad, adj, (0, 1, NX - 2, NX - 1), y_low, y_high)
    faces = (x_low, x_high)
    fill_pops_outer(adj_pad, x_low, x_high, lambda side, e: faces[side][5 + FIELDS + e, pl.ds(0, 1), :])
    for x in (0, NX - 1):
        step_plane(x, adj_pad, fluid_pad, speed, phase, adj_out, mom_out)
    put_pops(adj_out, (xa_out, xb_out), (ya_out, yb_out))
    corner_edges(adj, fluid, (y_high, y_low), faces, edges_out, corner_pad, corner_fluid)


def one_hots(index, row, hit_out, right_out, at):
    row_iota = lax.broadcasted_iota(jnp.int32, (64, NZ), 0)
    key = (lax.shift_right_logical(index, 6) & 1) * 32 + lax.shift_right_logical(index, 7)
    low = index & 63
    hit = jnp.where(row_iota == key[row : row + 1, :], 1.0, 0.0)
    hit_out[:, pl.ds(at, NZ)] = hit.astype(jnp.bfloat16)
    right = jnp.where(row_iota == low[row : row + 1, :], 1.0, 0.0)
    right_out[:, pl.ds(at, NZ)] = right.astype(jnp.bfloat16)


OWN = NX * NY * NZ
SIDES = 2 * NX * NZ
FACES = (2 * NY + 4) * NZ


def store_velocity(pops, out):
    def plane(x, carry):
        u = velocity([pops[i, x] for i in range(19)])
        for d in range(3):
            out[d, x] = u[d]
        return carry

    lax.fori_loop(0, NX, plane, 0, unroll=4)


def own_kernel(
    table_hbm, phase_a_hbm, phase_b_hbm, fluid_hbm, wall_hbm, patch_hbm, pops_hbm,
    phi_out, hit_out, right_out, wall_out, speed_out,
    table, phase_a, phase_b, fluid, wall, patch, pops, sem,
):
    hbm = (table_hbm, phase_a_hbm, phase_b_hbm, fluid_hbm, wall_hbm, patch_hbm, pops_hbm)
    copies = fetch(zip(hbm, (table, phase_a, phase_b, fluid, wall, patch, pops)), sem)
    for copy in copies[:-1]:
        copy.wait()

    def plane(x, carry):
        index = patch[x] & 4095
        wall_out[x] = wall[x].astype(f32)
        contact = wall[x].astype(f32) * look_up(table, index)
        wet = fluid[x].astype(f32)
        phi_out[0, x] = wet * phase_a[x] + contact
        phi_out[1, x] = wet * phase_b[x] + contact
        for r in range(NY):
            one_hots(index, r, hit_out, right_out, pl.multiple_of((x * NY + r) * NZ, NZ))
        return carry

    lax.fori_loop(0, NX, plane, 0, unroll=4)
    copies[-1].wait()
    store_velocity(pops, speed_out)


def imposed(table, slot):
    index = slot(4).astype(jnp.int32) & 4095
    contact = slot(3) * look_up(table, index)
    return index, [slot(2) * slot(t) + contact for t in range(2)]


def side_kernel(table, yb, ya, phi_out, wall_out, hit_out, right_out):
    for side, rows in enumerate(sides("cross", ya, yb)):
        index, values = imposed(table, lambda k: rows[pl.ds((5 + k) * NX, NX), :])
        wall_out[side] = rows[pl.ds(8 * NX, NX), :]
        for t in range(2):
            phi_out[side, t] = values[t]
        for x in range(NX):
            one_hots(index, x, hit_out, right_out, (side * NX + x) * NZ)


def middle_kernel(
    phi, table, fluid, mom, ya, yb, xa, xb, phi_side, wall_beside,
    dgrad_out, grad_out, fluid_out, wall_face, wall_side, hit_out, right_out,
    phi_pad,
):
    (x_low, x_high), (y_low, y_high) = sides("pipe", xa, xb), sides("cross", ya, yb)
    fill_field(fluid_out, (), fluid, 2, y_low, y_high)
    fill_field_outer(fluid_out, (), 2, x_low, x_high)
    for x in range(NX):
        for t in range(2):
            phi_pad[t, x + 1, pl.ds(LOW, NY), :] = phi[t, x]
            for side, y in enumerate((LOW - 1, LOW + NY)):
                phi_pad[t, x + 1, pl.ds(y, 1), :] = phi_side[side, t, pl.ds(x, 1), :]
    for side, (face, x) in enumerate(((x_low, 0), (x_high, WX - 1))):
        index, values = imposed(table, lambda k: face[5 + k])
        wall_face[side] = face[8]
        wall_side[side, pl.ds(1, NX), :] = wall_beside[side]
        for t in range(2):
            phi_pad[t, x, pl.ds(LOW, NY), :] = values[t]
        for r in range(NY):
            one_hots(index, r, hit_out, right_out, (side * NY + r) * NZ)

    def corner_tile(k):
        rows = [face[5 + FIELDS + 1 - e, pl.ds(1 + k, 1), :] for e in range(2) for face in (x_low, x_high)]
        return jnp.concatenate(rows + rows, axis=0)

    index, values = imposed(table, corner_tile)
    on_wall = corner_tile(3)
    for r in range(4):
        side, x, y = r // 2, (WX - 1) * (r % 2), (LOW - 1, LOW + NY)[r // 2]
        wall_side[side, pl.ds(x, 1), :] = on_wall[r : r + 1, :]
        for t in range(2):
            phi_pad[t, x, pl.ds(y, 1), :] = values[t][r : r + 1, :]
        one_hots(index, r, hit_out, right_out, (2 * NY + r) * NZ)

    def plane(x, carry):
        def view(t):
            return lambda a, b: tile(phi_pad, (t,), x, (a, b, 0))

        first, n = gradient(view(0)), gradient(view(1))
        for d in range(3):
            grad_out[d, x] = first[d]
        dgrad = gradient_back(mom[0, x], [mom[1 + k, x] for k in range(6)], n)
        for d in range(3):
            dgrad_out[d, x] = dgrad[d]
        return carry

    lax.fori_loop(0, NX, plane, 0, unroll=4)


def speed_kernel(pops_hbm, _, out, pops, sem):
    for copy in fetch([(pops_hbm, pops)], sem):
        copy.wait()
    store_velocity(pops, out)


def own_terms(*args):
    hots = ((64, OWN), jnp.bfloat16)
    scratch = [pltpu.VMEM(arg.shape, arg.dtype) for arg in args] + [pltpu.SemaphoreType.DMA((len(args),))]
    shapes = [((2, NX, NY, NZ), f32), hots, hots, ((NX, NY, NZ), f32), vector]
    return whole_call(own_kernel, "own_terms", shapes, args, scratch, specs=[pl.BlockSpec(memory_space=pl.ANY)] * len(args))


def side_terms(*args):
    shapes = [((2, 2, NX, NZ), f32), ((2, NX, NZ), f32)] + [((64, SIDES), jnp.bfloat16)] * 2
    return whole_call(side_kernel, "side_terms", shapes, args)


def middle(*args):
    shapes = [vector, vector, ((WX, ROWS, NZ), f32), ((2, NY, NZ), f32), ((2, WX, NZ), f32)]
    shapes += [((64, FACES), jnp.bfloat16)] * 2
    return whole_call(middle_kernel, "middle", shapes, args, [pltpu.VMEM((2, WX, ROWS, NZ), f32)])


def first_speed(pops, after):
    scratch = [pltpu.VMEM((19, NX, NY, NZ), f32), pltpu.SemaphoreType.DMA((1,))]
    specs = [pl.BlockSpec(memory_space=pl.ANY)] * 2
    return whole_call(speed_kernel, "first_speed", [vector], (pops, after), scratch, specs=specs)[0]


def weighted(hit, values):
    bigs, smalls = [], []
    for value in values:
        big = value.astype(jnp.bfloat16).astype(f32)
        for r in range(value.shape[0]):
            for rows, source in ((bigs, big), (smalls, value - big)):
                row = jnp.broadcast_to(source[r : r + 1, :], (16, NZ)).astype(jnp.bfloat16)
                rows.append(jnp.concatenate([row] * 4, axis=0))
    return jnp.concatenate(
        [hit * jnp.concatenate(bigs, axis=1), hit * jnp.concatenate(smalls, axis=1)], axis=0
    )


def table_sum(left, right):
    return lax.dot_general(left, right, (((1,), (1,)), ((), ())), preferred_element_type=f32)


def gradient_plane(x, adj_pad, fluid_pad, grad, dgrad_in, out):
    q0, _, q2 = moments(propagate_back(adj_pad, fluid_pad, x))
    dgrad = gradient_back(q0, q2, [grad[d, x] for d in range(3)])
    for d in range(3):
        out(d, x, dgrad[d] + dgrad_in[d, x])


def plane_adjoint(pad, x):
    return gradient_adjoint(lambda d, a, b: pad[d, x + 1 + a, pl.ds(LOW + b, NY), :])


GROUP = 6


def own_group(start, dgrad_pad, wall, hits, rights):
    values = [plane_adjoint(dgrad_pad, start + k + 1) * wall[start + k] for k in range(GROUP)]
    nodes = pl.ds(start * NY * NZ, GROUP * NY * NZ)
    return table_sum(weighted(hits[:, nodes], values), rights[:, nodes])


def first_inner_kernel(
    adj, fluid_pad, grad, dgrad_in, ya, yb, wall, hits, rights,
    dgrad_out, acc_out,
    adj_pad, dgrad_pad,
):
    y_low, y_high = sides("cross", ya, yb)
    fill_pops(adj_pad, adj, range(NX), y_low, y_high)
    dgrad_pad[pl.ds(0, 3)] = jnp.zeros((3, WX + 2, ROWS, NZ), f32)

    def out(d, x, value):
        dgrad_out[d, x] = value
        dgrad_pad[d, x + 2, pl.ds(LOW, NY), :] = value

    def plane(x, carry):
        gradient_plane(x, adj_pad, fluid_pad, grad, dgrad_in, out)
        return carry

    lax.fori_loop(1, NX - 1, plane, 0, unroll=7)
    total = own_group(2, dgrad_pad, wall, hits, rights)
    for start in range(2 + GROUP, NX - 2, GROUP):
        total = total + own_group(start, dgrad_pad, wall, hits, rights)
    acc_out[...] = total


def first_outer_kernel(
    adj, fluid_pad, grad, dgrad_in, ya, yb, xa, xb, edges, dgrad_inner, acc_in,
    wall, hits, rights, wall_face, wall_side, face_hits, face_rights, side_hits, side_rights,
    total_out,
    adj_pad, dgrad_pad, rows,
):
    (x_low, x_high), (y_low, y_high) = sides("pipe", xa, xb), sides("cross", ya, yb)
    fill_pops(adj_pad, adj, (0, 1, NX - 2, NX - 1), y_low, y_high)
    fill_pops_outer(adj_pad, x_low, x_high, edge_of(edges))
    for d in range(3):
        for x in (0, 1, 2, 3, NX, NX + 1, NX + 2, NX + 3):
            dgrad_pad[d, x] = jnp.zeros((ROWS, NZ), f32)

    def out(d, x, value):
        dgrad_pad[d, x + 2, pl.ds(LOW, NY), :] = value

    for x in (0, NX - 1):
        gradient_plane(x, adj_pad, fluid_pad, grad, dgrad_in, out)
    for x in inner:
        for d in range(3):
            out(d, x, dgrad_inner[d, x])
    values = [plane_adjoint(dgrad_pad, x + 1) * wall[x] for x in (0, 1, NX - 2, NX - 1)]
    total = acc_in[...]
    for k, start in enumerate((0, NX - 2)):
        nodes = pl.ds(start * NY * NZ, 2 * NY * NZ)
        total = total + table_sum(weighted(hits[:, nodes], values[2 * k : 2 * k + 2]), rights[:, nodes])
    values = [plane_adjoint(dgrad_pad, x) * wall_face[k] for k, x in enumerate((0, WX - 1))]
    flat = dgrad_pad.reshape(4 * (WX + 2) * ROWS, NZ)
    beside, corners = [], []
    for side, (row, sign) in enumerate(((LOW, 1.0), (LOW + NY - 1, -1.0))):
        for d in range(3):
            rows[d, pl.ds(0, WX + 2), :] = flat[pl.ds(d * (WX + 2) * ROWS + row, WX + 2, stride=ROWS), :]
        value = side_adjoint(rows, sign) * wall_side[side]
        beside.append(value[1 : WX - 1])
        corners += [value[:1], value[WX - 1 :]]
    values.append(jnp.concatenate(corners, axis=0))
    total = total + table_sum(weighted(face_hits[...], values), face_rights[...])
    total = total + table_sum(weighted(side_hits[...], beside), side_rights[...])
    both = total[:64] + total[64:]
    total_out[...] = jnp.concatenate([both[:32], both[32:]], axis=1)


shares = ((0, 6), (6, 5), (11, 5))


def first_adjoint_kernel(
    start, count, speed, phase, adj, fluid_pad, ya, yb, xa, xb, edges, *refs
):
    out, adj_pad, part, sem = refs[-4:]
    (x_low, x_high), (y_low, y_high) = sides("pipe", xa, xb), sides("cross", ya, yb)
    planes = range(max(start - 1, 0), min(start + count + 1, NX))
    fill_pops(adj_pad, adj, planes, y_low, y_high)
    if start == 0 or start + count == NX:
        fill_pops_outer(adj_pad, x_low, x_high, edge_of(edges))

    def plane(k, carry):
        step_plane(start + k, adj_pad, fluid_pad, speed, phase, part, None, start)
        return carry

    lax.fori_loop(0, count, plane, 0)
    (copy,) = fetch([(part, out.at[:, pl.ds(start, count)])], sem)
    copy.wait()


def first_adjoint(start, count, args, after, before):
    args = (*args, after) if before is None else (*args, after, before)
    specs = [pl.BlockSpec(memory_space=pltpu.VMEM)] * 9 + [pl.BlockSpec(memory_space=pl.ANY)] * (len(args) - 9)
    return pl.pallas_call(
        functools.partial(first_adjoint_kernel, start, count),
        out_shape=jax.ShapeDtypeStruct(*block),
        in_specs=specs,
        out_specs=pl.BlockSpec(memory_space=pl.ANY),
        scratch_shapes=[
            pltpu.VMEM((19, WX, ROWS, NZ), f32),
            pltpu.VMEM((19, count, NY, NZ), f32),
            pltpu.SemaphoreType.DMA((1,)),
        ],
        input_output_aliases={} if before is None else {10: 0},
        compiler_params=pltpu.CompilerParams(vmem_limit_bytes=24 * 1024 * 1024),
        name="first_adjoint",
    )(*args)


def swap(axis, a, b):
    count = lax.axis_size(axis)
    near = lax.ppermute(a, axis, [(i, i ^ 1) for i in range(count)])
    far = lax.ppermute(b, axis, [(i, (i + 2 * (i % 2) - 1) % count) for i in range(count)])
    return near, far


def mirror(index, low, size):
    digit = index // low % size
    return index + (size - 1 - 2 * digit) * low


def sum_rounds():
    return (
        (lambda p, c: (p ^ 1, c),),
        (
            lambda p, c: (p ^ 3, c),
            lambda p, c: (mirror(p, 2, 4) ^ 1, c),
            lambda p, c: (mirror(p, 2, 4) ^ 3, c),
        ),
        (
            lambda p, c: (p ^ 1, c ^ 1),
            lambda p, c: (p ^ 1, mirror(c, 1, 4)),
            lambda p, c: (p ^ 1, mirror(c, 1, 4) ^ 1),
        ),
        (
            lambda p, c: (p ^ 1, c ^ 4),
            lambda p, c: (p ^ 1, mirror(c, 4, 4)),
            lambda p, c: (p ^ 1, mirror(c, 4, 4) ^ 4),
        ),
    )


def exchange(value, place):
    pipe, cross = lax.axis_size("pipe"), lax.axis_size("cross")
    pairs = []
    for p in range(pipe):
        for c in range(cross):
            q, d = place(p, c)
            pairs.append((p * cross + c, q * cross + d))
    return lax.ppermute(value, ("pipe", "cross"), pairs)


def pack_pairs(packed):
    return packed[:2], packed[2:]


def shards(
    pops_first,
    pops_second,
    phase_first,
    phase_second,
    adjoint_last,
    wettability,
    fluid,
    wall,
    patch,
):
    table = wettability.reshape(32, NZ)
    fields = (phase_first, phase_second, fluid, wall, patch)
    x_swap, y_swap = pack_pairs(pack(adjoint_last, fields, pops_second))
    y_halo = swap("cross", *y_swap)
    phi, hits, rights, wall_own, speed = own_terms(table, *fields, pops_second)
    x_halo = swap("pipe", *pack_edges(x_swap, y_halo, phi))
    phi_side, wall_beside, side_hits, side_rights = side_terms(table, *y_halo[::-1])
    given = (speed, phase_second, adjoint_last, fluid, *y_halo[::-1])
    adjoint, mom = whole_call(
        second_inner_kernel, "second_inner", [block, seven], given, pad_scratch()
    )
    face, side = ((5, NY, NZ), f32), ((5 * NX, NZ), f32)
    adjoint, mom, *packed, edges = whole_call(
        second_outer_kernel,
        "second_outer",
        [block, seven, face, face, side, side, ((8, NZ), f32)],
        given + x_halo + (adjoint, mom, phi_side),
        pad_scratch() + [pltpu.VMEM((2, 19, 3, ROWS, NZ), f32), pltpu.VMEM((2, 3, ROWS, NZ), f32)],
        {8: 0, 9: 1},
    )
    x_swap, y_swap = pack_pairs(packed)
    y_halo2, x_halo2 = swap("cross", *y_swap), swap("pipe", *x_swap)
    dgrad, grad, fluid_pad, wall_face, wall_side, face_hits, face_rights = middle(
        phi, table, fluid, mom, *y_halo, *x_halo, phi_side, wall_beside
    )
    given = (adjoint, fluid_pad, grad, dgrad, *y_halo2)
    nodes = (wall_own, hits, rights)
    adj_scratch = pad_scratch()[:1]
    dgrad_scratch = adj_scratch + [pltpu.VMEM((4, WX + 2, ROWS, NZ), f32)]
    dgrad_inner, acc = whole_call(
        first_inner_kernel, "first_inner", [vector, ((128, 64), f32)], given + nodes, dgrad_scratch
    )
    (total,) = whole_call(
        first_outer_kernel,
        "first_outer",
        [((32, NZ), f32)],
        given + x_halo2 + (edges, dgrad_inner, acc) + nodes + (wall_face, wall_side, face_hits, face_rights, side_hits, side_rights),
        dgrad_scratch + [pltpu.VMEM((4, 32, NZ), f32)],
    )
    args = (first_speed(pops_first, total), phase_first, adjoint, fluid_pad, *y_halo2, *x_halo2, edges)
    result = None
    for k, places in enumerate(sum_rounds()):
        got = [exchange(total, place) for place in places]
        if k:
            result = first_adjoint(*shares[k - 1], args, total, result)
            *got, result = lax.optimization_barrier((*got, result))
        for part in got:
            total = total + part
    return result, total.reshape(wettability.shape)


def solution(mesh):
    return jax.shard_map(
        shards,
        mesh=mesh,
        in_specs=(
            P(None, "pipe", "cross", None),
            P(None, "pipe", "cross", None),
            P("pipe", "cross", None),
            P("pipe", "cross", None),
            P(None, "pipe", "cross", None),
            P(),
            P("pipe", "cross", None),
            P("pipe", "cross", None),
            P("pipe", "cross", None),
        ),
        out_specs=(P(None, "pipe", "cross", None), P()),
        check_vma=False,
    )
```
